32 devices in a mesh: dp: 8 (over y, x, core), seq: 4 (over z).
Axes of the slice: x: 2, y: 2, z: 4, core: 2. Of those that a mesh axis runs over, the one named last changes fastest.
Arguments:
- latents: bfloat16 [2, 16, 256, 768], P(None, 'dp', 'seq'), may hold values from -6 to 6
- conditions: bfloat16 [2, 16, 768], P(None, 'dp'), may hold values from -6 to 6
- modulator: bfloat16 [768, 4608], P('dp', 'seq'), may hold values from -0.21875 to 0.21875
- modbias: bfloat16 [4608], P('seq'), may hold values from -3 to 3
- qkvweight: bfloat16 [768, 2304], P('dp', 'seq'), may hold values from -0.21875 to 0.21875
- querybias: bfloat16 [768], P('seq'), may hold values from -3 to 3
- valuebias: bfloat16 [768], P('seq'), may hold values from -3 to 3
- projection: bfloat16 [768, 768], P('dp', 'seq'), may hold values from -0.875 to 0.875
- projbias: bfloat16 [768], P('seq'), may hold values from -3 to 3
- expand: bfloat16 [768, 3072], P('dp', 'seq'), may hold values from -0.21875 to 0.21875
- expandbias: bfloat16 [3072], P('seq'), may hold values from -3 to 3
- contract: bfloat16 [3072, 768], P('dp', 'seq'), may hold values from -0.109375 to 0.109375
- contractbias: bfloat16 [768], P('seq'), may hold values from -3 to 3
- cotangent: bfloat16 [2, 16, 256, 768], P(None, 'dp', 'seq'), may hold values from -6 to 6
Outputs:
- result: bfloat16 [2, 16, 256, 768], P(None, 'dp', 'seq')
- latents_grad: bfloat16 [2, 16, 256, 768], P(None, 'dp', 'seq')
- conditions_grad: float32 [2, 16, 768], P(None, 'dp')
- modulator_grad: float32 [768, 4608], P('dp', 'seq')
- modbias_grad: float32 [4608], P('seq')
- qkvweight_grad: float32 [768, 2304], P('dp', 'seq')
- querybias_grad: float32 [768], P('seq')
- valuebias_grad: float32 [768], P('seq')
- projection_grad: float32 [768, 768], P('dp', 'seq')
- projbias_grad: float32 [768], P('seq')
- expand_grad: float32 [768, 3072], P('dp', 'seq')
- expandbias_grad: float32 [3072], P('seq')
- contract_grad: float32 [3072, 768], P('dp', 'seq')
- contractbias_grad: float32 [768], P('seq')
The draws below stay inside these ranges and needn't reach their ends.
All inputs are finite; a program needn't handle non-finite values.
Results may differ from the reference program's by a relative error of at most 0.04.
Values may be sent and summed in bfloat16 or wider, within the bound.
No kernel may reach another device: no remote copies, remote signals or barrier semaphores. Data moves between devices by JAX's collectives and lax.ppermute only.
A program may use at most 128 MiB of HBM per device.

```python
import jax
import jax.numpy as jnp
from jax import lax

D = 768
H = 12
FF = 3072
SEQLEN = 256
MICRO = 2
LAT_DEV = 2
LATENTS = 16


def shard_levels(own_key, dims, pieces, smallest, largest):
    level, own = 1.0, jax.random.fold_in(own_key, 6)
    for dim, blocks in pieces:
        steps = jnp.exp(jax.random.uniform(jax.random.fold_in(own, dim), (blocks,), jnp.float32, smallest / len(pieces), largest / len(pieces)))
        level = level * jnp.repeat(steps, dims[dim] // blocks).reshape([-1 if axis == dim else 1 for axis in range(len(dims))])
    return level


def scatter_about(stream_key, extent, scale, bound, shards=(), dtype=jnp.bfloat16):
    entries = scale * jax.random.normal(stream_key, extent, jnp.float32)
    if shards:
        entries = entries * shard_levels(stream_key, extent, shards, -0.22, 0.18)
    return jnp.clip(entries, -bound, bound).astype(dtype)


def setup_inputs(seed: int = 0) -> dict:
    key_list = jax.random.split(jax.random.key(seed), 15)
    return {
        "latents": scatter_about(key_list[0], (MICRO, LATENTS, SEQLEN, D), 1.0, 6.0, ((1, 8), (2, 4))),
        "conditions": scatter_about(key_list[1], (MICRO, LATENTS, D), 1.0, 6.0, ((1, 8),)),
        "modulator": scatter_about(key_list[2], (D, 6 * D), D ** -0.5, 0.21875, ((0, 8), (1, 4))),
        "modbias": scatter_about(key_list[3], (6 * D,), 0.5, 3.0, ((0, 4),)),
        "qkvweight": scatter_about(key_list[4], (D, 3 * D), D ** -0.5, 0.21875, ((0, 8), (1, 4))),
        "querybias": scatter_about(key_list[5], (D,), 0.5, 3.0, ((0, 4),)),
        "valuebias": scatter_about(key_list[6], (D,), 0.5, 3.0, ((0, 4),)),
        "projection": scatter_about(key_list[7], (D, D), (D // 16) ** -0.5, 0.875, ((0, 8), (1, 4))),
        "projbias": scatter_about(key_list[8], (D,), 0.5, 3.0, ((0, 4),)),
        "expand": scatter_about(key_list[9], (D, FF), D ** -0.5, 0.21875, ((0, 8), (1, 4))),
        "expandbias": scatter_about(key_list[10], (FF,), 0.5, 3.0, ((0, 4),)),
        "contract": scatter_about(key_list[11], (FF, D), FF ** -0.5, 0.109375, ((0, 8), (1, 4))),
        "contractbias": scatter_about(key_list[12], (D,), 0.5, 3.0, ((0, 4),)),
        "cotangent": scatter_about(key_list[13], (MICRO, LATENTS, SEQLEN, D), 1.0, 6.0, ((1, 8), (2, 4))),
    }


EPSILON = 1e-06
HIGHEST = lax.Precision.HIGHEST

@jax.custom_vjp
def low(v):
    return lax.optimization_barrier(v.astype(jnp.bfloat16)).astype(jnp.float32)

@jax.custom_vjp
def low_back(v):
    return v

def low_keep(v):
    return (low(v), None)

def low_pass(kept, grad):
    return (grad,)

def back_keep(v):
    return (v, None)

def back_low(kept, grad):
    return (low(grad),)
low.defvjp(low_keep, low_pass)
low_back.defvjp(back_keep, back_low)

def normalize(values):
    center = values - lax.optimization_barrier(jnp.mean(values, axis=-1, keepdims=True))
    return center * lax.rsqrt(lax.optimization_barrier(jnp.mean(center * center, axis=-1, keepdims=True)) + EPSILON)

def project(values, matrix):
    return jnp.einsum('gsd,dn->gsn', values, matrix, precision=HIGHEST)

def attend(triple):
    queries, keys, values = triple
    logits = jnp.einsum('shd,thd->hst', queries, keys, precision=HIGHEST)
    scores = low_back(logits * (D // H) ** (-0.5))
    weights = low(jax.nn.softmax(scores, axis=-1))
    mixed = jnp.einsum('hst,thd->shd', weights, values, precision=HIGHEST)
    return low(low_back(mixed.reshape(mixed.shape[0], D)))

def layer(tokens, conds, modulator, modbias, qkvweight, querybias, valuebias, projection, projbias, expand, expandbias, contract, contractbias):
    group, length = (tokens.shape[0], tokens.shape[1])
    cond = low(jax.nn.silu(conds))
    modulation = low_back(jnp.dot(cond, modulator, precision=HIGHEST, preferred_element_type=jnp.float32) + modbias)
    shift1, scale1, gate1, shift2, scale2, gate2 = jnp.split(modulation[:, None, :], 6, axis=-1)
    hidden1 = low(normalize(tokens) * (1.0 + scale1) + shift1)
    offsets = jnp.concatenate([querybias, jnp.zeros_like(querybias), valuebias])
    qkv = low(low_back(project(hidden1, qkvweight) + offsets))
    qkv = qkv.reshape(group, length, 3, H, D // H)
    attended = lax.map(jax.checkpoint(attend), (qkv[:, :, 0], qkv[:, :, 1], qkv[:, :, 2]))
    branch1 = low_back(project(attended, projection) + projbias)
    middle = tokens + gate1 * branch1
    hidden2 = low(normalize(middle) * (1.0 + scale2) + shift2)
    before = low_back(project(hidden2, expand) + expandbias)
    active = low(jax.nn.gelu(before, approximate=True))
    branch2 = low_back(project(active, contract) + contractbias)
    return middle + gate2 * branch2

def reference(latents, conditions, modulator, modbias, qkvweight, querybias, valuebias, projection, projbias, expand, expandbias, contract, contractbias, cotangent):
    weights = tuple((w.astype(jnp.float32) for w in (modulator, modbias, qkvweight, querybias, valuebias, projection, projbias, expand, expandbias, contract, contractbias)))
    groups = MICRO * LATENTS // LAT_DEV
    token_groups = latents.astype(jnp.float32).reshape(groups, LAT_DEV, SEQLEN, D)
    cond_groups = conditions.astype(jnp.float32).reshape(groups, LAT_DEV, D)
    cot_groups = cotangent.astype(jnp.float32).reshape(groups, LAT_DEV, SEQLEN, D)

    def step(totals, entry):
        tokens, conds, cots = entry
        output, pullback = jax.vjp(layer, tokens, conds, *weights)
        grads = pullback(cots)
        totals = tuple((a + b for a, b in zip(totals, grads[2:])))
        return (totals, (output.astype(jnp.bfloat16), grads[0].astype(jnp.bfloat16), grads[1]))
    start = tuple((jnp.zeros_like(w) for w in weights))
    totals, (outputs, token_grads, cond_grads) = lax.scan(step, start, (token_groups, cond_groups, cot_groups))
    result = outputs.reshape(MICRO, LATENTS, SEQLEN, D)
    latents_grad = token_grads.reshape(MICRO, LATENTS, SEQLEN, D)
    conditions_grad = cond_grads.reshape(MICRO, LATENTS, D)
    return (result, latents_grad, conditions_grad, totals[0], totals[1], totals[2], totals[3], totals[4], totals[5], totals[6], totals[7], totals[8], totals[9], totals[10])
```

```python
import jax
import jax.numpy as jnp
from jax import lax
from jax.sharding import PartitionSpec as P

H = 12
EPSILON = 1e-06
BF = jnp.bfloat16
F32 = jnp.float32


def bits_of(count):
    bits = count.bit_length() - 1
    assert 1 << bits == count
    return bits


def swap(values, axis, bit):
    count = lax.axis_size(axis)
    return lax.ppermute(values, axis, [(i, i ^ (1 << bit)) for i in range(count)])


def own_bit(axis, bit):
    return (lax.axis_index(axis) >> bit) & 1


def join(values, axis, bit):
    other = swap(values, axis, bit)
    mine = own_bit(axis, bit) == 0
    return jnp.stack([jnp.where(mine, values, other), jnp.where(mine, other, values)])


def halve(values, axis, bit):
    index = own_bit(axis, bit)
    sent = lax.dynamic_index_in_dim(values, 1 - index, 0, keepdims=False)
    kept = lax.dynamic_index_in_dim(values, index, 0, keepdims=False)
    other = swap(sent.astype(BF), axis, bit)
    return kept.astype(F32) + other.astype(F32)


def gather_seq(values):
    count = bits_of(lax.axis_size("seq"))
    shape = values.shape
    order = list(range(count - 1, -1, -1))
    for bit in order:
        values = join(values, "seq", bit)
    values = values.transpose(list(range(count - 1, -1, -1)) + list(range(count, count + len(shape))))
    return values.reshape((1 << count,) + shape)


def scatter_seq(values):
    count = bits_of(lax.axis_size("seq"))
    shape = values.shape[1:]
    values = values.reshape((2,) * count + shape)
    values = values.transpose(list(range(count - 1, -1, -1)) + list(range(count, count + len(shape))))
    for bit in range(count):
        values = halve(values, "seq", bit)
    return values


def dp_orders():
    count = bits_of(lax.axis_size("dp"))
    upper = list(range(1, count))
    return (upper + [0], upper[::-1] + [0])


def gather_dp(units):
    count = bits_of(lax.axis_size("dp"))
    half = units.shape[-1] // 2
    parts = []
    for part, order in zip((units[..., :half], units[..., half:]), dp_orders()):
        for bit in order:
            part = join(part, "dp", bit)
        dims = [order[::-1].index(bit) for bit in range(count - 1, -1, -1)]
        part = part.transpose(dims + [count, count + 1, count + 2])
        parts.append(part.reshape((1 << count,) + part.shape[count:]))
    return jnp.concatenate(parts, axis=-1)


def scatter_dp(grads):
    count = bits_of(lax.axis_size("dp"))
    half = grads.shape[-1] // 2
    parts = []
    for part, order in zip((grads[..., :half], grads[..., half:]), dp_orders()):
        back = order[::-1]
        part = part.reshape((2,) * count + part.shape[1:])
        dims = [count - 1 - bit for bit in back]
        part = part.transpose(dims + [count, count + 1, count + 2])
        for bit in back:
            part = halve(part, "dp", bit)
        parts.append(part)
    return jnp.concatenate(parts, axis=-1)


def normalize(values):
    center = values - jnp.mean(values, axis=-1, keepdims=True)
    inverse = lax.rsqrt(jnp.mean(center * center, axis=-1, keepdims=True) + EPSILON)
    return (center * inverse, inverse)


def norm_back(grad_normed, normed, inverse):
    first = jnp.mean(grad_normed, axis=-1, keepdims=True)
    second = jnp.mean(grad_normed * normed, axis=-1, keepdims=True)
    return inverse * (grad_normed - first - normed * second)


def project(values, matrix):
    return jnp.einsum("lsd,dn->lsn", values, matrix, preferred_element_type=F32)


def project_back(grads, matrix):
    return jnp.einsum("lsn,dn->lsd", grads, matrix, preferred_element_type=F32)


def outer_sum(values, grads):
    return jnp.einsum("lsd,lsn->dn", values, grads, preferred_element_type=F32)


def column_sum(grads):
    return jnp.sum(grads.astype(F32), axis=(0, 1))


def gelu_tanh(values):
    return jax.nn.gelu(values, approximate=True)


def local(
    latents,
    conditions,
    modulator,
    modbias,
    qkvweight,
    querybias,
    valuebias,
    projection,
    projbias,
    expand,
    expandbias,
    contract,
    contractbias,
    cotangent,
):
    n_dp, n_seq = lax.axis_size("dp"), lax.axis_size("seq")
    micro, lats, tok, width = latents.shape
    held = micro * lats
    assert held % n_seq == 0
    own = held // n_seq
    rows = width // n_dp
    chunk = width // n_seq
    wide = contract.shape[0] // rows
    head = width // H
    factor = head ** (-0.5)

    g1 = gather_seq(jnp.concatenate([qkvweight, projection], axis=1))
    g2 = gather_seq(expand)
    g3 = gather_seq(contract)
    u_qkv = g1[:, :, : 3 * chunk].transpose(1, 0, 2).reshape(rows, 3, width).transpose(1, 0, 2)
    u_proj = g1[:, :, 3 * chunk :].transpose(1, 0, 2).reshape(1, rows, width)
    u1 = jnp.concatenate([u_qkv, u_proj], axis=0)
    u2 = g2.transpose(1, 0, 2).reshape(rows, wide, width).transpose(1, 0, 2)
    u3 = g3.transpose(1, 0, 2).reshape(wide, rows, width)
    w1 = gather_dp(u1)
    w2 = gather_dp(u2)
    w3 = gather_dp(u3)
    qkv_matrix = w1[:, :3].transpose(0, 2, 1, 3).reshape(width, 3 * width)
    proj_matrix = w1[:, 3].reshape(width, width)
    up_matrix = w2.transpose(0, 2, 1, 3).reshape(width, wide * width)
    down_matrix = w3.reshape(wide * width, width)

    biases = (querybias, valuebias, projbias, expandbias, contractbias)
    gathered = gather_seq(jnp.concatenate(biases))
    sizes = [b.shape[0] for b in biases]
    starts = [sum(sizes[:i]) for i in range(len(sizes))]
    query_offset, value_offset, proj_offset, up_offset, down_offset = [
        gathered[:, a : a + n].reshape(-1).astype(F32) for a, n in zip(starts, sizes)
    ]

    def to_latents(values):
        values = values.reshape(held, tok, width)
        return lax.all_to_all(values, "seq", 0, 1, tiled=True)

    def to_tokens(values):
        values = lax.all_to_all(values, "seq", 1, 0, tiled=True)
        return values.reshape(micro, lats, tok, width)

    tokens = to_latents(latents).astype(F32)
    dout = to_latents(cotangent).astype(F32)

    cond_float = conditions.reshape(held, width).astype(F32)
    cond_act = jax.nn.silu(cond_float).astype(BF)
    cond_rows = lax.all_to_all(
        cond_act.reshape(held, n_dp, rows), "dp", 1, 0, tiled=True
    ).reshape(n_dp * held, rows)
    part = jnp.dot(cond_rows, modulator, preferred_element_type=F32)
    part = lax.all_to_all(part.reshape(n_dp, held, -1), "dp", 0, 0, tiled=True)
    piece = jnp.sum(part, axis=0) + modbias.astype(F32)
    modulation = lax.all_to_all(piece, "seq", 0, 1, tiled=True)
    pieces = jnp.split(modulation[:, None, :], 6, axis=-1)

    normed1, inverse1 = normalize(tokens)
    hidden1 = (normed1 * (1.0 + pieces[1]) + pieces[0]).astype(BF)
    offsets = jnp.concatenate([query_offset, jnp.zeros_like(query_offset), value_offset])
    qkv_low = (project(hidden1, qkv_matrix) + offsets).astype(BF)
    length = qkv_low.shape[1]
    queries = qkv_low[..., :width].reshape(own, length, H, head)
    keys = qkv_low[..., width : 2 * width].reshape(own, length, H, head)
    values = qkv_low[..., 2 * width :].reshape(own, length, H, head)
    scores = jnp.einsum("lshd,lthd->lhst", queries, keys, preferred_element_type=F32) * factor
    highest = jnp.max(scores, axis=-1, keepdims=True)
    expo = jnp.exp(scores - highest)
    totals = jnp.sum(expo, axis=-1, keepdims=True)
    probs = expo / totals
    probs_low = probs.astype(BF)
    attended = jnp.einsum("lhst,lthd->lshd", probs_low, values, preferred_element_type=F32)
    attended = attended.reshape(own, length, width).astype(BF)
    branch1 = project(attended, proj_matrix) + proj_offset
    middle = tokens + pieces[2] * branch1
    normed2, inverse2 = normalize(middle)
    hidden2 = (normed2 * (1.0 + pieces[4]) + pieces[3]).astype(BF)
    before = project(hidden2, up_matrix) + up_offset
    active = gelu_tanh(before).astype(BF)
    branch2 = project(active, down_matrix) + down_offset
    result = to_tokens((middle + pieces[5] * branch2).astype(BF))

    dbranch2 = (pieces[5] * dout).astype(BF)
    dgate2 = jnp.sum(dout * branch2, axis=1)
    grad_down = outer_sum(active, dbranch2).astype(BF)
    grad_down_offset = column_sum(dbranch2)
    s3 = scatter_dp(grad_down.reshape(n_dp, wide, rows, width))
    dactive = project_back(dbranch2, down_matrix)
    dbefore = jax.vjp(gelu_tanh, before)[1](dactive)[0].astype(BF)
    grad_up = outer_sum(hidden2, dbefore).astype(BF)
    grad_up_offset = column_sum(dbefore)
    s2 = scatter_dp(grad_up.reshape(n_dp, rows, wide, width).transpose(0, 2, 1, 3))
    dhidden2 = project_back(dbefore, up_matrix)
    dshift2 = jnp.sum(dhidden2, axis=1)
    dscale2 = jnp.sum(dhidden2 * normed2, axis=1)
    dmiddle = dout + norm_back(dhidden2 * (1.0 + pieces[4]), normed2, inverse2)
    dbranch1 = (pieces[2] * dmiddle).astype(BF)
    dgate1 = jnp.sum(dmiddle * branch1, axis=1)
    grad_proj = outer_sum(attended, dbranch1).astype(BF)
    grad_proj_offset = column_sum(dbranch1)
    dattended = project_back(dbranch1, proj_matrix).astype(BF)
    dattended = dattended.reshape(own, length, H, head)
    dprobs = jnp.einsum("lshd,lthd->lhst", dattended, values, preferred_element_type=F32)
    rowsum = jnp.sum(dprobs * probs, axis=-1, keepdims=True)
    dscores = (probs * (dprobs - rowsum)).astype(BF)
    dqueries = jnp.einsum("lhst,lthd->lshd", dscores, keys, preferred_element_type=F32) * factor
    dkeys = jnp.einsum("lhst,lshd->lthd", dscores, queries, preferred_element_type=F32) * factor
    dvalues = jnp.einsum("lhst,lshd->lthd", probs_low, dattended, preferred_element_type=F32)
    dqkv = jnp.concatenate(
        [part.reshape(own, length, width) for part in (dqueries, dkeys, dvalues)], axis=-1
    ).astype(BF)
    grad_qkv = outer_sum(hidden1, dqkv).astype(BF)
    grad_query_offset = column_sum(dqkv[..., :width])
    grad_value_offset = column_sum(dqkv[..., 2 * width :])
    grad1 = jnp.concatenate([grad_qkv, grad_proj], axis=1)
    s1 = scatter_dp(grad1.reshape(n_dp, rows, 4, width).transpose(0, 2, 1, 3))
    dhidden1 = project_back(dqkv, qkv_matrix)
    dshift1 = jnp.sum(dhidden1, axis=1)
    dscale1 = jnp.sum(dhidden1 * normed1, axis=1)
    dtokens = dmiddle + norm_back(dhidden1 * (1.0 + pieces[1]), normed1, inverse1)
    token_grad = to_tokens(dtokens.astype(BF))

    dmod = jnp.concatenate([dshift1, dscale1, dgate1, dshift2, dscale2, dgate2], axis=-1)
    offset_grads = (
        grad_query_offset, grad_value_offset, grad_proj_offset, grad_up_offset, grad_down_offset
    )
    offset_grads = jnp.concatenate([g.reshape(n_seq, -1) for g in offset_grads], axis=1)
    dmod_cols = dmod.reshape(own, n_seq, -1).transpose(1, 0, 2).reshape(n_seq, -1)
    small = jnp.concatenate([dmod_cols, offset_grads], axis=1).astype(BF)
    small = lax.all_to_all(small, "seq", 0, 0, tiled=True)
    small = lax.all_gather(small, "dp", axis=0, tiled=True)
    cols = modulator.shape[1]
    dmod_all = small[:, : own * cols].reshape(n_dp * held, cols)
    offset_sums = jnp.sum(small[:, own * cols :].astype(F32), axis=0)
    grad_mod = jnp.einsum("ld,ln->dn", cond_rows, dmod_all, preferred_element_type=F32)
    grad_mod_offset = jnp.sum(dmod_all.astype(F32), axis=0)
    dcond_rows = jnp.einsum("ln,dn->ld", dmod_all, modulator, preferred_element_type=F32)
    dcond = lax.all_to_all(dcond_rows.reshape(n_dp, held, rows), "dp", 0, 2, tiled=True)
    dcond = dcond.reshape(held, width)
    for bit in range(bits_of(n_seq)):
        dcond = dcond + swap(dcond, "seq", bit)
    dconds = jax.vjp(jax.nn.silu, cond_float)[1](dcond)[0].reshape(micro, lats, width)

    t1 = jnp.concatenate([s1[u] for u in range(3)], axis=1).reshape(rows, n_seq, 3 * chunk)
    t1 = jnp.concatenate([t1, s1[3].reshape(rows, n_seq, chunk)], axis=2).transpose(1, 0, 2)
    t2 = s2.transpose(1, 0, 2).reshape(rows, n_seq, -1).transpose(1, 0, 2)
    t3 = s3.reshape(wide * rows, n_seq, chunk).transpose(1, 0, 2)
    r3 = scatter_seq(t3)
    r2 = scatter_seq(t2)
    r1 = scatter_seq(t1)
    sums = [offset_sums[a : a + n] for a, n in zip(starts, sizes)]
    return (
        result,
        token_grad,
        dconds,
        grad_mod,
        grad_mod_offset,
        r1[:, : 3 * chunk],
        sums[0],
        sums[1],
        r1[:, 3 * chunk :],
        sums[2],
        r2,
        sums[3],
        r3,
        sums[4],
    )


def solution(mesh):
    placed = (
        P(None, "dp", "seq", None),
        P(None, "dp", None),
        P("dp", "seq"),
        P("seq"),
        P("dp", "seq"),
        P("seq"),
        P("seq"),
        P("dp", "seq"),
        P("seq"),
        P("dp", "seq"),
        P("seq"),
        P("dp", "seq"),
        P("seq"),
        P(None, "dp", "seq", None),
    )
    return jax.shard_map(
        local,
        mesh=mesh,
        in_specs=placed,
        out_specs=(
            P(None, "dp", "seq", None),
            P(None, "dp", "seq", None),
            P(None, "dp", None),
            P("dp", "seq"),
            P("seq"),
            P("dp", "seq"),
            P("seq"),
            P("seq"),
            P("dp", "seq"),
            P("seq"),
            P("dp", "seq"),
            P("seq"),
            P("dp", "seq"),
            P("seq"),
        ),
        check_vma=False,
    )
```

```python
import functools

import jax
import jax.numpy as jnp
from jax import lax
from jax.experimental import pallas as pl
from jax.experimental.pallas import tpu as pltpu
from jax.sharding import PartitionSpec as P

H = 12
EPSILON = 1e-06
BF = jnp.bfloat16
F32 = jnp.float32


def bits_of(count):
    bits = count.bit_length() - 1
    assert 1 << bits == count
    return bits


def swap(values, axis, bit):
    count = lax.axis_size(axis)
    return lax.ppermute(values, axis, [(i, i ^ (1 << bit)) for i in range(count)])


def own_bit(axis, bit):
    return (lax.axis_index(axis) >> bit) & 1


def join(values, axis, bit):
    other = swap(values, axis, bit)
    mine = own_bit(axis, bit) == 0
    return jnp.stack([jnp.where(mine, values, other), jnp.where(mine, other, values)])


def halve(values, axis, bit):
    index = own_bit(axis, bit)
    sent = lax.dynamic_index_in_dim(values, 1 - index, 0, keepdims=False)
    kept = lax.dynamic_index_in_dim(values, index, 0, keepdims=False)
    other = swap(sent.astype(BF), axis, bit)
    return kept.astype(F32) + other.astype(F32)


def gather_seq(values):
    count = bits_of(lax.axis_size("seq"))
    shape = values.shape
    for bit in range(count - 1, -1, -1):
        values = join(values, "seq", bit)
    values = values.transpose(list(range(count - 1, -1, -1)) + list(range(count, count + len(shape))))
    return values.reshape((1 << count,) + shape)


def scatter_seq(values):
    count = bits_of(lax.axis_size("seq"))
    shape = values.shape[1:]
    values = values.reshape((2,) * count + shape)
    values = values.transpose(list(range(count - 1, -1, -1)) + list(range(count, count + len(shape))))
    for bit in range(count):
        values = halve(values, "seq", bit)
    return values


def upper_orders():
    upper = list(range(1, bits_of(lax.axis_size("dp"))))
    return (upper, upper[::-1])


class Layout:
    def __init__(self, n_dp, rows, width):
        self.direct = rows % 16 == 0 and n_dp > 1
        self.blocks = n_dp if self.direct else 1
        self.rows = rows if self.direct else width


def mask_of(place, order):
    return sum(((place >> j) & 1) << bit for j, bit in enumerate(order))


def gather_dp(units, layout):
    half = units.shape[-1] // 2
    pieces = []
    for index, order in enumerate(upper_orders()):
        part = units[None, :, :, index * half : (index + 1) * half]
        for bit in order:
            part = jnp.concatenate([part, swap(part, "dp", bit)], axis=0)
        other = swap(part, "dp", 0)
        masks = [mask_of(place, order) for place in range(part.shape[0])]
        pieces.append((part, masks, index * half))
        pieces.append((other, [mask | 1 for mask in masks], index * half))
    if layout.direct:
        return pieces
    me = lax.axis_index("dp")
    whole = []
    for first in range(0, len(pieces), 2):
        both = jnp.concatenate([pieces[first][0], pieces[first + 1][0]])
        masks = pieces[first][1] + pieces[first + 1][1]
        place = [0] * len(masks)
        for index, mask in enumerate(masks):
            place[mask] = index
        wanted = jnp.asarray(place)[jnp.arange(len(masks)) ^ me]
        whole.append((jnp.take(both, wanted, axis=0), pieces[first][2]))
    return whole


def scatter_dp(kept, sent):
    count = bits_of(lax.axis_size("dp"))
    other = swap(sent, "dp", 0)
    half = kept.shape[-1] // 2
    parts = []
    for index, order in enumerate(upper_orders()):
        cut = lambda v: v[..., index * half : (index + 1) * half].reshape(
            (2,) * (count - 1) + v.shape[1:-1] + (half,)
        )
        part = cut(kept).astype(F32) + cut(other).astype(F32)
        left = list(range(count - 1, 0, -1))
        for bit in order[::-1]:
            axis = left.index(bit)
            left.remove(bit)
            away = lax.index_in_dim(part, 1, axis, keepdims=False).astype(BF)
            part = lax.index_in_dim(part, 0, axis, keepdims=False) + swap(away, "dp", bit).astype(F32)
        parts.append(part)
    return parts


def dot(a, b):
    return jnp.dot(a, b, preferred_element_type=F32)


def dot_back(a, b):
    return lax.dot_general(a, b, (((1,), (1,)), ((), ())), preferred_element_type=F32)


def dot_outer(a, b):
    return lax.dot_general(a, b, (((0,), (0,)), ((), ())), preferred_element_type=F32)


def normalize(values):
    center = values - jnp.mean(values, axis=-1, keepdims=True)
    inverse = lax.rsqrt(jnp.mean(center * center, axis=-1, keepdims=True) + EPSILON)
    return (center * inverse, inverse)


def norm_back(grad_normed, normed, inverse):
    first = jnp.mean(grad_normed, axis=-1, keepdims=True)
    second = jnp.mean(grad_normed * normed, axis=-1, keepdims=True)
    return inverse * (grad_normed - first - normed * second)


def total(values):
    return jnp.sum(values.astype(F32), axis=0, keepdims=True)


def loads(pieces, refs, me, target, sems):
    copies = []
    for ref, (masks, column) in zip(refs, pieces):
        for place, mask in enumerate(masks):
            for view, units in target(me ^ mask, column, ref.shape[-1]):
                copies.append(
                    pltpu.make_async_copy(
                        ref.at[place, units[0] : units[1]], view, sems.at[len(copies)]
                    )
                )
    return copies


def start(copies):
    for copy in copies:
        copy.start()


def finish(copies):
    for copy in copies:
        copy.wait()


def by_unit(scratch, first, last):
    return lambda block, column, columns: [
        (scratch.at[:, block, :, pl.ds(column, columns)], (first, last))
    ]


def by_block(scratch, first, last):
    return lambda block, column, columns: [
        (scratch.at[block, :, :, pl.ds(column, columns)], (first, last))
    ]


def matrix_of(scratch, unit):
    block = scratch[unit]
    return block.reshape(block.shape[0] * block.shape[1], block.shape[2])


def stores(scratch, outs, me, units, sems, base):
    copies = []
    blocks = scratch.shape[0]
    for mask in range(blocks):
        out = outs[mask & 1] if blocks > 1 else outs[0]
        place = mask >> 1
        copies.append(
            pltpu.make_async_copy(
                scratch.at[me ^ mask], out.at[place, units[0] : units[1]], sems.at[base + len(copies)]
            )
        )
    return copies


def lanes(shape):
    return lax.broadcasted_iota(jnp.int32, shape, 1)


def attend_kernel(spec, me_ref, tokens_ref, mod_ref, qkv_off_ref, proj_off_ref, *rest):
    width, pieces, factor, pairs = spec
    refs, rest = rest[: len(pieces)], rest[len(pieces) :]
    hidden_ref, qkv_ref, att_ref, branch_ref, middle_ref, weights, sems = rest
    me = me_ref[0]
    copies = loads(pieces, refs, me, by_unit(weights, 0, 4), sems)
    start(copies)
    tokens = tokens_ref[...].astype(F32)
    part = lambda i: mod_ref[:, i * width : (i + 1) * width]
    normed, _ = normalize(tokens)
    hidden = (normed * (1.0 + part(1)) + part(0)).astype(BF)
    hidden_ref[...] = hidden
    finish(copies)
    for unit in range(3):
        offset = qkv_off_ref[:, unit * width : (unit + 1) * width]
        qkv_ref[unit] = (dot(hidden, matrix_of(weights, unit)) + offset).astype(BF)
    for pair in range(pairs):
        cols = slice(pair * 128, (pair + 1) * 128)
        q, k, v = qkv_ref[0, :, cols], qkv_ref[1, :, cols], qkv_ref[2, :, cols]
        first = lanes(k.shape) < 64
        mixed = []
        for which in range(2):
            masked = jnp.where(first if which == 0 else ~first, k, jnp.zeros_like(k))
            scores = dot_back(q, masked) * factor
            expo = jnp.exp(scores - jnp.max(scores, axis=-1, keepdims=True))
            probs = expo * (1.0 / jnp.sum(expo, axis=-1, keepdims=True))
            mixed.append(dot(probs.astype(BF), v))
        att_ref[:, cols] = jnp.where(first, mixed[0], mixed[1]).astype(BF)
    branch = dot(att_ref[...], matrix_of(weights, 3)) + proj_off_ref[...]
    branch_ref[...] = branch
    middle_ref[...] = tokens + part(2) * branch


GELU_C = 0.7978845608028654
GELU_A = 0.044715


def mlp_kernel(spec, me_ref, middle_ref, mod_ref, cot_ref, up_off_ref, down_off_ref, *rest):
    width, wide, pieces = spec
    refs, rest = rest[: len(pieces)], rest[len(pieces) :]
    outs, rest = rest[: len(rest) - 14], rest[len(rest) - 14 :]
    (
        result_ref, dbefore_ref, gate_ref, up_bias_ref, down_bias_ref,
        up, down, up_grad, down_grad, active, slope, up_sems, down_sems, out_sems,
    ) = rest
    me = me_ref[0]
    up_copies = loads(pieces, refs, me, by_unit(up, 0, wide), up_sems)
    down_copies = loads(pieces, refs, me, by_block(down, wide, 2 * wide), down_sems)
    start(up_copies)
    start(down_copies)
    part = lambda i: mod_ref[:, i * width : (i + 1) * width]
    middle = middle_ref[...]
    cot = cot_ref[...].astype(F32)
    normed, _ = normalize(middle)
    hidden = (normed * (1.0 + part(4)) + part(3)).astype(BF)
    gate = part(5)
    dbranch = (gate * cot).astype(BF)
    down_bias_ref[...] = total(dbranch)
    finish(up_copies)
    for unit in range(wide):
        before = dot(hidden, matrix_of(up, unit)) + up_off_ref[:, unit * width : (unit + 1) * width]
        square = before * before
        bent = jnp.tanh(GELU_C * before * (1.0 + GELU_A * square))
        active[unit] = (0.5 * before * (1.0 + bent)).astype(BF)
        slope[unit] = 0.5 * (1.0 + bent) + (0.5 * GELU_C) * before * (1.0 - bent * bent) * (
            1.0 + (3.0 * GELU_A) * square
        )
    finish(down_copies)
    down_rows = down[...].reshape(wide * width, width)
    grads = down_grad.shape
    span = grads[0] // wide if grads[0] > 1 else 0
    branch = down_off_ref[...]
    for unit in range(wide):
        branch = branch + dot(active[unit], down_rows[unit * width : (unit + 1) * width])
        grad = dot_outer(active[unit], dbranch).astype(BF)
        if span:
            down_grad[unit * span : (unit + 1) * span] = grad.reshape((span,) + grads[1:])
        else:
            down_grad[0, unit] = grad
    down_stores = stores(down_grad, outs, me, (wide, 2 * wide), out_sems, 0)
    start(down_stores)
    result_ref[...] = (middle + gate * branch).astype(BF)
    gate_ref[...] = total(cot * branch)
    for unit in range(wide):
        dactive = dot_back(dbranch, down_rows[unit * width : (unit + 1) * width])
        dbefore = (dactive * slope[unit]).astype(BF)
        dbefore_ref[unit] = dbefore
        up_bias_ref[:, unit * width : (unit + 1) * width] = total(dbefore)
        grad = dot_outer(hidden, dbefore).astype(BF)
        up_grad[:, unit] = grad.reshape(up_grad.shape[0], up_grad.shape[2], width)
    up_stores = stores(up_grad, outs, me, (0, wide), out_sems, up_grad.shape[0])
    start(up_stores)
    finish(down_stores)
    finish(up_stores)


def attend_back_kernel(spec, me_ref, middle_ref, mod_ref, cot_ref, dbefore_ref, branch_ref, att_ref,
                       hidden_ref, qkv_ref, *rest):
    width, wide, up_pieces, pieces, factor, pairs = spec
    up_refs, rest = rest[: len(up_pieces)], rest[len(up_pieces) :]
    refs, rest = rest[: len(pieces)], rest[len(pieces) :]
    outs, rest = rest[: len(rest) - 10], rest[len(rest) - 10 :]
    dmiddle_ref, dqkv_ref, sums_ref, bias_ref, up, proj, grads, up_sems, proj_sems, out_sems = rest
    me = me_ref[0]
    up_copies = loads(up_pieces, up_refs, me, by_unit(up, 0, wide), up_sems)
    proj_copies = loads(pieces, refs, me, by_unit(proj, 3, 4), proj_sems)
    start(up_copies)
    start(proj_copies)
    part = lambda i: mod_ref[:, i * width : (i + 1) * width]
    normed, inverse = normalize(middle_ref[...])
    finish(up_copies)
    dhidden = dot_back(dbefore_ref[0], matrix_of(up, 0))
    for unit in range(1, wide):
        dhidden = dhidden + dot_back(dbefore_ref[unit], matrix_of(up, unit))
    dmiddle = cot_ref[...].astype(F32) + norm_back(dhidden * (1.0 + part(4)), normed, inverse)
    dmiddle_ref[...] = dmiddle
    dbranch = (part(2) * dmiddle).astype(BF)
    sums_ref[:, :width] = total(dmiddle * branch_ref[...])
    sums_ref[:, width : 2 * width] = total(dhidden)
    sums_ref[:, 2 * width : 3 * width] = total(dhidden * normed)
    bias_ref[:, 2 * width : 3 * width] = total(dbranch)
    finish(proj_copies)
    datt = dot_back(dbranch, matrix_of(proj, 0)).astype(BF)
    for pair in range(pairs):
        cols = slice(pair * 128, (pair + 1) * 128)
        q, k, v = qkv_ref[0, :, cols], qkv_ref[1, :, cols], qkv_ref[2, :, cols]
        da = datt[:, cols]
        first = lanes(k.shape) < 64
        zero = jnp.zeros_like(k)
        grad_q, grad_k, grad_v = [], [], []
        for which in range(2):
            own = first if which == 0 else ~first
            scores = dot_back(q, jnp.where(own, k, zero)) * factor
            expo = jnp.exp(scores - jnp.max(scores, axis=-1, keepdims=True))
            probs = expo * (1.0 / jnp.sum(expo, axis=-1, keepdims=True))
            dprobs = dot_back(da, jnp.where(own, v, zero))
            rowsum = jnp.sum(dprobs * probs, axis=-1, keepdims=True)
            dscores = (probs * (dprobs - rowsum)).astype(BF)
            grad_q.append(dot(dscores, k))
            grad_k.append(dot_outer(dscores, q))
            grad_v.append(dot_outer(probs.astype(BF), da))
        dqkv_ref[0, :, cols] = (jnp.where(first, grad_q[0], grad_q[1]) * factor).astype(BF)
        dqkv_ref[1, :, cols] = (jnp.where(first, grad_k[0], grad_k[1]) * factor).astype(BF)
        dqkv_ref[2, :, cols] = jnp.where(first, grad_v[0], grad_v[1]).astype(BF)
    bias_ref[:, :width] = total(dqkv_ref[0])
    bias_ref[:, width : 2 * width] = total(dqkv_ref[2])
    shape = (grads.shape[0], grads.shape[2], width)
    for unit in range(3):
        grads[:, unit] = dot_outer(hidden_ref[...], dqkv_ref[unit]).astype(BF).reshape(shape)
    grads[:, 3] = dot_outer(att_ref[...], dbranch).astype(BF).reshape(shape)
    out_copies = stores(grads, outs, me, (0, 4), out_sems, 0)
    start(out_copies)
    finish(out_copies)


def input_back_kernel(spec, me_ref, tokens_ref, mod_ref, dmiddle_ref, dqkv_ref, *rest):
    width, pieces = spec
    refs, rest = rest[: len(pieces)], rest[len(pieces) :]
    dtokens_ref, sums_ref, weights, sems = rest
    copies = loads(pieces, refs, me_ref[0], by_unit(weights, 0, 3), sems)
    start(copies)
    normed, inverse = normalize(tokens_ref[...].astype(F32))
    finish(copies)
    dhidden = dot_back(dqkv_ref[0], matrix_of(weights, 0))
    for unit in range(1, 3):
        dhidden = dhidden + dot_back(dqkv_ref[unit], matrix_of(weights, unit))
    sums_ref[:, :width] = total(dhidden)
    sums_ref[:, width : 2 * width] = total(dhidden * normed)
    scale = 1.0 + mod_ref[:, width : 2 * width]
    dtokens_ref[...] = (dmiddle_ref[...] + norm_back(dhidden * scale, normed, inverse)).astype(BF)


def call(body, spec, me, inputs, pieces, outs, far_outs, scratch, flops, name):
    vmem = pl.BlockSpec(memory_space=pltpu.VMEM)
    far = pl.BlockSpec(memory_space=pl.ANY)
    moved = sum(v.size * v.dtype.itemsize for v in list(inputs) + list(pieces))
    return pl.pallas_call(
        functools.partial(body, spec),
        out_shape=far_outs + outs,
        in_specs=[pl.BlockSpec(memory_space=pltpu.SMEM)] + [vmem] * len(inputs) + [far] * len(pieces),
        out_specs=[far] * len(far_outs) + [vmem] * len(outs),
        scratch_shapes=scratch,
        compiler_params=pltpu.CompilerParams(vmem_limit_bytes=52 * 1024 * 1024),
        cost_estimate=pl.CostEstimate(flops=flops, bytes_accessed=moved, transcendentals=0),
        name=name,
    )(me, *inputs, *pieces)


def local(
    latents,
    conditions,
    modulator,
    modbias,
    qkvweight,
    querybias,
    valuebias,
    projection,
    projbias,
    expand,
    expandbias,
    contract,
    contractbias,
    cotangent,
):
    n_dp, n_seq = lax.axis_size("dp"), lax.axis_size("seq")
    micro, lats, tok, width = latents.shape
    held = micro * lats
    assert held == n_seq
    length = n_seq * tok
    rows = width // n_dp
    chunk = width // n_seq
    wide = contract.shape[0] // rows
    head = width // H
    assert 2 * head == 128
    factor = head ** (-0.5)
    layout = Layout(n_dp, rows, width)

    g1 = gather_seq(jnp.concatenate([qkvweight, projection], axis=1))
    u_qkv = g1[:, :, : 3 * chunk].transpose(1, 0, 2).reshape(rows, 3, width).transpose(1, 0, 2)
    u_proj = g1[:, :, 3 * chunk :].transpose(1, 0, 2).reshape(1, rows, width)
    u1 = jnp.concatenate([u_qkv, u_proj], axis=0)
    g2 = gather_seq(jnp.stack([expand, contract.reshape(wide, rows, chunk).transpose(1, 0, 2).reshape(rows, -1)]))
    u2 = g2[:, 0].transpose(1, 0, 2).reshape(rows, wide, width).transpose(1, 0, 2)
    u3 = g2[:, 1].reshape(n_seq, rows, wide, chunk).transpose(2, 1, 0, 3).reshape(wide, rows, width)
    w1 = gather_dp(u1, layout)
    w2 = gather_dp(jnp.concatenate([u2, u3]), layout)
    if layout.direct:
        me = lax.axis_index("dp").reshape(1).astype(jnp.int32)
    else:
        me = jnp.zeros((1,), jnp.int32)
        natural = lambda v: v.transpose(1, 0, 2, 3).reshape(1, v.shape[1], width, -1)
        stacked = lambda v: v.reshape(1, v.shape[1], width, -1)
        w1 = [(natural(v), [0], column) for v, column in w1]
        w2 = [
            (jnp.concatenate([natural(v[:, :wide]), stacked(v[:, wide:])], axis=1), [0], column)
            for v, column in w2
        ]
    arrays1, spec1 = [w[0] for w in w1], tuple(w[1:] for w in w1)
    arrays2, spec2 = [w[0] for w in w2], tuple(w[1:] for w in w2)

    biases = (querybias, valuebias, projbias, expandbias, contractbias)
    gathered = gather_seq(jnp.concatenate(biases))
    sizes = [b.shape[0] for b in biases]
    starts = [sum(sizes[:i]) for i in range(len(sizes))]
    query_offset, value_offset, proj_offset, up_offset, down_offset = [
        gathered[:, a : a + n].reshape(1, -1).astype(F32) for a, n in zip(starts, sizes)
    ]

    def to_latents(values):
        values = values.reshape(held, tok, width)
        return lax.all_to_all(values, "seq", 0, 0, tiled=True).reshape(length, width)

    def to_tokens(values):
        values = values.reshape(n_seq, tok, width)
        values = lax.all_to_all(values, "seq", 0, 0, tiled=True)
        return values.reshape(micro, lats, tok, width)

    tokens = to_latents(latents)
    cot = to_latents(cotangent)

    cond_float = conditions.reshape(held, width).astype(F32)
    cond_act = jax.nn.silu(cond_float).astype(BF)
    cond_rows = lax.all_to_all(
        cond_act.reshape(held, n_dp, rows), "dp", 1, 0, tiled=True
    ).reshape(n_dp * held, rows)
    part = jnp.dot(cond_rows, modulator, preferred_element_type=F32)
    part = lax.all_to_all(part.reshape(n_dp, held, -1), "dp", 0, 0, tiled=True)
    piece = jnp.sum(part, axis=0) + modbias.astype(F32)
    mod = lax.all_to_all(piece, "seq", 0, 1, tiled=True)

    shaped = jax.ShapeDtypeStruct
    pairs = H // 2
    blocks, block_rows = layout.blocks, layout.rows
    places = max(blocks // 2, 1)
    n_far = min(blocks, 2)
    n1, n2 = (sum(len(w[1]) for w in ws) for ws in (w1, w2))
    square = 2 * length * width * width
    dma = pltpu.SemaphoreType.DMA
    offsets = jnp.concatenate([query_offset, jnp.zeros_like(query_offset), value_offset], axis=1)
    hidden1, qkv, attended, branch1, middle = call(
        attend_kernel,
        (width, spec1, factor, pairs),
        me,
        [tokens, mod, offsets, proj_offset],
        arrays1,
        [
            shaped((length, width), BF),
            shaped((3, length, width), BF),
            shaped((length, width), BF),
            shaped((length, width), F32),
            shaped((length, width), F32),
        ],
        [],
        [pltpu.VMEM((4, blocks, block_rows, width), BF), dma((n1,))],
        6 * square,
        "attention",
    )
    *grads2, result, dbefore, dgate2, up_bias, down_bias = call(
        mlp_kernel,
        (width, wide, spec2),
        me,
        [middle, mod, cot, up_offset, down_offset],
        arrays2,
        [
            shaped((length, width), BF),
            shaped((wide, length, width), BF),
            shaped((1, width), F32),
            shaped((1, wide * width), F32),
            shaped((1, width), F32),
        ],
        [shaped((places, 2 * wide, block_rows, width), BF)] * n_far,
        [
            pltpu.VMEM((wide, blocks, block_rows, width), BF),
            pltpu.VMEM((blocks, wide, block_rows, width), BF),
            pltpu.VMEM((blocks, wide, block_rows, width), BF),
            pltpu.VMEM((blocks, wide, block_rows, width), BF),
            pltpu.VMEM((wide, length, width), BF),
            pltpu.VMEM((wide, length, width), F32),
            dma((n2,)),
            dma((n2,)),
            dma((2 * blocks,)),
        ],
        5 * wide * square,
        "mlp",
    )
    *grads1, dmiddle, dqkv, sums1, bias1 = call(
        attend_back_kernel,
        (width, wide, spec2, spec1, factor, pairs),
        me,
        [middle, mod, cot, dbefore, branch1, attended, hidden1, qkv],
        arrays2 + arrays1,
        [
            shaped((length, width), F32),
            shaped((3, length, width), BF),
            shaped((1, 3 * width), F32),
            shaped((1, 3 * width), F32),
        ],
        [shaped((places, 4, block_rows, width), BF)] * n_far,
        [
            pltpu.VMEM((wide, blocks, block_rows, width), BF),
            pltpu.VMEM((1, blocks, block_rows, width), BF),
            pltpu.VMEM((blocks, 4, block_rows, width), BF),
            dma((n2,)),
            dma((n1,)),
            dma((blocks,)),
        ],
        15 * square,
        "attention_back",
    )
    dtokens, sums0 = call(
        input_back_kernel,
        (width, spec1),
        me,
        [tokens, mod, dmiddle, dqkv],
        arrays1,
        [shaped((length, width), BF), shaped((1, 2 * width), F32)],
        [],
        [pltpu.VMEM((3, blocks, block_rows, width), BF), dma((n1,))],
        3 * square,
        "input_back",
    )
    result = to_tokens(result)
    token_grad = to_tokens(dtokens)

    def relative(grads, by_row):
        if layout.direct:
            return grads
        whole = grads[0][0]
        here = lax.axis_index("dp")
        if by_row:
            whole = whole.reshape(n_dp, -1, rows, width)
        else:
            whole = whole.reshape(-1, n_dp, rows, width).transpose(1, 0, 2, 3)
        order = jnp.arange(n_dp // 2) * 2
        return [jnp.take(whole, (order + low) ^ here, axis=0) for low in range(2)]

    if layout.direct:
        pass
    else:
        up_part = relative([grads2[0][:, :wide]], False)
        down_part = relative([grads2[0][:, wide:]], True)
        grads2 = [jnp.concatenate([a, b], axis=1) for a, b in zip(up_part, down_part)]
        grads1 = relative(grads1, False)
    s2 = jnp.concatenate(scatter_dp(*grads2), axis=-1)
    s1 = jnp.concatenate(scatter_dp(*grads1), axis=-1)

    dmod = jnp.concatenate([sums0, sums1[:, :width], sums1[:, width:], dgate2], axis=1)
    offset_grads = (
        bias1[:, :width], bias1[:, width : 2 * width], bias1[:, 2 * width :], up_bias, down_bias
    )
    offset_grads = jnp.concatenate([g.reshape(n_seq, -1) for g in offset_grads], axis=1)
    small = jnp.concatenate([dmod.reshape(n_seq, -1), offset_grads], axis=1).astype(BF)
    small = lax.all_to_all(small, "seq", 0, 0, tiled=True)
    small = lax.all_gather(small, "dp", axis=0, tiled=True)
    cols = modulator.shape[1]
    dmod_all = small[:, :cols]
    offset_sums = jnp.sum(small[:, cols:].astype(F32), axis=0)
    grad_mod = jnp.einsum("ld,ln->dn", cond_rows, dmod_all, preferred_element_type=F32)
    grad_mod_offset = jnp.sum(dmod_all.astype(F32), axis=0)
    dcond_rows = jnp.einsum("ln,dn->ld", dmod_all, modulator, preferred_element_type=F32)
    dcond = lax.all_to_all(dcond_rows.reshape(n_dp, held, rows), "dp", 0, 2, tiled=True)
    dcond = dcond.reshape(held, width)
    for bit in range(bits_of(n_seq)):
        dcond = dcond + swap(dcond, "seq", bit)
    dconds = jax.vjp(jax.nn.silu, cond_float)[1](dcond)[0].reshape(micro, lats, width)

    t1 = jnp.concatenate([s1[u] for u in range(3)], axis=1).reshape(rows, n_seq, 3 * chunk)
    t1 = jnp.concatenate([t1, s1[3].reshape(rows, n_seq, chunk)], axis=2).transpose(1, 0, 2)
    t2 = s2[:wide].transpose(1, 0, 2).reshape(rows, n_seq, -1).transpose(1, 0, 2)
    t3 = s2[wide:].reshape(wide, rows, n_seq, chunk).transpose(2, 1, 0, 3).reshape(n_seq, rows, -1)
    r2 = scatter_seq(jnp.stack([t2, t3], axis=1))
    r1 = scatter_seq(t1)
    down_out = r2[1].reshape(rows, wide, chunk).transpose(1, 0, 2).reshape(wide * rows, chunk)
    sums = [offset_sums[a : a + n] for a, n in zip(starts, sizes)]
    return (
        result,
        token_grad,
        dconds,
        grad_mod,
        grad_mod_offset,
        r1[:, : 3 * chunk],
        sums[0],
        sums[1],
        r1[:, 3 * chunk :],
        sums[2],
        r2[0],
        sums[3],
        down_out,
        sums[4],
    )


def solution(mesh):
    placed = (
        P(None, "dp", "seq", None),
        P(None, "dp", None),
        P("dp", "seq"),
        P("seq"),
        P("dp", "seq"),
        P("seq"),
        P("seq"),
        P("dp", "seq"),
        P("seq"),
        P("dp", "seq"),
        P("seq"),
        P("dp", "seq"),
        P("seq"),
        P(None, "dp", "seq", None),
    )
    return jax.shard_map(
        local,
        mesh=mesh,
        in_specs=placed,
        out_specs=(
            P(None, "dp", "seq", None),
            P(None, "dp", "seq", None),
            P(None, "dp", None),
            P("dp", "seq"),
            P("seq"),
            P("dp", "seq"),
            P("seq"),
            P("seq"),
            P("dp", "seq"),
            P("seq"),
            P("dp", "seq"),
            P("seq"),
            P("dp", "seq"),
            P("seq"),
        ),
        check_vma=False,
    )
```

```python
import functools

import jax
import jax.numpy as jnp
from jax import lax
from jax.experimental import pallas as pl
from jax.experimental.pallas import tpu as pltpu
from jax.sharding import PartitionSpec as P

H = 12
EPSILON = 1e-06
BF = jnp.bfloat16
F32 = jnp.float32


def bits_of(count):
    bits = count.bit_length() - 1
    assert 1 << bits == count
    return bits


def swap(values, axis, bit):
    count = lax.axis_size(axis)
    return lax.ppermute(values, axis, [(i, i ^ (1 << bit)) for i in range(count)])


def own_bit(axis, bit):
    return (lax.axis_index(axis) >> bit) & 1


def halve(values, axis, bit):
    index = own_bit(axis, bit)
    sent = lax.dynamic_index_in_dim(values, 1 - index, 0, keepdims=False)
    kept = lax.dynamic_index_in_dim(values, index, 0, keepdims=False)
    other = swap(sent.astype(BF), axis, bit)
    return kept.astype(F32) + other.astype(F32)


def scatter_seq(values):
    count = bits_of(lax.axis_size("seq"))
    shape = values.shape[1:]
    values = values.reshape((2,) * count + shape)
    values = values.transpose(list(range(count - 1, -1, -1)) + list(range(count, count + len(shape))))
    for bit in range(count):
        values = halve(values, "seq", bit)
    return values


class Layout:
    def __init__(self, n_dp, rows, width):
        self.direct = rows % 16 == 0 and n_dp == 8
        self.blocks = n_dp if self.direct else 1
        self.rows = rows if self.direct else width


def mask_of(place, order):
    return sum(((place >> j) & 1) << bit for j, bit in enumerate(order))


def gather_dp(units):
    part = units[None]
    order = list(range(bits_of(lax.axis_size("dp"))))[::-1]
    for bit in order:
        part = jnp.concatenate([part, swap(part, "dp", bit)], axis=0)
    count = part.shape[0]
    place = [0] * count
    for index in range(count):
        place[mask_of(index, order)] = index
    wanted = jnp.asarray(place)[jnp.arange(count) ^ lax.axis_index("dp")]
    return jnp.take(part, wanted, axis=0)


def scatter_dp(values):
    count = bits_of(values.shape[0])
    values = jnp.take(values, jnp.arange(1 << count) ^ lax.axis_index("dp"), axis=0)
    values = values.reshape((2,) * count + values.shape[1:]).astype(F32)
    for bit in range(count - 1, -1, -1):
        values = values[0] + swap(values[1].astype(BF), "dp", bit).astype(F32)
    return values


def gather_square(units):
    middle = units.shape[0] // 2
    over_x, over_y = swap(units, "dp", 1), swap(units, "dp", 2)
    low = swap(over_x[:middle], "dp", 2)
    high = swap(over_y[middle:], "dp", 1)
    near = [(units, 0, 0), (over_x, 2, 0), (over_y, 4, 0), (low, 6, 0), (high, 6, middle)]
    far = [(swap(part, "dp", 0), mask | 1, first) for part, mask, first in near]
    return [entry for pair in zip(near, far) for entry in pair]


def scatter_square(kept, sent):
    other = swap(sent, "dp", 0)
    middle = kept.shape[1] // 2
    both = lambda place, units: kept[place, units].astype(F32) + other[place, units].astype(F32)
    low, high, every = slice(0, middle), slice(middle, None), slice(0, None)
    low_in = swap(both(3, low).astype(BF), "dp", 2)
    high_in = swap(both(3, high).astype(BF), "dp", 1)
    to_x = jnp.concatenate([both(1, low) + low_in.astype(F32), both(1, high)]).astype(BF)
    to_y = jnp.concatenate([both(2, low), both(2, high) + high_in.astype(F32)]).astype(BF)
    return (kept, other, swap(to_x, "dp", 1), swap(to_y, "dp", 2))


def swap_seq(values):
    count = lax.axis_size("seq")
    return [
        lax.ppermute(values[mask - 1] if isinstance(values, list) else values, "seq",
                     [(i, i ^ mask) for i in range(count)])
        for mask in range(1, count)
    ]


def dot(a, b):
    return jnp.dot(a, b, preferred_element_type=F32)


def dot_back(a, b):
    return lax.dot_general(a, b, (((1,), (1,)), ((), ())), preferred_element_type=F32)


def dot_outer(a, b):
    return lax.dot_general(a, b, (((0,), (0,)), ((), ())), preferred_element_type=F32)


def normalize(values):
    center = values - jnp.mean(values, axis=-1, keepdims=True)
    inverse = lax.rsqrt(jnp.mean(center * center, axis=-1, keepdims=True) + EPSILON)
    return (center * inverse, inverse)


def norm_back(grad_normed, normed, inverse):
    first = jnp.mean(grad_normed, axis=-1, keepdims=True)
    second = jnp.mean(grad_normed * normed, axis=-1, keepdims=True)
    return inverse * (grad_normed - first - normed * second)


def total(values):
    return jnp.sum(values.astype(F32), axis=0, keepdims=True)


def loads(pieces, refs, me, target, span, sems):
    copies = []
    for ref, (mask, first) in zip(refs, pieces):
        low, high = max(span[0], first), min(span[1], first + ref.shape[0])
        if low < high:
            view = target(me ^ mask, low - span[0], high - span[0])
            copies.append(
                pltpu.make_async_copy(ref.at[low - first : high - first], view, sems.at[len(copies)])
            )
    return copies


def start(copies):
    for copy in copies:
        copy.start()


def finish(copies):
    for copy in copies:
        copy.wait()


def by_unit(scratch):
    return lambda block, low, high: scratch.at[low:high, block]


def by_block(scratch):
    return lambda block, low, high: scratch.at[block, low:high]


def matrix_of(scratch, unit):
    block = scratch[unit]
    return block.reshape(block.shape[0] * block.shape[1], block.shape[2])


def stores(scratch, outs, me, units, sems, base):
    copies = []
    blocks = scratch.shape[0]
    for mask in range(blocks):
        out = outs[mask & 1] if blocks > 1 else outs[0]
        place = mask >> 1
        copies.append(
            pltpu.make_async_copy(
                scratch.at[me ^ mask], out.at[place, units[0] : units[1]], sems.at[base + len(copies)]
            )
        )
    return copies


def lanes(shape):
    return lax.broadcasted_iota(jnp.int32, shape, 1)


def attend_kernel(spec, me_ref, tokens_ref, mod_ref, qkv_off_ref, proj_off_ref, *rest):
    width, pieces, factor, pairs = spec
    refs, rest = rest[: len(pieces)], rest[len(pieces) :]
    hidden_ref, qkv_ref, att_ref, branch_ref, middle_ref, weights, sems = rest
    me = me_ref[0]
    copies = loads(pieces, refs, me, by_unit(weights), (0, 4), sems)
    start(copies)
    tokens = tokens_ref[...].astype(F32)
    part = lambda i: mod_ref[:, i * width : (i + 1) * width]
    normed, _ = normalize(tokens)
    hidden = (normed * (1.0 + part(1)) + part(0)).astype(BF)
    hidden_ref[...] = hidden
    finish(copies)
    for unit in range(3):
        offset = qkv_off_ref[:, unit * width : (unit + 1) * width]
        qkv_ref[unit] = (dot(hidden, matrix_of(weights, unit)) + offset).astype(BF)
    for pair in range(pairs):
        cols = slice(pair * 128, (pair + 1) * 128)
        q, k, v = qkv_ref[0, :, cols], qkv_ref[1, :, cols], qkv_ref[2, :, cols]
        first = lanes(k.shape) < 64
        mixed = []
        for which in range(2):
            masked = jnp.where(first if which == 0 else ~first, k, jnp.zeros_like(k))
            scores = dot_back(q, masked) * factor
            expo = jnp.exp(scores - jnp.max(scores, axis=-1, keepdims=True))
            probs = expo * (1.0 / jnp.sum(expo, axis=-1, keepdims=True))
            mixed.append(dot(probs.astype(BF), v))
        att_ref[:, cols] = jnp.where(first, mixed[0], mixed[1]).astype(BF)
    branch = dot(att_ref[...], matrix_of(weights, 3)) + proj_off_ref[...]
    branch_ref[...] = branch
    middle_ref[...] = tokens + part(2) * branch


GELU_C = 0.7978845608028654
GELU_A = 0.044715


def mlp_kernel(spec, me_ref, middle_ref, mod_ref, cot_ref, up_off_ref, down_off_ref, *rest):
    width, wide, pieces = spec
    refs, rest = rest[: len(pieces)], rest[len(pieces) :]
    outs, rest = rest[: len(rest) - 14], rest[len(rest) - 14 :]
    (
        result_ref, dbefore_ref, gate_ref, up_bias_ref, down_bias_ref,
        up, down, up_grad, down_grad, active, slope, up_sems, down_sems, out_sems,
    ) = rest
    me = me_ref[0]
    up_copies = loads(pieces, refs, me, by_unit(up), (0, wide), up_sems)
    down_copies = loads(pieces, refs, me, by_block(down), (wide, 2 * wide), down_sems)
    start(up_copies)
    start(down_copies)
    part = lambda i: mod_ref[:, i * width : (i + 1) * width]
    middle = middle_ref[...]
    cot = cot_ref[...].astype(F32)
    normed, _ = normalize(middle)
    hidden = (normed * (1.0 + part(4)) + part(3)).astype(BF)
    gate = part(5)
    dbranch = (gate * cot).astype(BF)
    down_bias_ref[...] = total(dbranch)
    finish(up_copies)
    for unit in range(wide):
        before = dot(hidden, matrix_of(up, unit)) + up_off_ref[:, unit * width : (unit + 1) * width]
        square = before * before
        bent = jnp.tanh(GELU_C * before * (1.0 + GELU_A * square))
        active[unit] = (0.5 * before * (1.0 + bent)).astype(BF)
        slope[unit] = 0.5 * (1.0 + bent) + (0.5 * GELU_C) * before * (1.0 - bent * bent) * (
            1.0 + (3.0 * GELU_A) * square
        )
    finish(down_copies)
    down_rows = down[...].reshape(wide * width, width)
    grads = down_grad.shape
    span = grads[0] // wide if grads[0] > 1 else 0
    branch = down_off_ref[...]
    for unit in range(wide):
        branch = branch + dot(active[unit], down_rows[unit * width : (unit + 1) * width])
        grad = dot_outer(active[unit], dbranch).astype(BF)
        if span:
            down_grad[unit * span : (unit + 1) * span] = grad.reshape((span,) + grads[1:])
        else:
            down_grad[0, unit] = grad
    down_stores = stores(down_grad, outs, me, (wide, 2 * wide), out_sems, 0)
    start(down_stores)
    result_ref[...] = (middle + gate * branch).astype(BF)
    gate_ref[...] = total(cot * branch)
    for unit in range(wide):
        dactive = dot_back(dbranch, down_rows[unit * width : (unit + 1) * width])
        dbefore = (dactive * slope[unit]).astype(BF)
        dbefore_ref[unit] = dbefore
        up_bias_ref[:, unit * width : (unit + 1) * width] = total(dbefore)
        grad = dot_outer(hidden, dbefore).astype(BF)
        up_grad[:, unit] = grad.reshape(up_grad.shape[0], up_grad.shape[2], width)
    up_stores = stores(up_grad, outs, me, (0, wide), out_sems, up_grad.shape[0])
    start(up_stores)
    finish(down_stores)
    finish(up_stores)


def attend_back_kernel(spec, me_ref, middle_ref, mod_ref, cot_ref, dbefore_ref, branch_ref, att_ref,
                       hidden_ref, qkv_ref, *rest):
    width, wide, up_pieces, pieces, factor, pairs = spec
    up_refs, rest = rest[: len(up_pieces)], rest[len(up_pieces) :]
    refs, rest = rest[: len(pieces)], rest[len(pieces) :]
    outs, rest = rest[: len(rest) - 10], rest[len(rest) - 10 :]
    dmiddle_ref, dqkv_ref, sums_ref, bias_ref, up, proj, grads, up_sems, proj_sems, out_sems = rest
    me = me_ref[0]
    up_copies = loads(up_pieces, up_refs, me, by_unit(up), (0, wide), up_sems)
    proj_copies = loads(pieces, refs, me, by_unit(proj), (3, 4), proj_sems)
    start(up_copies)
    start(proj_copies)
    part = lambda i: mod_ref[:, i * width : (i + 1) * width]
    normed, inverse = normalize(middle_ref[...])
    finish(up_copies)
    dhidden = dot_back(dbefore_ref[0], matrix_of(up, 0))
    for unit in range(1, wide):
        dhidden = dhidden + dot_back(dbefore_ref[unit], matrix_of(up, unit))
    dmiddle = cot_ref[...].astype(F32) + norm_back(dhidden * (1.0 + part(4)), normed, inverse)
    dmiddle_ref[...] = dmiddle
    dbranch = (part(2) * dmiddle).astype(BF)
    sums_ref[:, :width] = total(dmiddle * branch_ref[...])
    sums_ref[:, width : 2 * width] = total(dhidden)
    sums_ref[:, 2 * width : 3 * width] = total(dhidden * normed)
    bias_ref[:, 2 * width : 3 * width] = total(dbranch)
    finish(proj_copies)
    datt = dot_back(dbranch, matrix_of(proj, 0)).astype(BF)
    for pair in range(pairs):
        cols = slice(pair * 128, (pair + 1) * 128)
        q, k, v = qkv_ref[0, :, cols], qkv_ref[1, :, cols], qkv_ref[2, :, cols]
        da = datt[:, cols]
        first = lanes(k.shape) < 64
        zero = jnp.zeros_like(k)
        grad_q, grad_k, grad_v = [], [], []
        for which in range(2):
            own = first if which == 0 else ~first
            scores = dot_back(q, jnp.where(own, k, zero)) * factor
            expo = jnp.exp(scores - jnp.max(scores, axis=-1, keepdims=True))
            probs = expo * (1.0 / jnp.sum(expo, axis=-1, keepdims=True))
            dprobs = dot_back(da, jnp.where(own, v, zero))
            rowsum = jnp.sum(dprobs * probs, axis=-1, keepdims=True)
            dscores = (probs * (dprobs - rowsum)).astype(BF)
            grad_q.append(dot(dscores, k))
            grad_k.append(dot_outer(dscores, q))
            grad_v.append(dot_outer(probs.astype(BF), da))
        dqkv_ref[0, :, cols] = (jnp.where(first, grad_q[0], grad_q[1]) * factor).astype(BF)
        dqkv_ref[1, :, cols] = (jnp.where(first, grad_k[0], grad_k[1]) * factor).astype(BF)
        dqkv_ref[2, :, cols] = jnp.where(first, grad_v[0], grad_v[1]).astype(BF)
    bias_ref[:, :width] = total(dqkv_ref[0])
    bias_ref[:, width : 2 * width] = total(dqkv_ref[2])
    shape = (grads.shape[0], grads.shape[2], width)
    for unit in range(3):
        grads[:, unit] = dot_outer(hidden_ref[...], dqkv_ref[unit]).astype(BF).reshape(shape)
    grads[:, 3] = dot_outer(att_ref[...], dbranch).astype(BF).reshape(shape)
    out_copies = stores(grads, outs, me, (0, 4), out_sems, 0)
    start(out_copies)
    finish(out_copies)


def input_back_kernel(spec, me_ref, tokens_ref, mod_ref, dmiddle_ref, dqkv_ref, *rest):
    width, pieces = spec
    refs, rest = rest[: len(pieces)], rest[len(pieces) :]
    dtokens_ref, sums_ref, weights, sems = rest
    copies = loads(pieces, refs, me_ref[0], by_unit(weights), (0, 3), sems)
    start(copies)
    normed, inverse = normalize(tokens_ref[...].astype(F32))
    finish(copies)
    dhidden = dot_back(dqkv_ref[0], matrix_of(weights, 0))
    for unit in range(1, 3):
        dhidden = dhidden + dot_back(dqkv_ref[unit], matrix_of(weights, unit))
    sums_ref[:, :width] = total(dhidden)
    sums_ref[:, width : 2 * width] = total(dhidden * normed)
    scale = 1.0 + mod_ref[:, width : 2 * width]
    dtokens_ref[...] = (dmiddle_ref[...] + norm_back(dhidden * scale, normed, inverse)).astype(BF)


def chunks(width, chunk, wide):
    table = []
    for seq in range(width // chunk):
        entry = []
        for j in range(3):
            index = 3 * seq + j
            per = width // chunk
            entry.append((index // per, index % per * chunk, j * chunk, chunk))
        entry.append((3, seq * chunk, 3 * chunk, chunk))
        table.append(entry)
    return table


def pick(refs, me, seq):
    value = refs[0][...]
    for mask in range(1, len(refs)):
        value = jnp.where((me ^ seq) == mask, refs[mask][...], value)
    return value


def spread1_kernel(spec, me_ref, *refs):
    width, chunk, rows, n_seq = spec
    blocks, (units_ref, qkv_off_ref, proj_off_ref, up_off_ref, down_off_ref) = refs[:n_seq], refs[n_seq:]
    me = me_ref[0]
    qkv_off_ref[...] = jnp.zeros_like(qkv_off_ref)
    for seq, entry in enumerate(chunks(width, chunk, 0)):
        value = pick(blocks, me, seq)
        for unit, there, here, columns in entry:
            units_ref[unit, :, there : there + columns] = value[:rows, here : here + columns]
        tail = value[rows:].astype(F32)
        for index, ref in enumerate((qkv_off_ref, qkv_off_ref, proj_off_ref, down_off_ref)):
            at = seq * chunk + (2 * width if index == 1 else 0)
            ref[:, at : at + chunk] = tail[0:1, index * chunk : (index + 1) * chunk]
        up_off_ref[:, seq * width : (seq + 1) * width] = tail[1:2]


def spread2_kernel(spec, me_ref, *refs):
    width, chunk, wide, n_seq = spec
    blocks, units_ref = refs[:n_seq], refs[n_seq]
    me = me_ref[0]
    for seq in range(n_seq):
        value = pick(blocks, me, seq)
        units_ref[seq] = value[0]
        for unit in range(wide):
            units_ref[wide + unit, :, seq * chunk : (seq + 1) * chunk] = value[
                1, :, unit * chunk : (unit + 1) * chunk
            ]


def summed(refs, unit):
    kept, other, over_x, over_y = refs
    value = kept[0, unit].astype(F32) + other[0, unit].astype(F32)
    return value + (over_x[unit].astype(F32) + over_y[unit].astype(F32))


def send_blocks(scratch, outs, me, sems):
    copies = [
        pltpu.make_async_copy(scratch.at[me ^ mask], out, sems.at[mask]) for mask, out in enumerate(outs)
    ]
    start(copies)
    finish(copies)


def collect1_kernel(spec, me_ref, *refs):
    width, chunk, wide, n_seq = spec
    ins, outs, (scratch, sems) = refs[:4], refs[4 : 4 + n_seq], refs[4 + n_seq :]
    table = chunks(width, chunk, wide)
    for unit in range(4):
        value = summed(ins, unit).astype(BF)
        for seq, entry in enumerate(table):
            for source, there, here, columns in entry:
                if source == unit:
                    scratch[seq, :, here : here + columns] = value[:, there : there + columns]
    send_blocks(scratch, outs, me_ref[0], sems)


def collect2_kernel(spec, me_ref, *refs):
    width, chunk, wide, n_seq = spec
    ins, outs, (scratch, sems) = refs[:4], refs[4 : 4 + n_seq], refs[4 + n_seq :]
    for unit in range(wide):
        scratch[unit, 0] = summed(ins, unit).astype(BF)
        value = summed(ins, wide + unit).astype(BF)
        for seq in range(n_seq):
            scratch[seq, 1, :, unit * chunk : (unit + 1) * chunk] = value[:, seq * chunk : (seq + 1) * chunk]
    send_blocks(scratch, outs, me_ref[0], sems)


def final1_kernel(spec, me_ref, *refs):
    width, chunk, wide, n_seq = spec
    value = refs[0][...].astype(F32)
    for ref in refs[1:n_seq]:
        value = value + ref[...].astype(F32)
    qkv_ref, proj_ref = refs[n_seq:]
    qkv_ref[...] = value[:, : 3 * chunk]
    proj_ref[...] = value[:, 3 * chunk :]


def final2_kernel(spec, me_ref, *refs):
    width, chunk, wide, n_seq = spec
    up_ref, down_ref = refs[n_seq:]
    rows = up_ref.shape[0]
    for index in range(2):
        value = refs[0][index].astype(F32)
        for ref in refs[1:n_seq]:
            value = value + ref[index].astype(F32)
        if index == 0:
            up_ref[...] = value
        else:
            for unit in range(wide):
                down_ref[unit * rows : (unit + 1) * rows] = value[:, unit * chunk : (unit + 1) * chunk]


def call(body, spec, me, inputs, pieces, outs, far_outs, scratch, name):
    vmem = pl.BlockSpec(memory_space=pltpu.VMEM)
    far = pl.BlockSpec(memory_space=pl.ANY)
    return pl.pallas_call(
        functools.partial(body, spec),
        out_shape=far_outs + outs,
        in_specs=[pl.BlockSpec(memory_space=pltpu.SMEM)] + [vmem] * len(inputs) + [far] * len(pieces),
        out_specs=[far] * len(far_outs) + [vmem] * len(outs),
        scratch_shapes=scratch,
        compiler_params=pltpu.CompilerParams(vmem_limit_bytes=52 * 1024 * 1024),
        cost_estimate=pl.CostEstimate(flops=0, bytes_accessed=0, transcendentals=0),
        name=name,
    )(me, *inputs, *pieces)


def local(
    latents,
    conditions,
    modulator,
    modbias,
    qkvweight,
    querybias,
    valuebias,
    projection,
    projbias,
    expand,
    expandbias,
    contract,
    contractbias,
    cotangent,
):
    n_dp, n_seq = lax.axis_size("dp"), lax.axis_size("seq")
    micro, lats, tok, width = latents.shape
    held = micro * lats
    assert held == n_seq
    length = n_seq * tok
    rows = width // n_dp
    chunk = width // n_seq
    wide = contract.shape[0] // rows
    head = width // H
    assert 2 * head == 128
    factor = head ** (-0.5)
    layout = Layout(n_dp, rows, width)

    shaped = jax.ShapeDtypeStruct
    dma = pltpu.SemaphoreType.DMA
    here = lax.axis_index("seq").reshape(1).astype(jnp.int32)
    spec_seq = (width, chunk, wide, n_seq)
    offsets_low = jnp.concatenate([querybias, valuebias, projbias, contractbias, expandbias])
    tail = jnp.pad(offsets_low.reshape(-1, width), ((0, 14), (0, 0)))
    shards1 = jnp.concatenate([jnp.concatenate([qkvweight, projection], axis=1), tail])
    down_shard = contract.reshape(wide, rows, chunk)
    shards2 = jnp.stack([expand, jnp.concatenate([down_shard[i] for i in range(wide)], axis=1)])
    blocks1 = [shards1] + swap_seq(shards1)
    blocks2 = [shards2] + swap_seq(shards2)
    offset_shapes = [shaped((1, n), F32) for n in (3 * width, width, wide * width, width)]
    if layout.direct:
        me = lax.axis_index("dp").reshape(1).astype(jnp.int32)
        u1, offsets, proj_offset, up_offset, down_offset = call(
            spread1_kernel, (width, chunk, rows, n_seq), here, blocks1, [],
            [shaped((4, rows, width), BF)] + offset_shapes, [], [], "spread1",
        )
        (u2,) = call(
            spread2_kernel, spec_seq, here, blocks2, [],
            [shaped((2 * wide, rows, width), BF)], [], [], "spread2",
        )
        w1, w2 = gather_square(u1), gather_square(u2)
    else:
        me = jnp.zeros((1,), jnp.int32)
        order = jnp.arange(n_seq) ^ lax.axis_index("seq")
        b1 = jnp.take(jnp.stack(blocks1), order, axis=0)
        b2 = jnp.take(jnp.stack(blocks2), order, axis=0)
        u_qkv = b1[:, :rows, : 3 * chunk].transpose(1, 0, 2).reshape(rows, 3, width).transpose(1, 0, 2)
        u_proj = b1[:, :rows, 3 * chunk :].transpose(1, 0, 2).reshape(1, rows, width)
        u_up = b2[:, 0].transpose(1, 0, 2).reshape(rows, wide, width).transpose(1, 0, 2)
        u_down = b2[:, 1].reshape(n_seq, rows, wide, chunk).transpose(2, 1, 0, 3).reshape(wide, rows, width)
        natural = lambda v: gather_dp(v).transpose(1, 0, 2, 3).reshape(v.shape[0], width, width)
        w1 = [(natural(jnp.concatenate([u_qkv, u_proj])), 0, 0)]
        w2 = [(natural(u_up), 0, 0), (gather_dp(u_down).reshape(wide, width, width), 0, wide)]
        four = b1[:, rows].reshape(n_seq, 4, chunk).transpose(1, 0, 2).reshape(4, 1, width).astype(F32)
        offsets = jnp.concatenate([four[0], jnp.zeros_like(four[0]), four[1]], axis=1)
        proj_offset, down_offset = four[2], four[3]
        up_offset = b1[:, rows + 1].reshape(1, -1).astype(F32)
    arrays1, spec1 = [w[0] for w in w1], tuple(w[1:] for w in w1)
    arrays2, spec2 = [w[0] for w in w2], tuple(w[1:] for w in w2)

    def to_latents(values):
        values = values.reshape(held, tok, width)
        return lax.all_to_all(values, "seq", 0, 0, tiled=True).reshape(length, width)

    def to_tokens(*values):
        values = jnp.stack([v.reshape(n_seq, tok, width) for v in values], axis=1)
        values = lax.all_to_all(values, "seq", 0, 0, tiled=True)
        return [values[:, i].reshape(micro, lats, tok, width) for i in range(values.shape[1])]

    tokens = to_latents(latents)
    cot = to_latents(cotangent)

    cond_float = conditions.reshape(held, width).astype(F32)
    cond_act = jax.nn.silu(cond_float).astype(BF)
    cond_rows = lax.all_to_all(
        cond_act.reshape(held, n_dp, rows), "dp", 1, 0, tiled=True
    ).reshape(n_dp * held, rows)
    part = jnp.dot(cond_rows, modulator, preferred_element_type=F32)
    part = part + jnp.where(lax.axis_index("dp") == 0, modbias.astype(F32), 0.0)
    part = lax.all_to_all(part, ("dp", "seq"), 0, 0, tiled=True)
    mod = jnp.sum(part.reshape(n_dp, n_seq, -1), axis=0)
    mod = mod.reshape(1, -1)

    pairs = H // 2
    blocks, block_rows = layout.blocks, layout.rows
    places = max(blocks // 2, 1)
    n_far = min(blocks, 2)
    n1, n2 = len(w1), len(w2)
    hidden1, qkv, attended, branch1, middle = call(
        attend_kernel,
        (width, spec1, factor, pairs),
        me,
        [tokens, mod, offsets, proj_offset],
        arrays1,
        [
            shaped((length, width), BF),
            shaped((3, length, width), BF),
            shaped((length, width), BF),
            shaped((length, width), F32),
            shaped((length, width), F32),
        ],
        [],
        [pltpu.VMEM((4, blocks, block_rows, width), BF), dma((n1,))],
        "attention",
    )
    *grads2, result, dbefore, dgate2, up_bias, down_bias = call(
        mlp_kernel,
        (width, wide, spec2),
        me,
        [middle, mod, cot, up_offset, down_offset],
        arrays2,
        [
            shaped((length, width), BF),
            shaped((wide, length, width), BF),
            shaped((1, width), F32),
            shaped((1, wide * width), F32),
            shaped((1, width), F32),
        ],
        [shaped((places, 2 * wide, block_rows, width), BF)] * n_far,
        [
            pltpu.VMEM((wide, blocks, block_rows, width), BF),
            pltpu.VMEM((blocks, wide, block_rows, width), BF),
            pltpu.VMEM((blocks, wide, block_rows, width), BF),
            pltpu.VMEM((blocks, wide, block_rows, width), BF),
            pltpu.VMEM((wide, length, width), BF),
            pltpu.VMEM((wide, length, width), F32),
            dma((n2,)),
            dma((n2,)),
            dma((2 * blocks,)),
        ],
        "mlp",
    )
    *grads1, dmiddle, dqkv, sums1, bias1 = call(
        attend_back_kernel,
        (width, wide, spec2, spec1, factor, pairs),
        me,
        [middle, mod, cot, dbefore, branch1, attended, hidden1, qkv],
        arrays2 + arrays1,
        [
            shaped((length, width), F32),
            shaped((3, length, width), BF),
            shaped((1, 3 * width), F32),
            shaped((1, 3 * width), F32),
        ],
        [shaped((places, 4, block_rows, width), BF)] * n_far,
        [
            pltpu.VMEM((wide, blocks, block_rows, width), BF),
            pltpu.VMEM((1, blocks, block_rows, width), BF),
            pltpu.VMEM((blocks, 4, block_rows, width), BF),
            dma((n2,)),
            dma((n1,)),
            dma((blocks,)),
        ],
        "attention_back",
    )
    dtokens, sums0 = call(
        input_back_kernel,
        (width, spec1),
        me,
        [tokens, mod, dmiddle, dqkv],
        arrays1,
        [shaped((length, width), BF), shaped((1, 2 * width), F32)],
        [],
        [pltpu.VMEM((3, blocks, block_rows, width), BF), dma((n1,))],
        "input_back",
    )
    result, token_grad = to_tokens(result, dtokens)

    dmod = jnp.concatenate([sums0, sums1, dgate2], axis=1)
    offset_grads = (
        bias1[:, :width], bias1[:, width : 2 * width], bias1[:, 2 * width :], up_bias, down_bias
    )
    offset_grads = jnp.concatenate([g.reshape(n_seq, -1) for g in offset_grads], axis=1)
    small = jnp.concatenate([dmod.reshape(n_seq, -1), offset_grads], axis=1).astype(BF)
    small = jnp.broadcast_to(small[None], (n_dp,) + small.shape).reshape(n_dp * n_seq, -1)
    small = lax.all_to_all(small, ("dp", "seq"), 0, 0, tiled=True)
    cols = modulator.shape[1]
    dmod_all = small[:, :cols]
    offset_sums = jnp.sum(small[:, cols:].astype(F32), axis=0)
    grad_mod = jnp.einsum("ld,ln->dn", cond_rows, dmod_all, preferred_element_type=F32)
    grad_mod_offset = jnp.sum(dmod_all.astype(F32), axis=0)
    dcond_rows = jnp.einsum("ln,dn->ld", dmod_all, modulator, preferred_element_type=F32)
    dcond = jnp.broadcast_to(
        dcond_rows.reshape(n_dp, 1, held, rows), (n_dp, n_seq, held, rows)
    ).reshape(n_dp * n_seq, held, rows)
    dcond = lax.all_to_all(dcond, ("dp", "seq"), 0, 0, tiled=True)
    dcond = jnp.sum(dcond.reshape(n_dp, n_seq, held, rows), axis=1)
    dcond = dcond.transpose(1, 0, 2).reshape(held, width)
    dconds = jax.vjp(jax.nn.silu, cond_float)[1](dcond)[0].reshape(micro, lats, width)

    if layout.direct:
        blocks2 = call(
            collect2_kernel, spec_seq, here, list(scatter_square(*grads2)), [], [],
            [shaped((2, rows, width), BF)] * n_seq,
            [pltpu.VMEM((n_seq, 2, rows, width), BF), dma((n_seq,))], "collect2",
        )
        blocks1 = call(
            collect1_kernel, spec_seq, here, list(scatter_square(*grads1)), [], [],
            [shaped((rows, width), BF)] * n_seq,
            [pltpu.VMEM((n_seq, rows, width), BF), dma((n_seq,))], "collect1",
        )
        up_out, down_out = call(
            final2_kernel, spec_seq, here, [blocks2[0]] + swap_seq(list(blocks2[1:])), [],
            [shaped((rows, width), F32), shaped((wide * rows, chunk), F32)], [], [], "final2",
        )
        qkv_out, proj_out = call(
            final1_kernel, spec_seq, here, [blocks1[0]] + swap_seq(list(blocks1[1:])), [],
            [shaped((rows, 3 * chunk), F32), shaped((rows, chunk), F32)], [], [], "final1",
        )
    else:
        unit_rows = lambda v: v.reshape(-1, n_dp, rows, width).transpose(1, 0, 2, 3)
        s1 = scatter_dp(unit_rows(grads1[0][0]))
        s_up = scatter_dp(unit_rows(grads2[0][0, :wide]))
        s_down = scatter_dp(grads2[0][0, wide:].reshape(n_dp, wide, rows, width))
        t1 = s1[:3].transpose(1, 0, 2).reshape(rows, n_seq, 3 * chunk)
        t1 = jnp.concatenate([t1, s1[3].reshape(rows, n_seq, chunk)], axis=2).transpose(1, 0, 2)
        t2 = s_up.transpose(1, 0, 2).reshape(rows, n_seq, -1).transpose(1, 0, 2)
        t3 = s_down.reshape(wide * rows, n_seq, chunk).transpose(1, 0, 2)
        r1, up_out, down_out = scatter_seq(t1), scatter_seq(t2), scatter_seq(t3)
        qkv_out, proj_out = r1[:, : 3 * chunk], r1[:, 3 * chunk :]
    sizes = [b.shape[0] for b in (querybias, valuebias, projbias, expandbias, contractbias)]
    starts = [sum(sizes[:i]) for i in range(len(sizes))]
    sums = [offset_sums[a : a + n] for a, n in zip(starts, sizes)]
    return (
        result,
        token_grad,
        dconds,
        grad_mod,
        grad_mod_offset,
        qkv_out,
        sums[0],
        sums[1],
        proj_out,
        sums[2],
        up_out,
        sums[3],
        down_out,
        sums[4],
    )


def solution(mesh):
    placed = (
        P(None, "dp", "seq", None),
        P(None, "dp", None),
        P("dp", "seq"),
        P("seq"),
        P("dp", "seq"),
        P("seq"),
        P("seq"),
        P("dp", "seq"),
        P("seq"),
        P("dp", "seq"),
        P("seq"),
        P("dp", "seq"),
        P("seq"),
        P(None, "dp", "seq", None),
    )
    return jax.shard_map(
        local,
        mesh=mesh,
        in_specs=placed,
        out_specs=(
            P(None, "dp", "seq", None),
            P(None, "dp", "seq", None),
            P(None, "dp", None),
            P("dp", "seq"),
            P("seq"),
            P("dp", "seq"),
            P("seq"),
            P("seq"),
            P("dp", "seq"),
            P("seq"),
            P("dp", "seq"),
            P("seq"),
            P("dp", "seq"),
            P("seq"),
        ),
        check_vma=False,
    )
```

```python
import functools

import jax
import jax.numpy as jnp
from jax import lax
from jax.experimental import pallas as pl
from jax.experimental.pallas import tpu as pltpu
from jax.sharding import PartitionSpec as P

H = 12
EPSILON = 1e-06
BF = jnp.bfloat16
F32 = jnp.float32


def bits_of(count):
    bits = count.bit_length() - 1
    assert 1 << bits == count
    return bits


def swap(values, axis, bit):
    count = lax.axis_size(axis)
    return lax.ppermute(values, axis, [(i, i ^ (1 << bit)) for i in range(count)])


def own_bit(axis, bit):
    return (lax.axis_index(axis) >> bit) & 1


def after(values, first):
    far = pl.BlockSpec(memory_space=pl.ANY)
    return pl.pallas_call(
        lambda *refs: None,
        out_shape=[jax.ShapeDtypeStruct(v.shape, v.dtype) for v in values],
        in_specs=[far] * (len(values) + len(first)),
        out_specs=[far] * len(values),
        input_output_aliases={i: i for i in range(len(values))},
        cost_estimate=pl.CostEstimate(flops=0, bytes_accessed=0, transcendentals=0),
        name="after",
    )(*values, *first)


def halve(values, axis, bit):
    index = own_bit(axis, bit)
    sent = lax.dynamic_index_in_dim(values, 1 - index, 0, keepdims=False)
    kept = lax.dynamic_index_in_dim(values, index, 0, keepdims=False)
    other = swap(sent.astype(BF), axis, bit)
    return kept.astype(F32) + other.astype(F32)


def scatter_seq(values):
    count = bits_of(lax.axis_size("seq"))
    shape = values.shape[1:]
    values = values.reshape((2,) * count + shape)
    values = values.transpose(list(range(count - 1, -1, -1)) + list(range(count, count + len(shape))))
    for bit in range(count):
        values = halve(values, "seq", bit)
    return values


class Layout:
    def __init__(self, n_dp, n_seq, rows, width):
        self.direct = rows % 16 == 0 and n_dp == 8 and n_seq == 4
        self.blocks = n_dp if self.direct else 1
        self.rows = rows if self.direct else width


def mask_of(place, order):
    return sum(((place >> j) & 1) << bit for j, bit in enumerate(order))


def gather_dp(units):
    part = units[None]
    order = list(range(bits_of(lax.axis_size("dp"))))[::-1]
    for bit in order:
        part = jnp.concatenate([part, swap(part, "dp", bit)], axis=0)
    count = part.shape[0]
    place = [0] * count
    for index in range(count):
        place[mask_of(index, order)] = index
    wanted = jnp.asarray(place)[jnp.arange(count) ^ lax.axis_index("dp")]
    return jnp.take(part, wanted, axis=0)


def scatter_dp(values):
    count = bits_of(values.shape[0])
    values = jnp.take(values, jnp.arange(1 << count) ^ lax.axis_index("dp"), axis=0)
    values = values.reshape((2,) * count + values.shape[1:]).astype(F32)
    for bit in range(count - 1, -1, -1):
        values = values[0] + swap(values[1].astype(BF), "dp", bit).astype(F32)
    return values


def gather_square(units, first=()):
    middle = units.shape[0] // 2
    over_x, over_y = swap(units, "dp", 1), swap(units, "dp", 2)
    low, high = cut(over_x, over_y, first)
    low, high = swap(low, "dp", 2), swap(high, "dp", 1)
    near = [(units, 0, 0), (over_x, 2, 0), (over_y, 4, 0), (low, 6, 0), (high, 6, middle)]
    far = [(swap(part, "dp", 0), mask | 1, first) for part, mask, first in near]
    return [entry for pair in zip(near, far) for entry in pair]


def scatter_first(kept, others, first=()):
    _, units, rows, columns = kept.shape
    middle = units // 2
    half = jax.ShapeDtypeStruct((middle, rows, columns), BF)
    part = lambda place, high: (kept, (place, high), (1, middle))
    low_in, high_in, over_x, over_y = others[3], others[4], others[1], others[2]
    return call(
        add_kernel, 2, jnp.zeros((1,), jnp.int32),
        [part(3, 0), low_in, part(3, 1), high_in]
        + [part(1, 1), (over_x, (1,), (middle,)), part(2, 0), (over_y, (0,), (middle,))],
        [], [half] * 4, [], [], "first_sums", first,
    )


def scatter_last(kept, others, low_in, high_in, first=()):
    _, units, rows, columns = kept.shape
    middle = units // 2
    half = jax.ShapeDtypeStruct((middle, rows, columns), BF)
    part = lambda place, high: (kept, (place, high), (1, middle))
    return call(
        add_kernel, 3, jnp.zeros((1,), jnp.int32),
        [part(1, 0), (others[1], (0,), (middle,)), low_in]
        + [part(2, 1), (others[2], (1,), (middle,)), high_in],
        [], [half] * 2, [], [], "last_sums", first,
    )


def cut(over_x, over_y, first=()):
    half = jax.ShapeDtypeStruct((over_x.shape[0] // 2,) + over_x.shape[1:], BF)
    return call(
        cut_kernel, None, jnp.zeros((1,), jnp.int32),
        [(over_x, (0,), half.shape[:1]), (over_y, (1,), half.shape[:1])], [],
        [half, half], [], [], "cut", first,
    )


def gather_seq(values):
    found = {0: values}
    for bit in range(bits_of(lax.axis_size("seq")) - 1, -1, -1):
        found.update({mask | 1 << bit: swap(v, "seq", bit) for mask, v in list(found.items())})
    return [found[mask] for mask in range(len(found))]


def swap_seq(values):
    count = lax.axis_size("seq")
    return [
        lax.ppermute(value, "seq", [(i, i ^ (mask + 1)) for i in range(count)])
        for mask, value in enumerate(values)
    ]


def dot(a, b):
    return jnp.dot(a, b, preferred_element_type=F32)


def dot_back(a, b):
    return lax.dot_general(a, b, (((1,), (1,)), ((), ())), preferred_element_type=F32)


def dot_outer(a, b):
    return lax.dot_general(a, b, (((0,), (0,)), ((), ())), preferred_element_type=F32)


def normalize(values):
    center = values - jnp.mean(values, axis=-1, keepdims=True)
    inverse = lax.rsqrt(jnp.mean(center * center, axis=-1, keepdims=True) + EPSILON)
    return (center * inverse, inverse)


def norm_back(grad_normed, normed, inverse):
    first = jnp.mean(grad_normed, axis=-1, keepdims=True)
    second = jnp.mean(grad_normed * normed, axis=-1, keepdims=True)
    return inverse * (grad_normed - first - normed * second)


def total(values):
    return jnp.sum(values.astype(F32), axis=0, keepdims=True)


def loads(pieces, refs, me, target, span, sems):
    copies = []
    for ref, (mask, first) in zip(refs, pieces):
        low, high = max(span[0], first), min(span[1], first + ref.shape[0])
        if low < high:
            view = target(me ^ mask, low - span[0], high - span[0])
            copies.append(
                pltpu.make_async_copy(ref.at[low - first : high - first], view, sems.at[len(copies)])
            )
    return copies


def start(copies):
    for copy in copies:
        copy.start()


def finish(copies):
    for copy in copies:
        copy.wait()


def by_unit(scratch):
    return lambda block, low, high: scratch.at[low:high, block]


def by_block(scratch):
    return lambda block, low, high: scratch.at[block, low:high]


def matrix_of(scratch, unit):
    block = scratch[unit]
    return block.reshape(block.shape[0] * block.shape[1], block.shape[2])


def stores(scratch, outs, me, units, sems, base):
    copies = []
    blocks = scratch.shape[0]
    for mask in range(blocks):
        place = mask >> 1
        out = outs[0].at[place]
        if mask & 1:
            out = outs[1 + place] if place < 3 else None
        count = units[1] - units[0]
        spans = [(out, 0, units[0], count)]
        if out is None:
            middle = outs[4].shape[0]
            spans = [
                (outs[4 + half], max(half * middle - units[0], 0), max(units[0] - half * middle, 0),
                 min(units[1], (half + 1) * middle) - max(units[0], half * middle))
                for half in range(2)
            ]
        for target, source, first, number in spans:
            if number > 0:
                copies.append(
                    pltpu.make_async_copy(
                        scratch.at[me ^ mask, source : source + number],
                        target.at[first : first + number],
                        sems.at[base + len(copies)],
                    )
                )
    return copies


def lanes(shape):
    return lax.broadcasted_iota(jnp.int32, shape, 1)


def copy_kernel(spec, me_ref, source, target):
    target[...] = source[...]


def pack_kernel(spec, me_ref, tokens_ref, part_ref, out_ref, rows):
    held, tok, width = tokens_ref.shape
    half = width // 2
    mod = part_ref[0]
    for index in range(1, part_ref.shape[0]):
        mod = mod + part_ref[index]
    high = mod.astype(BF).astype(F32)
    low = mod - high
    rows[...] = jnp.zeros_like(rows)
    for index in range(held):
        out_ref[index, :tok] = tokens_ref[index]
        own = slice(index, index + 1)
        rows[0:1] = high[own, :width]
        rows[1:2] = low[own, :width]
        rows[2:3, :half] = high[own, width:]
        rows[2:3, half:] = low[own, width:]
        out_ref[index, tok:] = rows[...].astype(BF)


def attend_kernel(spec, me_ref, packed_ref, qkv_off_ref, proj_off_ref, *rest):
    width, pieces, factor, pairs = spec
    refs, rest = rest[: len(pieces)], rest[len(pieces) :]
    hidden_ref, qkv_ref, att_ref, branch_ref, middle_ref, mod_ref, tokens_ref, weights, sems = rest
    me = me_ref[0]
    count, tok = packed_ref.shape[0], packed_ref.shape[1] - 16
    half = width // 2
    for seq in range(count):
        tokens_ref[seq * tok : (seq + 1) * tok] = packed_ref[seq, :tok]
        row = packed_ref[seq, tok:].astype(F32)
        at = seq * (width + half)
        mod_ref[:, at : at + width] = row[0:1] + row[1:2]
        mod_ref[:, at + width : at + width + half] = row[2:3, :half] + row[2:3, half:]
    copies = loads(pieces, refs, me, by_unit(weights), (0, 4), sems)
    start(copies)
    tokens = tokens_ref[...].astype(F32)
    part = lambda i: mod_ref[:, i * width : (i + 1) * width]
    normed, _ = normalize(tokens)
    hidden = (normed * (1.0 + part(1)) + part(0)).astype(BF)
    hidden_ref[...] = hidden
    finish(copies)
    for unit in range(3):
        offset = qkv_off_ref[:, unit * width : (unit + 1) * width]
        qkv_ref[unit] = (dot(hidden, matrix_of(weights, unit)) + offset).astype(BF)
    for pair in range(pairs):
        cols = slice(pair * 128, (pair + 1) * 128)
        q, k, v = qkv_ref[0, :, cols], qkv_ref[1, :, cols], qkv_ref[2, :, cols]
        first = lanes(k.shape) < 64
        mixed = []
        for which in range(2):
            masked = jnp.where(first if which == 0 else ~first, k, jnp.zeros_like(k))
            scores = dot_back(q, masked) * factor
            expo = jnp.exp(scores - jnp.max(scores, axis=-1, keepdims=True))
            probs = expo * (1.0 / jnp.sum(expo, axis=-1, keepdims=True))
            mixed.append(dot(probs.astype(BF), v))
        att_ref[:, cols] = jnp.where(first, mixed[0], mixed[1]).astype(BF)
    branch = dot(att_ref[...], matrix_of(weights, 3)) + proj_off_ref[...]
    branch_ref[...] = branch
    middle_ref[...] = tokens + part(2) * branch


GELU_C = 0.7978845608028654
GELU_A = 0.044715


def mlp_kernel(spec, me_ref, middle_ref, mod_ref, cot_ref, up_off_ref, down_off_ref, *rest):
    width, wide, pieces = spec
    refs, rest = rest[: len(pieces)], rest[len(pieces) :]
    outs, rest = rest[: len(rest) - 14], rest[len(rest) - 14 :]
    (
        result_ref, dbefore_ref, gate_ref, up_bias_ref, down_bias_ref,
        up, down, up_grad, down_grad, active, slope, up_sems, down_sems, out_sems,
    ) = rest
    me = me_ref[0]
    up_copies = loads(pieces, refs, me, by_unit(up), (0, wide), up_sems)
    down_copies = loads(pieces, refs, me, by_block(down), (wide, 2 * wide), down_sems)
    start(up_copies)
    start(down_copies)
    part = lambda i: mod_ref[:, i * width : (i + 1) * width]
    middle = middle_ref[...]
    cot = cot_ref[...].astype(F32)
    normed, _ = normalize(middle)
    hidden = (normed * (1.0 + part(4)) + part(3)).astype(BF)
    gate = part(5)
    dbranch = (gate * cot).astype(BF)
    down_bias_ref[...] = total(dbranch)
    finish(up_copies)
    for unit in range(wide):
        before = dot(hidden, matrix_of(up, unit)) + up_off_ref[:, unit * width : (unit + 1) * width]
        square = before * before
        bent = jnp.tanh(GELU_C * before * (1.0 + GELU_A * square))
        active[unit] = (0.5 * before * (1.0 + bent)).astype(BF)
        slope[unit] = 0.5 * (1.0 + bent) + (0.5 * GELU_C) * before * (1.0 - bent * bent) * (
            1.0 + (3.0 * GELU_A) * square
        )
    finish(down_copies)
    down_rows = down[...].reshape(wide * width, width)
    grads = down_grad.shape
    span = grads[0] // wide if grads[0] > 1 else 0
    branch = down_off_ref[...]
    for unit in range(wide):
        branch = branch + dot(active[unit], down_rows[unit * width : (unit + 1) * width])
        grad = dot_outer(active[unit], dbranch).astype(BF)
        if span:
            down_grad[unit * span : (unit + 1) * span] = grad.reshape((span,) + grads[1:])
        else:
            down_grad[0, unit] = grad
    down_stores = stores(down_grad, outs, me, (wide, 2 * wide), out_sems, 0)
    start(down_stores)
    result_ref[...] = (middle + gate * branch).astype(BF)
    gate_ref[...] = total(cot * branch)
    for unit in range(wide):
        dactive = dot_back(dbranch, down_rows[unit * width : (unit + 1) * width])
        dbefore = (dactive * slope[unit]).astype(BF)
        dbefore_ref[unit] = dbefore
        up_bias_ref[:, unit * width : (unit + 1) * width] = total(dbefore)
        grad = dot_outer(hidden, dbefore).astype(BF)
        up_grad[:, unit] = grad.reshape(up_grad.shape[0], up_grad.shape[2], width)
    up_stores = stores(up_grad, outs, me, (0, wide), out_sems, len(down_stores))
    start(up_stores)
    finish(down_stores)
    finish(up_stores)


def middle_back_kernel(spec, me_ref, middle_ref, mod_ref, cot_ref, dbefore_ref, branch_ref, *rest):
    width, wide, up_pieces, pieces = spec
    up_refs, rest = rest[: len(up_pieces)], rest[len(up_pieces) :]
    refs, rest = rest[: len(pieces)], rest[len(pieces) :]
    dmiddle_ref, dbranch_ref, datt_ref, sums_ref, bias_ref, up, proj, up_sems, proj_sems = rest
    me = me_ref[0]
    up_copies = loads(up_pieces, up_refs, me, by_unit(up), (0, wide), up_sems)
    proj_copies = loads(pieces, refs, me, by_unit(proj), (3, 4), proj_sems)
    start(up_copies)
    start(proj_copies)
    part = lambda i: mod_ref[:, i * width : (i + 1) * width]
    normed, inverse = normalize(middle_ref[...])
    finish(up_copies)
    dhidden = dot_back(dbefore_ref[0], matrix_of(up, 0))
    for unit in range(1, wide):
        dhidden = dhidden + dot_back(dbefore_ref[unit], matrix_of(up, unit))
    dmiddle = cot_ref[...].astype(F32) + norm_back(dhidden * (1.0 + part(4)), normed, inverse)
    dmiddle_ref[...] = dmiddle
    dbranch = (part(2) * dmiddle).astype(BF)
    dbranch_ref[...] = dbranch
    sums_ref[:, :width] = total(dmiddle * branch_ref[...])
    sums_ref[:, width : 2 * width] = total(dhidden)
    sums_ref[:, 2 * width : 3 * width] = total(dhidden * normed)
    bias_ref[...] = total(dbranch)
    finish(proj_copies)
    datt_ref[...] = dot_back(dbranch, matrix_of(proj, 0)).astype(BF)


def attend_back_kernel(spec, me_ref, dbranch_ref, datt_ref, att_ref, hidden_ref, qkv_ref, *rest):
    width, factor, pairs = spec
    outs, rest = rest[: len(rest) - 4], rest[len(rest) - 4 :]
    dqkv_ref, bias_ref, grads, out_sems = rest
    me = me_ref[0]
    for pair in range(pairs):
        cols = slice(pair * 128, (pair + 1) * 128)
        q, k, v = qkv_ref[0, :, cols], qkv_ref[1, :, cols], qkv_ref[2, :, cols]
        da = datt_ref[:, cols]
        first = lanes(k.shape) < 64
        zero = jnp.zeros_like(k)
        grad_q, grad_k, grad_v = [], [], []
        for which in range(2):
            own = first if which == 0 else ~first
            scores = dot_back(q, jnp.where(own, k, zero)) * factor
            expo = jnp.exp(scores - jnp.max(scores, axis=-1, keepdims=True))
            probs = expo * (1.0 / jnp.sum(expo, axis=-1, keepdims=True))
            dprobs = dot_back(da, jnp.where(own, v, zero))
            rowsum = jnp.sum(dprobs * probs, axis=-1, keepdims=True)
            dscores = (probs * (dprobs - rowsum)).astype(BF)
            grad_q.append(dot(dscores, k))
            grad_k.append(dot_outer(dscores, q))
            grad_v.append(dot_outer(probs.astype(BF), da))
        dqkv_ref[0, :, cols] = (jnp.where(first, grad_q[0], grad_q[1]) * factor).astype(BF)
        dqkv_ref[1, :, cols] = (jnp.where(first, grad_k[0], grad_k[1]) * factor).astype(BF)
        dqkv_ref[2, :, cols] = jnp.where(first, grad_v[0], grad_v[1]).astype(BF)
    bias_ref[:, :width] = total(dqkv_ref[0])
    bias_ref[:, width : 2 * width] = total(dqkv_ref[2])
    shape = (grads.shape[0], grads.shape[2], width)
    for unit in range(3):
        grads[:, unit] = dot_outer(hidden_ref[...], dqkv_ref[unit]).astype(BF).reshape(shape)
    grads[:, 3] = dot_outer(att_ref[...], dbranch_ref[...]).astype(BF).reshape(shape)
    out_copies = stores(grads, outs, me, (0, 4), out_sems, 0)
    start(out_copies)
    finish(out_copies)


def input_back_kernel(spec, me_ref, tokens_ref, mod_ref, dmiddle_ref, dqkv_ref, sums_ref, gate_ref,
                      qv_ref, proj_off_ref, up_off_ref, down_off_ref, *rest):
    width, tok, chunk, pieces = spec
    refs, rest = rest[: len(pieces)], rest[len(pieces) :]
    packed_ref, weights, dmod, rows, sems = rest
    copies = loads(pieces, refs, me_ref[0], by_unit(weights), (0, 3), sems)
    start(copies)
    normed, inverse = normalize(tokens_ref[...].astype(F32))
    finish(copies)
    dhidden = dot_back(dqkv_ref[0], matrix_of(weights, 0))
    for unit in range(1, 3):
        dhidden = dhidden + dot_back(dqkv_ref[unit], matrix_of(weights, unit))
    dmod[:, :width] = total(dhidden)
    dmod[:, width : 2 * width] = total(dhidden * normed)
    dmod[:, 2 * width : 5 * width] = sums_ref[...]
    dmod[:, 5 * width :] = gate_ref[...]
    scale = 1.0 + mod_ref[:, width : 2 * width]
    dtokens = (dmiddle_ref[...] + norm_back(dhidden * scale, normed, inverse)).astype(BF)
    rows[...] = jnp.zeros_like(rows)
    half = width // 2
    for seq in range(packed_ref.shape[0]):
        packed_ref[seq, :tok] = dtokens[seq * tok : (seq + 1) * tok]
        at, own = seq * (width + half), slice(seq * chunk, (seq + 1) * chunk)
        rows[0:1, :] = dmod[:, at : at + width]
        rows[1:2, :half] = dmod[:, at + width : at + width + half]
        rows[1:2, half : half + chunk] = qv_ref[:, own]
        rows[1:2, half + chunk :] = qv_ref[:, width + seq * chunk : width + (seq + 1) * chunk]
        rows[2:3, :] = up_off_ref[:, seq * width : (seq + 1) * width]
        rows[3:4, :chunk] = proj_off_ref[:, own]
        rows[3:4, chunk : 2 * chunk] = down_off_ref[:, own]
        packed_ref[seq, tok:] = rows[...].astype(BF)


def mod_grad_kernel(spec, me_ref, small_ref, cond_ref, matrix_ref, grad_ref, sums_ref, dcond_ref):
    n_seq = spec
    columns = matrix_ref.shape[1]
    dmod = small_ref[:, :columns]
    grad_ref[...] = dot_outer(cond_ref[...], dmod)
    sums_ref[...] = total(small_ref[...])
    dcond = dot_back(dmod, matrix_ref[...])
    held = dcond_ref.shape[1]
    for index in range(dcond_ref.shape[0]):
        first = index // n_seq * held
        dcond_ref[index] = dcond[first : first + held]


def chunks(width, chunk):
    table = []
    for seq in range(width // chunk):
        entry = []
        for j in range(3):
            index = 3 * seq + j
            per = width // chunk
            entry.append((index // per, index % per * chunk, j * chunk, chunk))
        entry.append((3, seq * chunk, 3 * chunk, chunk))
        table.append(entry)
    return table


def pick(values, me, seq):
    value = values[0]
    for mask in range(1, len(values)):
        value = jnp.where((me ^ seq) == mask, values[mask], value)
    return value


def spread1_kernel(spec, me_ref, *refs):
    width, chunk, rows, n_seq = spec
    blocks, (units_ref, qkv_off_ref, proj_off_ref, up_off_ref, down_off_ref) = refs[:n_seq], refs[n_seq:]
    me = me_ref[0]
    qkv_off_ref[...] = jnp.zeros_like(qkv_off_ref)
    for seq, entry in enumerate(chunks(width, chunk)):
        value = pick([ref[...] for ref in blocks], me, seq)
        for unit, there, here, columns in entry:
            units_ref[unit, :, there : there + columns] = value[:rows, here : here + columns]
        tail = value[rows:].astype(F32)
        for index, ref in enumerate((qkv_off_ref, qkv_off_ref, proj_off_ref, down_off_ref)):
            at = seq * chunk + (2 * width if index == 1 else 0)
            ref[:, at : at + chunk] = tail[0:1, index * chunk : (index + 1) * chunk]
        up_off_ref[:, seq * width : (seq + 1) * width] = tail[1:2]


def spread2_kernel(spec, me_ref, own_ref, far_ref, near_ref, units_ref):
    width, chunk, wide, n_seq = spec
    me = me_ref[0]
    for seq in range(n_seq):
        value = pick([own_ref[...], near_ref[0], far_ref[...], near_ref[1]], me, seq)
        units_ref[seq] = value[0]
        for unit in range(wide):
            units_ref[wide + unit, :, seq * chunk : (seq + 1) * chunk] = value[
                1, :, unit * chunk : (unit + 1) * chunk
            ]


def add_kernel(spec, me_ref, *refs):
    outs = refs[len(refs) * spec // (spec + 1) :]
    for index, out in enumerate(outs):
        terms = refs[index * spec : (index + 1) * spec]
        for unit in range(out.shape[0]):
            value = terms[0][0, unit].astype(F32)
            for term in terms[1:]:
                value = value + term[unit].astype(F32)
            out[unit] = value.astype(BF)


def cut_kernel(spec, me_ref, over_x, over_y, low, high):
    low[...] = over_x[...]
    high[...] = over_y[...]


def summed(refs, unit):
    kept, other, x_low, x_high, y_low, y_high = refs
    middle = x_low.shape[0]
    over_x, over_y = (x_low, y_low) if unit < middle else (x_high, y_high)
    value = kept[0, unit].astype(F32) + other[unit].astype(F32)
    return value + (over_x[unit % middle].astype(F32) + over_y[unit % middle].astype(F32))


def send_blocks(scratch, outs, me, sems):
    copies = [
        pltpu.make_async_copy(scratch.at[me ^ mask], out, sems.at[mask]) for mask, out in enumerate(outs)
    ]
    start(copies)
    finish(copies)


def collect1_kernel(spec, me_ref, *refs):
    width, chunk, wide, n_seq = spec
    ins, outs, (scratch, sems) = refs[:6], refs[6 : 6 + n_seq], refs[6 + n_seq :]
    table = chunks(width, chunk)
    for unit in range(4):
        value = summed(ins, unit).astype(BF)
        for seq, entry in enumerate(table):
            for source, there, here, columns in entry:
                if source == unit:
                    scratch[seq, :, here : here + columns] = value[:, there : there + columns]
    send_blocks(scratch, outs, me_ref[0], sems)


def collect2_kernel(spec, me_ref, *refs):
    width, chunk, wide, n_seq = spec
    ins, outs, (scratch, sems) = refs[:6], refs[6 : 6 + n_seq], refs[6 + n_seq :]
    for unit in range(wide):
        scratch[unit, 0] = summed(ins, unit).astype(BF)
        value = summed(ins, wide + unit).astype(BF)
        for seq in range(n_seq):
            scratch[seq, 1, :, unit * chunk : (unit + 1) * chunk] = value[:, seq * chunk : (seq + 1) * chunk]
    send_blocks(scratch, outs, me_ref[0], sems)


def final1_kernel(spec, me_ref, *refs):
    width, chunk, wide, n_seq = spec
    value = refs[0][...].astype(F32)
    for ref in refs[1:n_seq]:
        value = value + ref[...].astype(F32)
    qkv_ref, proj_ref = refs[n_seq:]
    qkv_ref[...] = value[:, : 3 * chunk]
    proj_ref[...] = value[:, 3 * chunk :]


def final2_kernel(spec, me_ref, *refs):
    width, chunk, wide, n_seq = spec
    up_ref, down_ref = refs[n_seq:]
    rows = up_ref.shape[0]
    for index in range(2):
        value = refs[0][index].astype(F32)
        for ref in refs[1:n_seq]:
            value = value + ref[index].astype(F32)
        if index == 0:
            up_ref[...] = value
        else:
            for unit in range(wide):
                down_ref[unit * rows : (unit + 1) * rows] = value[:, unit * chunk : (unit + 1) * chunk]


def call(body, spec, me, inputs, pieces, outs, far_outs, scratch, name, first=(), flops=0):
    vmem = pl.BlockSpec(memory_space=pltpu.VMEM)
    far = pl.BlockSpec(memory_space=pl.ANY)
    specs, arrays = [], []
    for value in inputs:
        if isinstance(value, tuple):
            value, index, shape = value
            index = index + (0,) * (value.ndim - len(index))
            shape = shape + value.shape[len(shape) :]
            specs.append(pl.BlockSpec(shape, lambda step, index=index: index))
        else:
            specs.append(vmem)
        arrays.append(value)
    used = 1 + len(inputs) + len(pieces)

    def run(*refs):
        body(spec, *refs[:used], *refs[used + len(first) :])

    return pl.pallas_call(
        run,
        grid=(1,),
        out_shape=far_outs + outs,
        in_specs=[pl.BlockSpec(memory_space=pltpu.SMEM)]
        + specs
        + [far] * (len(pieces) + len(first)),
        out_specs=[far] * len(far_outs) + [vmem] * len(outs),
        scratch_shapes=scratch,
        compiler_params=pltpu.CompilerParams(vmem_limit_bytes=52 * 1024 * 1024),
        cost_estimate=pl.CostEstimate(flops=flops, bytes_accessed=0, transcendentals=0),
        name=name,
    )(me, *arrays, *pieces, *first)


def local(
    latents,
    conditions,
    modulator,
    modbias,
    qkvweight,
    querybias,
    valuebias,
    projection,
    projbias,
    expand,
    expandbias,
    contract,
    contractbias,
    cotangent,
):
    n_dp, n_seq = lax.axis_size("dp"), lax.axis_size("seq")
    micro, lats, tok, width = latents.shape
    held = micro * lats
    assert held == n_seq
    length = n_seq * tok
    rows = width // n_dp
    chunk = width // n_seq
    wide = contract.shape[0] // rows
    head = width // H
    assert 2 * head == 128
    factor = head ** (-0.5)
    layout = Layout(n_dp, n_seq, rows, width)

    def to_latents(values):
        return lax.all_to_all(values, "seq", 0, 0, tiled=True)

    def to_tokens(values):
        values = values.reshape(n_seq, tok, width)
        values = lax.all_to_all(values, "seq", 0, 0, tiled=True)
        return values.reshape(micro, lats, tok, width)

    shaped = jax.ShapeDtypeStruct
    dma = pltpu.SemaphoreType.DMA
    here = lax.axis_index("seq").reshape(1).astype(jnp.int32)
    spec_seq = (width, chunk, wide, n_seq)
    offsets_low = jnp.concatenate([querybias, valuebias, projbias, contractbias, expandbias])
    tail = jnp.pad(offsets_low.reshape(-1, width), ((0, 14), (0, 0)))
    down_shard = contract.reshape(wide, rows, chunk)
    shards1 = jnp.concatenate([jnp.concatenate([qkvweight, projection], axis=1), tail])
    shards2 = jnp.stack([expand, jnp.concatenate([down_shard[i] for i in range(wide)], axis=1)])
    if layout.direct:
        blocks1 = [shards1] + swap_seq([shards1] * (n_seq - 1))
    else:
        blocks1, blocks2 = gather_seq(shards1), gather_seq(shards2)

    cond_float = conditions.reshape(held, width).astype(F32)
    cond_act = jax.nn.silu(cond_float).astype(BF)
    cond_parts = cond_act.reshape(held, n_dp, rows)
    if layout.direct:
        (cond_parts,) = after([cond_parts], [swap(modbias, "dp", 0)])
    cond_rows = lax.all_to_all(cond_parts, "dp", 1, 0, tiled=True).reshape(n_dp * held, rows)
    part = jnp.dot(cond_rows, modulator, preferred_element_type=F32)
    part = part + jnp.where(lax.axis_index("dp") == 0, modbias.astype(F32), 0.0)
    part = lax.all_to_all(part.reshape(n_dp, held, -1), "dp", 0, 0, tiled=True)

    def pack(*first):
        return call(
            pack_kernel, None, here, [latents.reshape(held, tok, width), part], [],
            [shaped((held, tok + 16, width), BF)], [], [pltpu.VMEM((16, width), F32)], "pack", first,
        )[0]

    offset_shapes = [shaped((1, n), F32) for n in ( 3 * width, width, wide * width, width)]
    if layout.direct:
        me = lax.axis_index("dp").reshape(1).astype(jnp.int32)
        u1, offsets, proj_offset, up_offset, down_offset = call(
            spread1_kernel, (width, chunk, rows, n_seq), here, blocks1, [],
            [shaped((4, rows, width), BF)] + offset_shapes, [], [], "spread1", [part],
        )
        (shards2,) = after([shards2], blocks1[1:])
        far2 = swap(shards2, "seq", 1)
        near2 = swap(jnp.stack([shards2, far2]), "seq", 0)
        w1 = gather_square(u1, [near2])
        (u2,) = call(
            spread2_kernel, spec_seq, here, [shards2, far2, near2], [],
            [shaped((2 * wide, rows, width), BF)], [], [], "spread2", [w1[6][0], w1[8][0]],
        )
        packed = to_latents(pack(near2))
        (cotangent,) = call(
            copy_kernel, None, here, [cotangent], [],
            [shaped(cotangent.shape, BF)], [], [], "cotangent", [packed],
        )
        cot = to_latents(cotangent.reshape(held, tok, width)).reshape(length, width)
    else:
        packed = to_latents(pack())
        cot = to_latents(cotangent.reshape(held, tok, width)).reshape(length, width)
        me = jnp.zeros((1,), jnp.int32)
        order = jnp.arange(n_seq) ^ lax.axis_index("seq")
        b1, b2 = (jnp.take(jnp.stack(b), order, axis=0) for b in (blocks1, blocks2))
        b1, b_off = b1[:, :rows], b1[:, rows:]
        b_up, b_down = b2[:, 0], b2[:, 1]
        u_qkv = b1[:, :, : 3 * chunk].transpose(1, 0, 2).reshape(rows, 3, width).transpose(1, 0, 2)
        u_proj = b1[:, :, 3 * chunk :].transpose(1, 0, 2).reshape(1, rows, width)
        u_up = b_up.transpose(1, 0, 2).reshape(rows, wide, width).transpose(1, 0, 2)
        u_down = b_down.reshape(n_seq, rows, wide, chunk).transpose(2, 1, 0, 3).reshape(wide, rows, width)
        natural = lambda v: gather_dp(v).transpose(1, 0, 2, 3).reshape(v.shape[0], width, width)
        w1 = [(natural(jnp.concatenate([u_qkv, u_proj])), 0, 0)]
        w2 = [(natural(u_up), 0, 0), (gather_dp(u_down).reshape(wide, width, width), 0, wide)]
        four = b_off[:, 0].reshape(n_seq, 4, chunk).transpose(1, 0, 2).reshape(4, 1, width).astype(F32)
        offsets = jnp.concatenate([four[0], jnp.zeros_like(four[0]), four[1]], axis=1)
        proj_offset, down_offset = four[2], four[3]
        up_offset = b_off[:, 1].reshape(1, -1).astype(F32)
    arrays1, spec1 = [w[0] for w in w1], tuple(w[1:] for w in w1)

    pairs = H // 2
    blocks, block_rows = layout.blocks, layout.rows

    def far_shapes(units):
        if not layout.direct:
            return [shaped((1, units, block_rows, width), BF)]
        block = (block_rows, width)
        return (
            [shaped((4, units) + block, BF)]
            + [shaped((units,) + block, BF)] * 3
            + [shaped((units // 2,) + block, BF)] * 2
        )

    n1, n2 = len(w1), 10 if layout.direct else len(w2)
    hidden1, qkv, attended, branch1, middle, mod, tokens = call(
        attend_kernel,
        (width, spec1, factor, pairs),
        me,
        [packed, offsets, proj_offset],
        arrays1,
        [
            shaped((length, width), BF),
            shaped((3, length, width), BF),
            shaped((length, width), BF),
            shaped((length, width), F32),
            shaped((length, width), F32),
            shaped((1, 6 * width), F32),
            shaped((length, width), BF),
        ],
        [],
        [pltpu.VMEM((4, blocks, block_rows, width), BF), dma((n1,))],
        "attention",
    )
    if layout.direct:
        w2 = gather_square(u2, [middle, cot])
    arrays2, spec2 = [w[0] for w in w2], tuple(w[1:] for w in w2)
    *grads2, result, dbefore, dgate2, up_bias, down_bias = call(
        mlp_kernel,
        (width, wide, spec2),
        me,
        [middle, mod, cot, up_offset, down_offset],
        arrays2,
        [
            shaped((length, width), BF),
            shaped((wide, length, width), BF),
            shaped((1, width), F32),
            shaped((1, wide * width), F32),
            shaped((1, width), F32),
        ],
        far_shapes(2 * wide),
        [
            pltpu.VMEM((wide, blocks, block_rows, width), BF),
            pltpu.VMEM((blocks, wide, block_rows, width), BF),
            pltpu.VMEM((blocks, wide, block_rows, width), BF),
            pltpu.VMEM((blocks, wide, block_rows, width), BF),
            pltpu.VMEM((wide, length, width), BF),
            pltpu.VMEM((wide, length, width), F32),
            dma((n2,)),
            dma((n2,)),
            dma((2 * blocks + 2,)),
        ],
        "mlp",
    )
    dmiddle, dbranch1, datt, sums1, proj_bias = call(
        middle_back_kernel,
        (width, wide, spec2, spec1),
        me,
        [middle, mod, cot, dbefore, branch1],
        arrays2 + arrays1,
        [
            shaped((length, width), F32),
            shaped((length, width), BF),
            shaped((length, width), BF),
            shaped((1, 3 * width), F32),
            shaped((1, width), F32),
        ],
        [],
        [
            pltpu.VMEM((wide, blocks, block_rows, width), BF),
            pltpu.VMEM((1, blocks, block_rows, width), BF),
            dma((n2,)),
            dma((n1,)),
        ],
        "middle_back",
    )
    if layout.direct:
        kept2, others2 = grads2[0], [swap(g, "dp", 0) for g in grads2[1:]]
        first2 = scatter_first(kept2, others2, [datt])
        low2, high2 = swap(first2[0], "dp", 2), swap(first2[1], "dp", 1)
        x_high2, y_low2 = swap(first2[2], "dp", 1), swap(first2[3], "dp", 2)
        result = to_tokens(result)
    *grads1, dqkv, qv_bias = call(
        attend_back_kernel,
        (width, factor, pairs),
        me,
        [dbranch1, datt, attended, hidden1, qkv],
        [],
        [shaped((3, length, width), BF), shaped((1, 2 * width), F32)],
        far_shapes(4),
        [pltpu.VMEM((blocks, 4, block_rows, width), BF), dma((blocks + 1,))],
        "attention_back",
        first2 if layout.direct else (),
    )
    if layout.direct:
        kept1, others1 = grads1[0], [swap(g, "dp", 0) for g in grads1[1:]]
        last2 = scatter_last(kept2, others2, low2, high2, [dqkv, x_high2, y_low2])
        x_low2, y_high2 = swap(last2[0], "dp", 1), swap(last2[1], "dp", 2)
    assert n_seq == 4 and wide == 4
    (packed,) = call(
        input_back_kernel,
        (width, tok, chunk, spec1),
        me,
        [tokens, mod, dmiddle, dqkv, sums1, dgate2, qv_bias, proj_bias, up_bias, down_bias],
        arrays1,
        [shaped((n_seq, tok + 16, width), BF)],
        [],
        [
            pltpu.VMEM((3, blocks, block_rows, width), BF),
            pltpu.VMEM((1, 6 * width), F32),
            pltpu.VMEM((16, width), F32),
            dma((n1,)),
        ],
        "input_back",
        [result] + list(last2) if layout.direct else (),
        4 * 10**9,
    )

    if layout.direct:
        first1 = scatter_first(kept1, others1, [x_low2, y_high2])
        low1, high1 = swap(first1[0], "dp", 2), swap(first1[1], "dp", 1)
        x_high1, y_low1 = swap(first1[2], "dp", 1), swap(first1[3], "dp", 2)
        (packed,) = after([packed], [x_low2, y_high2])
    packed = lax.all_to_all(packed, "seq", 0, 0, tiled=True)
    token_grad = packed[:, :tok].reshape(micro, lats, tok, width)
    small = packed[:, tok : tok + 4].reshape(n_seq, 4 * width)
    small = jnp.broadcast_to(small[None], (n_dp,) + small.shape)
    small = lax.all_to_all(small, "dp", 0, 0, tiled=True).reshape(n_dp * held, 4 * width)
    grad_mod, row_sums, dcond = call(
        mod_grad_kernel, n_seq, here, [small, cond_rows, modulator], [],
        [
            shaped(modulator.shape, F32),
            shaped((1, 4 * width), F32),
            shaped((n_dp * n_seq, held, rows), F32),
        ],
        [], [], "mod_grad",
    )
    row_sums = row_sums.reshape(4 * width)
    grad_mod_offset = row_sums[: modulator.shape[1]]
    dcond = lax.all_to_all(dcond, ("dp", "seq"), 0, 0, tiled=True)
    if layout.direct:
        blocks2 = call(
            collect2_kernel, spec_seq, here,
            [(kept2, (0,), (1,)), others2[0], x_low2, x_high2, y_low2, y_high2], [], [],
            [shaped((2, rows, width), BF)] * n_seq,
            [pltpu.VMEM((n_seq, 2, rows, width), BF), dma((n_seq,))], "collect2",
        )
        over_z2 = swap_seq(blocks2[1:])
        last1 = scatter_last(kept1, others1, low1, high1, [blocks2[0], x_high1, y_low1])
        x_low1, y_high1 = swap(last1[0], "dp", 1), swap(last1[1], "dp", 2)
    if layout.direct:
        blocks1 = call(
            collect1_kernel, spec_seq, here,
            [(kept1, (0,), (1,)), others1[0], x_low1, x_high1, y_low1, y_high1], [], [],
            [shaped((rows, width), BF)] * n_seq,
            [pltpu.VMEM((n_seq, rows, width), BF), dma((n_seq,))], "collect1", over_z2,
        )
        over_z1 = swap_seq(blocks1[1:])

    if layout.direct:
        up_out, down_out = call(
            final2_kernel, spec_seq, here, [blocks2[0]] + over_z2, [],
            [shaped((rows, width), F32), shaped((wide * rows, chunk), F32)], [], [], "final2",
        )
        qkv_out, proj_out = call(
            final1_kernel, spec_seq, here, [blocks1[0]] + over_z1, [],
            [shaped((rows, 3 * chunk), F32), shaped((rows, chunk), F32)], [], [], "final1", [dcond],
        )
    else:
        unit_rows = lambda v: v.reshape(-1, n_dp, rows, width).transpose(1, 0, 2, 3)
        s1 = scatter_dp(unit_rows(grads1[0][0]))
        s_up = scatter_dp(unit_rows(grads2[0][0, :wide]))
        s_down = scatter_dp(grads2[0][0, wide:].reshape(n_dp, wide, rows, width))
        t1 = s1[:3].transpose(1, 0, 2).reshape(rows, n_seq, 3 * chunk)
        t1 = jnp.concatenate([t1, s1[3].reshape(rows, n_seq, chunk)], axis=2).transpose(1, 0, 2)
        t2 = s_up.transpose(1, 0, 2).reshape(rows, n_seq, -1).transpose(1, 0, 2)
        t3 = s_down.reshape(wide * rows, n_seq, chunk).transpose(1, 0, 2)
        r1, up_out, down_out = scatter_seq(t1), scatter_seq(t2), scatter_seq(t3)
        qkv_out, proj_out = r1[:, : 3 * chunk], r1[:, 3 * chunk :]
        result = to_tokens(result)
    dcond = jnp.sum(dcond.reshape(n_dp, n_seq, held, rows), axis=1)
    dcond = dcond.transpose(1, 0, 2).reshape(held, width)
    dconds = jax.vjp(jax.nn.silu, cond_float)[1](dcond)[0].reshape(micro, lats, width)

    at_q = 3 * width // 2
    at = [at_q, at_q + chunk, 3 * width, 2 * width, 3 * width + chunk]
    bias_grads = (querybias, valuebias, projbias, expandbias, contractbias)
    sums = [row_sums[first : first + b.shape[0]] for first, b in zip(at, bias_grads)]
    return (
        result,
        token_grad,
        dconds,
        grad_mod,
        grad_mod_offset,
        qkv_out,
        sums[0],
        sums[1],
        proj_out,
        sums[2],
        up_out,
        sums[3],
        down_out,
        sums[4],
    )


def solution(mesh):
    placed = (
        P(None, "dp", "seq", None),
        P(None, "dp", None),
        P("dp", "seq"),
        P("seq"),
        P("dp", "seq"),
        P("seq"),
        P("seq"),
        P("dp", "seq"),
        P("seq"),
        P("dp", "seq"),
        P("seq"),
        P("dp", "seq"),
        P("seq"),
        P(None, "dp", "seq", None),
    )
    return jax.shard_map(
        local,
        mesh=mesh,
        in_specs=placed,
        out_specs=(
            P(None, "dp", "seq", None),
            P(None, "dp", "seq", None),
            P(None, "dp", None),
            P("dp", "seq"),
            P("seq"),
            P("dp", "seq"),
            P("seq"),
            P("seq"),
            P("dp", "seq"),
            P("seq"),
            P("dp", "seq"),
            P("seq"),
            P("dp", "seq"),
            P("seq"),
        ),
        check_vma=False,
    )
```

```python
import functools

import jax
import jax.numpy as jnp
from jax import lax
from jax.experimental import pallas as pl
from jax.experimental.pallas import tpu as pltpu
from jax.sharding import PartitionSpec as P

H = 12
EPSILON = 1e-06
BF = jnp.bfloat16
F32 = jnp.float32


def bits_of(count):
    bits = count.bit_length() - 1
    assert 1 << bits == count
    return bits


def swap(values, axis, bit):
    count = lax.axis_size(axis)
    return lax.ppermute(values, axis, [(i, i ^ (1 << bit)) for i in range(count)])


def own_bit(axis, bit):
    return (lax.axis_index(axis) >> bit) & 1


def after(values, first):
    far = pl.BlockSpec(memory_space=pl.ANY)
    return pl.pallas_call(
        lambda *refs: None,
        out_shape=[jax.ShapeDtypeStruct(v.shape, v.dtype) for v in values],
        in_specs=[far] * (len(values) + len(first)),
        out_specs=[far] * len(values),
        input_output_aliases={i: i for i in range(len(values))},
        cost_estimate=pl.CostEstimate(flops=0, bytes_accessed=0, transcendentals=0),
        name="after",
    )(*values, *first)


def halve(values, axis, bit):
    index = own_bit(axis, bit)
    sent = lax.dynamic_index_in_dim(values, 1 - index, 0, keepdims=False)
    kept = lax.dynamic_index_in_dim(values, index, 0, keepdims=False)
    other = swap(sent.astype(BF), axis, bit)
    return kept.astype(F32) + other.astype(F32)


def scatter_seq(values):
    count = bits_of(lax.axis_size("seq"))
    shape = values.shape[1:]
    values = values.reshape((2,) * count + shape)
    values = values.transpose(list(range(count - 1, -1, -1)) + list(range(count, count + len(shape))))
    for bit in range(count):
        values = halve(values, "seq", bit)
    return values


class Layout:
    def __init__(self, n_dp, n_seq, rows, width):
        self.direct = rows % 16 == 0 and n_dp == 8 and n_seq == 4
        self.blocks = n_dp if self.direct else 1
        self.rows = rows if self.direct else width


def mask_of(place, order):
    return sum(((place >> j) & 1) << bit for j, bit in enumerate(order))


def gather_dp(units):
    part = units[None]
    order = list(range(bits_of(lax.axis_size("dp"))))[::-1]
    for bit in order:
        part = jnp.concatenate([part, swap(part, "dp", bit)], axis=0)
    count = part.shape[0]
    place = [0] * count
    for index in range(count):
        place[mask_of(index, order)] = index
    wanted = jnp.asarray(place)[jnp.arange(count) ^ lax.axis_index("dp")]
    return jnp.take(part, wanted, axis=0)


def scatter_dp(values):
    count = bits_of(values.shape[0])
    values = jnp.take(values, jnp.arange(1 << count) ^ lax.axis_index("dp"), axis=0)
    values = values.reshape((2,) * count + values.shape[1:]).astype(F32)
    for bit in range(count - 1, -1, -1):
        values = values[0] + swap(values[1].astype(BF), "dp", bit).astype(F32)
    return values


def gather_square(units, first=()):
    middle = units.shape[0] // 2
    over_x, over_y = swap(units, "dp", 1), swap(units, "dp", 2)
    low, high = cut(over_x, over_y, first)
    low, high = swap(low, "dp", 2), swap(high, "dp", 1)
    near = [(units, 0, 0), (over_x, 2, 0), (over_y, 4, 0), (low, 6, 0), (high, 6, middle)]
    far = [(swap(part, "dp", 0), mask | 1, first) for part, mask, first in near]
    return [entry for pair in zip(near, far) for entry in pair]


def scatter_first(kept, others, first=()):
    _, units, rows, columns = kept.shape
    middle = units // 2
    half = jax.ShapeDtypeStruct((middle, rows, columns), BF)
    part = lambda place, high: (kept, (place, high), (1, middle))
    low_in, high_in, over_x, over_y = others[3], others[4], others[1], others[2]
    return call(
        add_kernel, 2, jnp.zeros((1,), jnp.int32),
        [part(3, 0), low_in, part(3, 1), high_in]
        + [part(1, 1), (over_x, (1,), (middle,)), part(2, 0), (over_y, (0,), (middle,))],
        [], [half] * 4, [], [], "first_sums", first,
    )


def scatter_last(kept, others, low_in, high_in, first=()):
    _, units, rows, columns = kept.shape
    middle = units // 2
    half = jax.ShapeDtypeStruct((middle, rows, columns), BF)
    part = lambda place, high: (kept, (place, high), (1, middle))
    return call(
        add_kernel, 3, jnp.zeros((1,), jnp.int32),
        [part(1, 0), (others[1], (0,), (middle,)), low_in]
        + [part(2, 1), (others[2], (1,), (middle,)), high_in],
        [], [half] * 2, [], [], "last_sums", first,
    )


def cut(over_x, over_y, first=()):
    half = jax.ShapeDtypeStruct((over_x.shape[0] // 2,) + over_x.shape[1:], BF)
    return call(
        cut_kernel, None, jnp.zeros((1,), jnp.int32),
        [(over_x, (0,), half.shape[:1]), (over_y, (1,), half.shape[:1])], [],
        [half, half], [], [], "cut", first,
    )


def gather_seq(values):
    found = {0: values}
    for bit in range(bits_of(lax.axis_size("seq")) - 1, -1, -1):
        found.update({mask | 1 << bit: swap(v, "seq", bit) for mask, v in list(found.items())})
    return [found[mask] for mask in range(len(found))]


def swap_seq(values):
    count = lax.axis_size("seq")
    return [
        lax.ppermute(value, "seq", [(i, i ^ (mask + 1)) for i in range(count)])
        for mask, value in enumerate(values)
    ]


def dot(a, b):
    return jnp.dot(a, b, preferred_element_type=F32)


def dot_back(a, b):
    return lax.dot_general(a, b, (((1,), (1,)), ((), ())), preferred_element_type=F32)


def dot_outer(a, b):
    return lax.dot_general(a, b, (((0,), (0,)), ((), ())), preferred_element_type=F32)


def normalize(values):
    center = values - jnp.mean(values, axis=-1, keepdims=True)
    inverse = lax.rsqrt(jnp.mean(center * center, axis=-1, keepdims=True) + EPSILON)
    return (center * inverse, inverse)


def norm_back(grad_normed, normed, inverse):
    first = jnp.mean(grad_normed, axis=-1, keepdims=True)
    second = jnp.mean(grad_normed * normed, axis=-1, keepdims=True)
    return inverse * (grad_normed - first - normed * second)


def total(values):
    return jnp.sum(values.astype(F32), axis=0, keepdims=True)


def loads(pieces, refs, me, target, span, sems):
    copies = []
    for ref, (mask, first) in zip(refs, pieces):
        low, high = max(span[0], first), min(span[1], first + ref.shape[0])
        if low < high:
            view = target(me ^ mask, low - span[0], high - span[0])
            copies.append(
                pltpu.make_async_copy(ref.at[low - first : high - first], view, sems.at[len(copies)])
            )
    return copies


def start(copies):
    for copy in copies:
        copy.start()


def finish(copies):
    for copy in copies:
        copy.wait()


def by_unit(scratch):
    return lambda block, low, high: scratch.at[low:high, block]


def by_block(scratch):
    return lambda block, low, high: scratch.at[block, low:high]


def matrix_of(scratch, unit):
    block = scratch[unit]
    return block.reshape(block.shape[0] * block.shape[1], block.shape[2])


def stores(scratch, outs, me, units, sems, base):
    copies = []
    blocks = scratch.shape[0]
    for mask in range(blocks):
        place = mask >> 1
        out = outs[0].at[place]
        if mask & 1:
            out = outs[1 + place] if place < 3 else None
        count = units[1] - units[0]
        spans = [(out, 0, units[0], count)]
        if out is None:
            middle = outs[4].shape[0]
            spans = [
                (outs[4 + half], max(half * middle - units[0], 0), max(units[0] - half * middle, 0),
                 min(units[1], (half + 1) * middle) - max(units[0], half * middle))
                for half in range(2)
            ]
        for target, source, first, number in spans:
            if number > 0:
                copies.append(
                    pltpu.make_async_copy(
                        scratch.at[me ^ mask, source : source + number],
                        target.at[first : first + number],
                        sems.at[base + len(copies)],
                    )
                )
    return copies


def lanes(shape):
    return lax.broadcasted_iota(jnp.int32, shape, 1)


def copy_kernel(spec, me_ref, source, target):
    target[...] = source[...]


def pack_kernel(spec, me_ref, tokens_ref, part_ref, out_ref, rows):
    held, tok, width = tokens_ref.shape
    half = width // 2
    mod = part_ref[0]
    for index in range(1, part_ref.shape[0]):
        mod = mod + part_ref[index]
    high = mod.astype(BF).astype(F32)
    low = mod - high
    rows[...] = jnp.zeros_like(rows)
    for index in range(held):
        out_ref[index, :tok] = tokens_ref[index]
        own = slice(index, index + 1)
        rows[0:1] = high[own, :width]
        rows[1:2] = low[own, :width]
        rows[2:3, :half] = high[own, width:]
        rows[2:3, half:] = low[own, width:]
        out_ref[index, tok:] = rows[...].astype(BF)


def attend_kernel(spec, me_ref, packed_ref, qkv_off_ref, proj_off_ref, *rest):
    width, pieces, factor, pairs = spec
    refs, rest = rest[: len(pieces)], rest[len(pieces) :]
    hidden_ref, qkv_ref, att_ref, branch_ref, middle_ref, mod_ref, tokens_ref, weights, sems = rest
    me = me_ref[0]
    count, tok = packed_ref.shape[0], packed_ref.shape[1] - 16
    half = width // 2
    for seq in range(count):
        tokens_ref[seq * tok : (seq + 1) * tok] = packed_ref[seq, :tok]
        row = packed_ref[seq, tok:].astype(F32)
        at = seq * (width + half)
        mod_ref[:, at : at + width] = row[0:1] + row[1:2]
        mod_ref[:, at + width : at + width + half] = row[2:3, :half] + row[2:3, half:]
    copies = loads(pieces, refs, me, by_unit(weights), (0, 4), sems)
    start(copies)
    tokens = tokens_ref[...].astype(F32)
    part = lambda i: mod_ref[:, i * width : (i + 1) * width]
    normed, _ = normalize(tokens)
    hidden = (normed * (1.0 + part(1)) + part(0)).astype(BF)
    hidden_ref[...] = hidden
    finish(copies)
    for unit in range(3):
        offset = qkv_off_ref[:, unit * width : (unit + 1) * width]
        qkv_ref[unit] = (dot(hidden, matrix_of(weights, unit)) + offset).astype(BF)
    for pair in range(pairs):
        cols = slice(pair * 128, (pair + 1) * 128)
        q, k, v = qkv_ref[0, :, cols], qkv_ref[1, :, cols], qkv_ref[2, :, cols]
        first = lanes(k.shape) < 64
        mixed = []
        for which in range(2):
            masked = jnp.where(first if which == 0 else ~first, k, jnp.zeros_like(k))
            scores = dot_back(q, masked) * factor
            expo = jnp.exp(scores - jnp.max(scores, axis=-1, keepdims=True))
            probs = expo * (1.0 / jnp.sum(expo, axis=-1, keepdims=True))
            mixed.append(dot(probs.astype(BF), v))
        att_ref[:, cols] = jnp.where(first, mixed[0], mixed[1]).astype(BF)
    branch = dot(att_ref[...], matrix_of(weights, 3)) + proj_off_ref[...]
    branch_ref[...] = branch
    middle_ref[...] = tokens + part(2) * branch


GELU_C = 0.7978845608028654
GELU_A = 0.044715


def mlp_kernel(spec, me_ref, middle_ref, mod_ref, cot_ref, up_off_ref, down_off_ref, *rest):
    width, wide, pieces = spec
    refs, rest = rest[: len(pieces)], rest[len(pieces) :]
    outs, rest = rest[: len(rest) - 14], rest[len(rest) - 14 :]
    (
        result_ref, dbefore_ref, gate_ref, up_bias_ref, down_bias_ref,
        up, down, up_grad, down_grad, active, slope, up_sems, down_sems, out_sems,
    ) = rest
    me = me_ref[0]
    up_copies = loads(pieces, refs, me, by_unit(up), (0, wide), up_sems)
    down_copies = loads(pieces, refs, me, by_block(down), (wide, 2 * wide), down_sems)
    start(up_copies)
    start(down_copies)
    part = lambda i: mod_ref[:, i * width : (i + 1) * width]
    middle = middle_ref[...]
    cot = cot_ref[...].astype(F32)
    normed, _ = normalize(middle)
    hidden = (normed * (1.0 + part(4)) + part(3)).astype(BF)
    gate = part(5)
    dbranch = (gate * cot).astype(BF)
    down_bias_ref[...] = total(dbranch)
    finish(up_copies)
    for unit in range(wide):
        before = dot(hidden, matrix_of(up, unit)) + up_off_ref[:, unit * width : (unit + 1) * width]
        square = before * before
        bent = jnp.tanh(GELU_C * before * (1.0 + GELU_A * square))
        active[unit] = (0.5 * before * (1.0 + bent)).astype(BF)
        slope[unit] = 0.5 * (1.0 + bent) + (0.5 * GELU_C) * before * (1.0 - bent * bent) * (
            1.0 + (3.0 * GELU_A) * square
        )
    finish(down_copies)
    down_rows = down[...].reshape(wide * width, width)
    grads = down_grad.shape
    span = grads[0] // wide if grads[0] > 1 else 0
    branch = down_off_ref[...]
    for unit in range(wide):
        branch = branch + dot(active[unit], down_rows[unit * width : (unit + 1) * width])
        grad = dot_outer(active[unit], dbranch).astype(BF)
        if span:
            down_grad[unit * span : (unit + 1) * span] = grad.reshape((span,) + grads[1:])
        else:
            down_grad[0, unit] = grad
    down_stores = stores(down_grad, outs, me, (wide, 2 * wide), out_sems, 0)
    start(down_stores)
    result_ref[...] = (middle + gate * branch).astype(BF)
    gate_ref[...] = total(cot * branch)
    for unit in range(wide):
        dactive = dot_back(dbranch, down_rows[unit * width : (unit + 1) * width])
        dbefore = (dactive * slope[unit]).astype(BF)
        dbefore_ref[unit] = dbefore
        up_bias_ref[:, unit * width : (unit + 1) * width] = total(dbefore)
        grad = dot_outer(hidden, dbefore).astype(BF)
        up_grad[:, unit] = grad.reshape(up_grad.shape[0], up_grad.shape[2], width)
    up_stores = stores(up_grad, outs, me, (0, wide), out_sems, len(down_stores))
    start(up_stores)
    finish(down_stores)
    finish(up_stores)


def middle_back_kernel(spec, me_ref, middle_ref, mod_ref, cot_ref, dbefore_ref, branch_ref, *rest):
    width, wide, up_pieces, pieces = spec
    up_refs, rest = rest[: len(up_pieces)], rest[len(up_pieces) :]
    refs, rest = rest[: len(pieces)], rest[len(pieces) :]
    dmiddle_ref, dbranch_ref, datt_ref, sums_ref, bias_ref, up, proj, up_sems, proj_sems = rest
    me = me_ref[0]
    up_copies = loads(up_pieces, up_refs, me, by_unit(up), (0, wide), up_sems)
    proj_copies = loads(pieces, refs, me, by_unit(proj), (3, 4), proj_sems)
    start(up_copies)
    start(proj_copies)
    part = lambda i: mod_ref[:, i * width : (i + 1) * width]
    normed, inverse = normalize(middle_ref[...])
    finish(up_copies)
    dhidden = dot_back(dbefore_ref[0], matrix_of(up, 0))
    for unit in range(1, wide):
        dhidden = dhidden + dot_back(dbefore_ref[unit], matrix_of(up, unit))
    dmiddle = cot_ref[...].astype(F32) + norm_back(dhidden * (1.0 + part(4)), normed, inverse)
    dmiddle_ref[...] = dmiddle
    dbranch = (part(2) * dmiddle).astype(BF)
    dbranch_ref[...] = dbranch
    sums_ref[:, :width] = total(dmiddle * branch_ref[...])
    sums_ref[:, width : 2 * width] = total(dhidden)
    sums_ref[:, 2 * width : 3 * width] = total(dhidden * normed)
    bias_ref[...] = total(dbranch)
    finish(proj_copies)
    datt_ref[...] = dot_back(dbranch, matrix_of(proj, 0)).astype(BF)


def attend_back_kernel(spec, me_ref, dbranch_ref, datt_ref, att_ref, hidden_ref, qkv_ref, *rest):
    width, factor, pairs = spec
    outs, rest = rest[: len(rest) - 4], rest[len(rest) - 4 :]
    dqkv_ref, bias_ref, grads, out_sems = rest
    me = me_ref[0]
    for pair in range(pairs):
        cols = slice(pair * 128, (pair + 1) * 128)
        q, k, v = qkv_ref[0, :, cols], qkv_ref[1, :, cols], qkv_ref[2, :, cols]
        da = datt_ref[:, cols]
        first = lanes(k.shape) < 64
        zero = jnp.zeros_like(k)
        grad_q, grad_k, grad_v = [], [], []
        for which in range(2):
            own = first if which == 0 else ~first
            scores = dot_back(q, jnp.where(own, k, zero)) * factor
            expo = jnp.exp(scores - jnp.max(scores, axis=-1, keepdims=True))
            probs = expo * (1.0 / jnp.sum(expo, axis=-1, keepdims=True))
            dprobs = dot_back(da, jnp.where(own, v, zero))
            rowsum = jnp.sum(dprobs * probs, axis=-1, keepdims=True)
            dscores = (probs * (dprobs - rowsum)).astype(BF)
            grad_q.append(dot(dscores, k))
            grad_k.append(dot_outer(dscores, q))
            grad_v.append(dot_outer(probs.astype(BF), da))
        dqkv_ref[0, :, cols] = (jnp.where(first, grad_q[0], grad_q[1]) * factor).astype(BF)
        dqkv_ref[1, :, cols] = (jnp.where(first, grad_k[0], grad_k[1]) * factor).astype(BF)
        dqkv_ref[2, :, cols] = jnp.where(first, grad_v[0], grad_v[1]).astype(BF)
    bias_ref[:, :width] = total(dqkv_ref[0])
    bias_ref[:, width : 2 * width] = total(dqkv_ref[2])
    shape = (grads.shape[0], grads.shape[2], width)
    for unit in range(3):
        grads[:, unit] = dot_outer(hidden_ref[...], dqkv_ref[unit]).astype(BF).reshape(shape)
    grads[:, 3] = dot_outer(att_ref[...], dbranch_ref[...]).astype(BF).reshape(shape)
    out_copies = stores(grads, outs, me, (0, 4), out_sems, 0)
    start(out_copies)
    finish(out_copies)


def input_back_kernel(spec, me_ref, tokens_ref, mod_ref, dmiddle_ref, dqkv_ref, sums_ref, gate_ref,
                      qv_ref, proj_off_ref, up_off_ref, down_off_ref, *rest):
    width, tok, chunk, pieces = spec
    refs, rest = rest[: len(pieces)], rest[len(pieces) :]
    packed_ref, weights, dmod, rows, sems = rest
    copies = loads(pieces, refs, me_ref[0], by_unit(weights), (0, 3), sems)
    start(copies)
    normed, inverse = normalize(tokens_ref[...].astype(F32))
    finish(copies)
    dhidden = dot_back(dqkv_ref[0], matrix_of(weights, 0))
    for unit in range(1, 3):
        dhidden = dhidden + dot_back(dqkv_ref[unit], matrix_of(weights, unit))
    dmod[:, :width] = total(dhidden)
    dmod[:, width : 2 * width] = total(dhidden * normed)
    dmod[:, 2 * width : 5 * width] = sums_ref[...]
    dmod[:, 5 * width :] = gate_ref[...]
    scale = 1.0 + mod_ref[:, width : 2 * width]
    dtokens = (dmiddle_ref[...] + norm_back(dhidden * scale, normed, inverse)).astype(BF)
    rows[...] = jnp.zeros_like(rows)
    half = width // 2
    for seq in range(packed_ref.shape[0]):
        packed_ref[seq, :tok] = dtokens[seq * tok : (seq + 1) * tok]
        at, own = seq * (width + half), slice(seq * chunk, (seq + 1) * chunk)
        rows[0:1, :] = dmod[:, at : at + width]
        rows[1:2, :half] = dmod[:, at + width : at + width + half]
        rows[1:2, half : half + chunk] = qv_ref[:, own]
        rows[1:2, half + chunk :] = qv_ref[:, width + seq * chunk : width + (seq + 1) * chunk]
        rows[2:3, :] = up_off_ref[:, seq * width : (seq + 1) * width]
        rows[3:4, :chunk] = proj_off_ref[:, own]
        rows[3:4, chunk : 2 * chunk] = down_off_ref[:, own]
        packed_ref[seq, tok:] = rows[...].astype(BF)


def mod_grad_kernel(spec, me_ref, small_ref, cond_ref, matrix_ref, grad_ref, sums_ref, dcond_ref):
    n_seq = spec
    columns = matrix_ref.shape[1]
    dmod = small_ref[:, :columns]
    grad_ref[...] = dot_outer(cond_ref[...], dmod)
    sums_ref[...] = total(small_ref[...])
    dcond = dot_back(dmod, matrix_ref[...])
    held = dcond_ref.shape[1]
    for index in range(dcond_ref.shape[0]):
        first = index // n_seq * held
        dcond_ref[index] = dcond[first : first + held]


def chunks(width, chunk):
    table = []
    for seq in range(width // chunk):
        entry = []
        for j in range(3):
            index = 3 * seq + j
            per = width // chunk
            entry.append((index // per, index % per * chunk, j * chunk, chunk))
        entry.append((3, seq * chunk, 3 * chunk, chunk))
        table.append(entry)
    return table


def pick(values, me, seq):
    value = values[0]
    for mask in range(1, len(values)):
        value = jnp.where((me ^ seq) == mask, values[mask], value)
    return value


def spread1_kernel(spec, me_ref, *refs):
    width, chunk, rows, n_seq = spec
    blocks, (units_ref, qkv_off_ref, proj_off_ref, up_off_ref, down_off_ref) = refs[:n_seq], refs[n_seq:]
    me = me_ref[0]
    qkv_off_ref[...] = jnp.zeros_like(qkv_off_ref)
    for seq, entry in enumerate(chunks(width, chunk)):
        value = pick([ref[...] for ref in blocks], me, seq)
        for unit, there, here, columns in entry:
            units_ref[unit, :, there : there + columns] = value[:rows, here : here + columns]
        tail = value[rows:].astype(F32)
        for index, ref in enumerate((qkv_off_ref, qkv_off_ref, proj_off_ref, down_off_ref)):
            at = seq * chunk + (2 * width if index == 1 else 0)
            ref[:, at : at + chunk] = tail[0:1, index * chunk : (index + 1) * chunk]
        up_off_ref[:, seq * width : (seq + 1) * width] = tail[1:2]


def spread2_kernel(spec, me_ref, own_ref, far_ref, near_ref, units_ref):
    width, chunk, wide, n_seq = spec
    me = me_ref[0]
    for seq in range(n_seq):
        value = pick([own_ref[...], near_ref[0], far_ref[...], near_ref[1]], me, seq)
        units_ref[seq] = value[0]
        for unit in range(wide):
            units_ref[wide + unit, :, seq * chunk : (seq + 1) * chunk] = value[
                1, :, unit * chunk : (unit + 1) * chunk
            ]


def add_kernel(spec, me_ref, *refs):
    outs = refs[len(refs) * spec // (spec + 1) :]
    for index, out in enumerate(outs):
        terms = refs[index * spec : (index + 1) * spec]
        for unit in range(out.shape[0]):
            value = terms[0][0, unit].astype(F32)
            for term in terms[1:]:
                value = value + term[unit].astype(F32)
            out[unit] = value.astype(BF)


def cut_kernel(spec, me_ref, over_x, over_y, low, high):
    low[...] = over_x[...]
    high[...] = over_y[...]


def summed(refs, unit):
    kept, other, x_low, x_high, y_low, y_high = refs
    middle = x_low.shape[0]
    over_x, over_y = (x_low, y_low) if unit < middle else (x_high, y_high)
    value = kept[0, unit].astype(F32) + other[unit].astype(F32)
    return value + (over_x[unit % middle].astype(F32) + over_y[unit % middle].astype(F32))


def send_blocks(scratch, outs, me, sems):
    copies = [
        pltpu.make_async_copy(scratch.at[me ^ mask], out, sems.at[mask]) for mask, out in enumerate(outs)
    ]
    start(copies)
    finish(copies)


def collect1_kernel(spec, me_ref, *refs):
    width, chunk, wide, n_seq = spec
    ins, outs, (scratch, sems) = refs[:6], refs[6 : 6 + n_seq], refs[6 + n_seq :]
    table = chunks(width, chunk)
    for unit in range(4):
        value = summed(ins, unit).astype(BF)
        for seq, entry in enumerate(table):
            for source, there, here, columns in entry:
                if source == unit:
                    scratch[seq, :, here : here + columns] = value[:, there : there + columns]
    send_blocks(scratch, outs, me_ref[0], sems)


def collect2_kernel(spec, me_ref, *refs):
    width, chunk, wide, n_seq = spec
    ins, outs, (scratch, sems) = refs[:6], refs[6 : 6 + n_seq], refs[6 + n_seq :]
    for unit in range(wide):
        scratch[unit, 0] = summed(ins, unit).astype(BF)
        value = summed(ins, wide + unit).astype(BF)
        for seq in range(n_seq):
            scratch[seq, 1, :, unit * chunk : (unit + 1) * chunk] = value[:, seq * chunk : (seq + 1) * chunk]
    send_blocks(scratch, outs, me_ref[0], sems)


def final1_kernel(spec, me_ref, *refs):
    width, chunk, wide, n_seq = spec
    value = refs[0][...].astype(F32)
    for ref in refs[1:n_seq]:
        value = value + ref[...].astype(F32)
    qkv_ref, proj_ref = refs[n_seq:]
    qkv_ref[...] = value[:, : 3 * chunk]
    proj_ref[...] = value[:, 3 * chunk :]


def final2_kernel(spec, me_ref, *refs):
    width, chunk, wide, n_seq = spec
    result_in, packed_ref, up_ref, down_ref, result_ref, tokens_ref = refs[n_seq:]
    result_ref[...] = result_in[...]
    tokens_ref[...] = packed_ref[:, : tokens_ref.shape[1]]
    rows = up_ref.shape[0]
    for index in range(2):
        value = refs[0][index].astype(F32)
        for ref in refs[1:n_seq]:
            value = value + ref[index].astype(F32)
        if index == 0:
            up_ref[...] = value
        else:
            for unit in range(wide):
                down_ref[unit * rows : (unit + 1) * rows] = value[:, unit * chunk : (unit + 1) * chunk]


def call(body, spec, me, inputs, pieces, outs, far_outs, scratch, name, first=(), flops=0):
    vmem = pl.BlockSpec(memory_space=pltpu.VMEM)
    far = pl.BlockSpec(memory_space=pl.ANY)
    specs, arrays = [], []
    for value in inputs:
        if isinstance(value, tuple):
            value, index, shape = value
            index = index + (0,) * (value.ndim - len(index))
            shape = shape + value.shape[len(shape) :]
            specs.append(pl.BlockSpec(shape, lambda step, index=index: index))
        else:
            specs.append(vmem)
        arrays.append(value)
    used = 1 + len(inputs) + len(pieces)

    def run(*refs):
        body(spec, *refs[:used], *refs[used + len(first) :])

    return pl.pallas_call(
        run,
        grid=(1,),
        out_shape=far_outs + outs,
        in_specs=[pl.BlockSpec(memory_space=pltpu.SMEM)]
        + specs
        + [far] * (len(pieces) + len(first)),
        out_specs=[far] * len(far_outs) + [vmem] * len(outs),
        scratch_shapes=scratch,
        compiler_params=pltpu.CompilerParams(vmem_limit_bytes=52 * 1024 * 1024),
        cost_estimate=pl.CostEstimate(flops=flops, bytes_accessed=0, transcendentals=0),
        name=name,
    )(me, *arrays, *pieces, *first)


def local(
    latents,
    conditions,
    modulator,
    modbias,
    qkvweight,
    querybias,
    valuebias,
    projection,
    projbias,
    expand,
    expandbias,
    contract,
    contractbias,
    cotangent,
):
    n_dp, n_seq = lax.axis_size("dp"), lax.axis_size("seq")
    micro, lats, tok, width = latents.shape
    held = micro * lats
    assert held == n_seq
    length = n_seq * tok
    rows = width // n_dp
    chunk = width // n_seq
    wide = contract.shape[0] // rows
    head = width // H
    assert 2 * head == 128
    factor = head ** (-0.5)
    layout = Layout(n_dp, n_seq, rows, width)

    def to_latents(values):
        return lax.all_to_all(values, "seq", 0, 0, tiled=True)

    def to_tokens(values):
        return lax.all_to_all(values.reshape(n_seq, tok, width), "seq", 0, 0, tiled=True)

    shaped = jax.ShapeDtypeStruct
    dma = pltpu.SemaphoreType.DMA
    here = lax.axis_index("seq").reshape(1).astype(jnp.int32)
    spec_seq = (width, chunk, wide, n_seq)
    offsets_low = jnp.concatenate([querybias, valuebias, projbias, contractbias, expandbias])
    tail = jnp.pad(offsets_low.reshape(-1, width), ((0, 14), (0, 0)))
    down_shard = contract.reshape(wide, rows, chunk)
    shards1 = jnp.concatenate([jnp.concatenate([qkvweight, projection], axis=1), tail])
    shards2 = jnp.stack([expand, jnp.concatenate([down_shard[i] for i in range(wide)], axis=1)])
    if layout.direct:
        blocks1 = [shards1] + swap_seq([shards1] * (n_seq - 1))
    else:
        blocks1, blocks2 = gather_seq(shards1), gather_seq(shards2)

    cond_float = conditions.reshape(held, width).astype(F32)
    cond_act = jax.nn.silu(cond_float).astype(BF)
    cond_parts = cond_act.reshape(held, n_dp, rows)
    if layout.direct:
        (cond_parts,) = after([cond_parts], [swap(modbias, "dp", 0)])
    cond_rows = lax.all_to_all(cond_parts, "dp", 1, 0, tiled=True).reshape(n_dp * held, rows)
    part = jnp.dot(cond_rows, modulator, preferred_element_type=F32)
    part = part + jnp.where(lax.axis_index("dp") == 0, modbias.astype(F32), 0.0)
    part = lax.all_to_all(part.reshape(n_dp, held, -1), "dp", 0, 0, tiled=True)

    def pack(*first):
        return call(
            pack_kernel, None, here, [latents.reshape(held, tok, width), part], [],
            [shaped((held, tok + 16, width), BF)], [], [pltpu.VMEM((16, width), F32)], "pack", first,
        )[0]

    offset_shapes = [shaped((1, n), F32) for n in ( 3 * width, width, wide * width, width)]
    if layout.direct:
        me = lax.axis_index("dp").reshape(1).astype(jnp.int32)
        u1, offsets, proj_offset, up_offset, down_offset = call(
            spread1_kernel, (width, chunk, rows, n_seq), here, blocks1, [],
            [shaped((4, rows, width), BF)] + offset_shapes, [], [], "spread1", [part],
        )
        (shards2,) = after([shards2], blocks1[1:])
        far2 = swap(shards2, "seq", 1)
        near2 = swap(jnp.stack([shards2, far2]), "seq", 0)
        w1 = gather_square(u1, [near2])
        (u2,) = call(
            spread2_kernel, spec_seq, here, [shards2, far2, near2], [],
            [shaped((2 * wide, rows, width), BF)], [], [], "spread2", [w1[6][0], w1[8][0]],
        )
        packed = to_latents(pack(near2))
        (cotangent,) = call(
            copy_kernel, None, here, [cotangent], [],
            [shaped(cotangent.shape, BF)], [], [], "cotangent", [packed],
        )
        cot = to_latents(cotangent.reshape(held, tok, width)).reshape(length, width)
    else:
        packed = to_latents(pack())
        cot = to_latents(cotangent.reshape(held, tok, width)).reshape(length, width)
        me = jnp.zeros((1,), jnp.int32)
        order = jnp.arange(n_seq) ^ lax.axis_index("seq")
        b1, b2 = (jnp.take(jnp.stack(b), order, axis=0) for b in (blocks1, blocks2))
        b1, b_off = b1[:, :rows], b1[:, rows:]
        b_up, b_down = b2[:, 0], b2[:, 1]
        u_qkv = b1[:, :, : 3 * chunk].transpose(1, 0, 2).reshape(rows, 3, width).transpose(1, 0, 2)
        u_proj = b1[:, :, 3 * chunk :].transpose(1, 0, 2).reshape(1, rows, width)
        u_up = b_up.transpose(1, 0, 2).reshape(rows, wide, width).transpose(1, 0, 2)
        u_down = b_down.reshape(n_seq, rows, wide, chunk).transpose(2, 1, 0, 3).reshape(wide, rows, width)
        natural = lambda v: gather_dp(v).transpose(1, 0, 2, 3).reshape(v.shape[0], width, width)
        w1 = [(natural(jnp.concatenate([u_qkv, u_proj])), 0, 0)]
        w2 = [(natural(u_up), 0, 0), (gather_dp(u_down).reshape(wide, width, width), 0, wide)]
        four = b_off[:, 0].reshape(n_seq, 4, chunk).transpose(1, 0, 2).reshape(4, 1, width).astype(F32)
        offsets = jnp.concatenate([four[0], jnp.zeros_like(four[0]), four[1]], axis=1)
        proj_offset, down_offset = four[2], four[3]
        up_offset = b_off[:, 1].reshape(1, -1).astype(F32)
    arrays1, spec1 = [w[0] for w in w1], tuple(w[1:] for w in w1)

    pairs = H // 2
    blocks, block_rows = layout.blocks, layout.rows

    def far_shapes(units):
        if not layout.direct:
            return [shaped((1, units, block_rows, width), BF)]
        block = (block_rows, width)
        return (
            [shaped((4, units) + block, BF)]
            + [shaped((units,) + block, BF)] * 3
            + [shaped((units // 2,) + block, BF)] * 2
        )

    n1, n2 = len(w1), 10 if layout.direct else len(w2)
    hidden1, qkv, attended, branch1, middle, mod, tokens = call(
        attend_kernel,
        (width, spec1, factor, pairs),
        me,
        [packed, offsets, proj_offset],
        arrays1,
        [
            shaped((length, width), BF),
            shaped((3, length, width), BF),
            shaped((length, width), BF),
            shaped((length, width), F32),
            shaped((length, width), F32),
            shaped((1, 6 * width), F32),
            shaped((length, width), BF),
        ],
        [],
        [pltpu.VMEM((4, blocks, block_rows, width), BF), dma((n1,))],
        "attention",
    )
    if layout.direct:
        w2 = gather_square(u2, [middle, cot])
    arrays2, spec2 = [w[0] for w in w2], tuple(w[1:] for w in w2)
    *grads2, result, dbefore, dgate2, up_bias, down_bias = call(
        mlp_kernel,
        (width, wide, spec2),
        me,
        [middle, mod, cot, up_offset, down_offset],
        arrays2,
        [
            shaped((length, width), BF),
            shaped((wide, length, width), BF),
            shaped((1, width), F32),
            shaped((1, wide * width), F32),
            shaped((1, width), F32),
        ],
        far_shapes(2 * wide),
        [
            pltpu.VMEM((wide, blocks, block_rows, width), BF),
            pltpu.VMEM((blocks, wide, block_rows, width), BF),
            pltpu.VMEM((blocks, wide, block_rows, width), BF),
            pltpu.VMEM((blocks, wide, block_rows, width), BF),
            pltpu.VMEM((wide, length, width), BF),
            pltpu.VMEM((wide, length, width), F32),
            dma((n2,)),
            dma((n2,)),
            dma((2 * blocks + 2,)),
        ],
        "mlp",
    )
    dmiddle, dbranch1, datt, sums1, proj_bias = call(
        middle_back_kernel,
        (width, wide, spec2, spec1),
        me,
        [middle, mod, cot, dbefore, branch1],
        arrays2 + arrays1,
        [
            shaped((length, width), F32),
            shaped((length, width), BF),
            shaped((length, width), BF),
            shaped((1, 3 * width), F32),
            shaped((1, width), F32),
        ],
        [],
        [
            pltpu.VMEM((wide, blocks, block_rows, width), BF),
            pltpu.VMEM((1, blocks, block_rows, width), BF),
            dma((n2,)),
            dma((n1,)),
        ],
        "middle_back",
    )
    if layout.direct:
        kept2, others2 = grads2[0], [swap(g, "dp", 0) for g in grads2[1:]]
        first2 = scatter_first(kept2, others2, [datt])
        low2, high2 = swap(first2[0], "dp", 2), swap(first2[1], "dp", 1)
        x_high2, y_low2 = swap(first2[2], "dp", 1), swap(first2[3], "dp", 2)
        result = to_tokens(result)
    *grads1, dqkv, qv_bias = call(
        attend_back_kernel,
        (width, factor, pairs),
        me,
        [dbranch1, datt, attended, hidden1, qkv],
        [],
        [shaped((3, length, width), BF), shaped((1, 2 * width), F32)],
        far_shapes(4),
        [pltpu.VMEM((blocks, 4, block_rows, width), BF), dma((blocks + 1,))],
        "attention_back",
        first2 if layout.direct else (),
    )
    if layout.direct:
        kept1, others1 = grads1[0], [swap(g, "dp", 0) for g in grads1[1:]]
        last2 = scatter_last(kept2, others2, low2, high2, [dqkv, x_high2, y_low2])
        x_low2, y_high2 = swap(last2[0], "dp", 1), swap(last2[1], "dp", 2)
    assert n_seq == 4 and wide == 4
    (packed,) = call(
        input_back_kernel,
        (width, tok, chunk, spec1),
        me,
        [tokens, mod, dmiddle, dqkv, sums1, dgate2, qv_bias, proj_bias, up_bias, down_bias],
        arrays1,
        [shaped((n_seq, tok + 16, width), BF)],
        [],
        [
            pltpu.VMEM((3, blocks, block_rows, width), BF),
            pltpu.VMEM((1, 6 * width), F32),
            pltpu.VMEM((16, width), F32),
            dma((n1,)),
        ],
        "input_back",
        list(last2) if layout.direct else (),
        4 * 10**9,
    )

    if layout.direct:
        first1 = scatter_first(kept1, others1, [x_low2, y_high2])
        low1, high1 = swap(first1[0], "dp", 2), swap(first1[1], "dp", 1)
        x_high1, y_low1 = swap(first1[2], "dp", 1), swap(first1[3], "dp", 2)
        (packed,) = after([packed], list(first1) + [result])
    packed = lax.all_to_all(packed, "seq", 0, 0, tiled=True)
    token_grad = packed[:, :tok]
    small = packed[:, tok : tok + 4].reshape(n_seq, 4 * width)
    small = jnp.broadcast_to(small[None], (n_dp,) + small.shape)
    small = lax.all_to_all(small, "dp", 0, 0, tiled=True).reshape(n_dp * held, 4 * width)
    grad_mod, row_sums, dcond_part = call(
        mod_grad_kernel, n_seq, here, [small, cond_rows, modulator], [],
        [
            shaped(modulator.shape, F32),
            shaped((1, 4 * width), F32),
            shaped((n_dp * n_seq, held, rows), F32),
        ],
        [], [], "mod_grad",
    )
    row_sums = row_sums.reshape(4 * width)
    grad_mod_offset = row_sums[: modulator.shape[1]]
    dcond = lax.all_to_all(dcond_part, ("dp", "seq"), 0, 0, tiled=True)
    if layout.direct:
        blocks2 = call(
            collect2_kernel, spec_seq, here,
            [(kept2, (0,), (1,)), others2[0], x_low2, x_high2, y_low2, y_high2], [], [],
            [shaped((2, rows, width), BF)] * n_seq,
            [pltpu.VMEM((n_seq, 2, rows, width), BF), dma((n_seq,))], "collect2",
        )
        over_z2 = swap_seq(blocks2[1:])
        last1 = scatter_last(kept1, others1, low1, high1, [blocks2[0], x_high1, y_low1])
        x_low1, y_high1 = swap(last1[0], "dp", 1), swap(last1[1], "dp", 2)
    if layout.direct:
        blocks1 = call(
            collect1_kernel, spec_seq, here,
            [(kept1, (0,), (1,)), others1[0], x_low1, x_high1, y_low1, y_high1], [], [],
            [shaped((rows, width), BF)] * n_seq,
            [pltpu.VMEM((n_seq, rows, width), BF), dma((n_seq,))], "collect1", over_z2,
        )
        over_z1 = swap_seq(blocks1[1:])

    if layout.direct:
        up_out, down_out, result, token_grad = call(
            final2_kernel, spec_seq, here, [blocks2[0]] + over_z2 + [result, packed], [],
            [shaped((rows, width), F32), shaped((wide * rows, chunk), F32)]
            + [shaped((held, tok, width), BF)] * 2, [], [], "final2", [dcond_part],
        )
        qkv_out, proj_out = call(
            final1_kernel, spec_seq, here, [blocks1[0]] + over_z1, [],
            [shaped((rows, 3 * chunk), F32), shaped((rows, chunk), F32)], [], [], "final1", [dcond],
        )
    else:
        unit_rows = lambda v: v.reshape(-1, n_dp, rows, width).transpose(1, 0, 2, 3)
        s1 = scatter_dp(unit_rows(grads1[0][0]))
        s_up = scatter_dp(unit_rows(grads2[0][0, :wide]))
        s_down = scatter_dp(grads2[0][0, wide:].reshape(n_dp, wide, rows, width))
        t1 = s1[:3].transpose(1, 0, 2).reshape(rows, n_seq, 3 * chunk)
        t1 = jnp.concatenate([t1, s1[3].reshape(rows, n_seq, chunk)], axis=2).transpose(1, 0, 2)
        t2 = s_up.transpose(1, 0, 2).reshape(rows, n_seq, -1).transpose(1, 0, 2)
        t3 = s_down.reshape(wide * rows, n_seq, chunk).transpose(1, 0, 2)
        r1, up_out, down_out = scatter_seq(t1), scatter_seq(t2), scatter_seq(t3)
        qkv_out, proj_out = r1[:, : 3 * chunk], r1[:, 3 * chunk :]
        result = to_tokens(result)
    dcond = jnp.sum(dcond.reshape(n_dp, n_seq, held, rows), axis=1)
    dcond = dcond.transpose(1, 0, 2).reshape(held, width)
    dconds = jax.vjp(jax.nn.silu, cond_float)[1](dcond)[0].reshape(micro, lats, width)

    at_q = 3 * width // 2
    at = [at_q, at_q + chunk, 3 * width, 2 * width, 3 * width + chunk]
    bias_grads = (querybias, valuebias, projbias, expandbias, contractbias)
    sums = [row_sums[first : first + b.shape[0]] for first, b in zip(at, bias_grads)]
    return (
        result.reshape(micro, lats, tok, width),
        token_grad.reshape(micro, lats, tok, width),
        dconds,
        grad_mod,
        grad_mod_offset,
        qkv_out,
        sums[0],
        sums[1],
        proj_out,
        sums[2],
        up_out,
        sums[3],
        down_out,
        sums[4],
    )


def solution(mesh):
    placed = (
        P(None, "dp", "seq", None),
        P(None, "dp", None),
        P("dp", "seq"),
        P("seq"),
        P("dp", "seq"),
        P("seq"),
        P("seq"),
        P("dp", "seq"),
        P("seq"),
        P("dp", "seq"),
        P("seq"),
        P("dp", "seq"),
        P("seq"),
        P(None, "dp", "seq", None),
    )
    return jax.shard_map(
        local,
        mesh=mesh,
        in_specs=placed,
        out_specs=(
            P(None, "dp", "seq", None),
            P(None, "dp", "seq", None),
            P(None, "dp", None),
            P("dp", "seq"),
            P("seq"),
            P("dp", "seq"),
            P("seq"),
            P("seq"),
            P("dp", "seq"),
            P("seq"),
            P("dp", "seq"),
            P("seq"),
            P("dp", "seq"),
            P("seq"),
        ),
        check_vma=False,
    )
```

```python
import functools

import jax
import jax.numpy as jnp
from jax import lax
from jax.experimental import pallas as pl
from jax.experimental.pallas import tpu as pltpu
from jax.sharding import PartitionSpec as P

H = 12
EPSILON = 1e-06
BF = jnp.bfloat16
F32 = jnp.float32


def bits_of(count):
    bits = count.bit_length() - 1
    assert 1 << bits == count
    return bits


def swap(values, axis, bit):
    count = lax.axis_size(axis)
    return lax.ppermute(values, axis, [(i, i ^ (1 << bit)) for i in range(count)])


def own_bit(axis, bit):
    return (lax.axis_index(axis) >> bit) & 1


def after(values, first):
    far = pl.BlockSpec(memory_space=pl.ANY)
    return pl.pallas_call(
        lambda *refs: None,
        out_shape=[jax.ShapeDtypeStruct(v.shape, v.dtype) for v in values],
        in_specs=[far] * (len(values) + len(first)),
        out_specs=[far] * len(values),
        input_output_aliases={i: i for i in range(len(values))},
        cost_estimate=pl.CostEstimate(flops=0, bytes_accessed=0, transcendentals=0),
        name="after",
    )(*values, *first)


def halve(values, axis, bit):
    index = own_bit(axis, bit)
    sent = lax.dynamic_index_in_dim(values, 1 - index, 0, keepdims=False)
    kept = lax.dynamic_index_in_dim(values, index, 0, keepdims=False)
    other = swap(sent.astype(BF), axis, bit)
    return kept.astype(F32) + other.astype(F32)


def scatter_seq(values):
    count = bits_of(lax.axis_size("seq"))
    shape = values.shape[1:]
    values = values.reshape((2,) * count + shape)
    values = values.transpose(list(range(count - 1, -1, -1)) + list(range(count, count + len(shape))))
    for bit in range(count):
        values = halve(values, "seq", bit)
    return values


class Layout:
    def __init__(self, n_dp, n_seq, rows, width):
        self.direct = rows % 16 == 0 and n_dp == 8 and n_seq == 4
        self.blocks = n_dp if self.direct else 1
        self.rows = rows if self.direct else width


def mask_of(place, order):
    return sum(((place >> j) & 1) << bit for j, bit in enumerate(order))


def gather_dp(units):
    part = units[None]
    order = list(range(bits_of(lax.axis_size("dp"))))[::-1]
    for bit in order:
        part = jnp.concatenate([part, swap(part, "dp", bit)], axis=0)
    count = part.shape[0]
    place = [0] * count
    for index in range(count):
        place[mask_of(index, order)] = index
    wanted = jnp.asarray(place)[jnp.arange(count) ^ lax.axis_index("dp")]
    return jnp.take(part, wanted, axis=0)


def scatter_dp(values):
    count = bits_of(values.shape[0])
    values = jnp.take(values, jnp.arange(1 << count) ^ lax.axis_index("dp"), axis=0)
    values = values.reshape((2,) * count + values.shape[1:]).astype(F32)
    for bit in range(count - 1, -1, -1):
        values = values[0] + swap(values[1].astype(BF), "dp", bit).astype(F32)
    return values


def gather_square(units, first=()):
    middle = units.shape[0] // 2
    over_x, over_y = swap(units, "dp", 1), swap(units, "dp", 2)
    low, high = cut(over_x, over_y, first)
    low, high = swap(low, "dp", 2), swap(high, "dp", 1)
    near = [(units, 0, 0), (over_x, 2, 0), (over_y, 4, 0), (low, 6, 0), (high, 6, middle)]
    far = [(swap(part, "dp", 0), mask | 1, first) for part, mask, first in near]
    return [entry for pair in zip(near, far) for entry in pair]


def scatter_first(kept, others, first=()):
    _, units, rows, columns = kept.shape
    middle = units // 2
    half = jax.ShapeDtypeStruct((middle, rows, columns), BF)
    part = lambda place, high: (kept, (place, high), (1, middle))
    low_in, high_in, over_x, over_y = others[3], others[4], others[1], others[2]
    return call(
        add_kernel, 2, jnp.zeros((1,), jnp.int32),
        [part(3, 0), low_in, part(3, 1), high_in]
        + [part(1, 1), (over_x, (1,), (middle,)), part(2, 0), (over_y, (0,), (middle,))],
        [], [half] * 4, [], [], "first_sums", first,
    )


def scatter_last(kept, others, low_in, high_in, first=()):
    _, units, rows, columns = kept.shape
    middle = units // 2
    half = jax.ShapeDtypeStruct((middle, rows, columns), BF)
    part = lambda place, high: (kept, (place, high), (1, middle))
    return call(
        add_kernel, 3, jnp.zeros((1,), jnp.int32),
        [part(1, 0), (others[1], (0,), (middle,)), low_in]
        + [part(2, 1), (others[2], (1,), (middle,)), high_in],
        [], [half] * 2, [], [], "last_sums", first,
    )


def whole_first(kept, others, first=()):
    whole = jax.ShapeDtypeStruct(kept.shape[1:], BF)
    return call(
        whole_kernel, None, jnp.zeros((1,), jnp.int32),
        [(kept, (3,), (1,)), others[3], others[4], (kept, (1,), (1,)), others[1]],
        [], [whole, whole], [], [], "whole_sums", first,
    )


def whole_last(kept, others, corner_in, first=()):
    whole = jax.ShapeDtypeStruct(kept.shape[1:], BF)
    return call(
        add_kernel, 3, jnp.zeros((1,), jnp.int32), [(kept, (2,), (1,)), others[2], corner_in],
        [], [whole], [], [], "whole_last", first,
    )[0]


def cut(over_x, over_y, first=()):
    half = jax.ShapeDtypeStruct((over_x.shape[0] // 2,) + over_x.shape[1:], BF)
    return call(
        cut_kernel, None, jnp.zeros((1,), jnp.int32),
        [(over_x, (0,), half.shape[:1]), (over_y, (1,), half.shape[:1])], [],
        [half, half], [], [], "cut", first,
    )


def gather_seq(values):
    found = {0: values}
    for bit in range(bits_of(lax.axis_size("seq")) - 1, -1, -1):
        found.update({mask | 1 << bit: swap(v, "seq", bit) for mask, v in list(found.items())})
    return [found[mask] for mask in range(len(found))]


def swap_seq(values):
    count = lax.axis_size("seq")
    return [
        lax.ppermute(value, "seq", [(i, i ^ (mask + 1)) for i in range(count)])
        for mask, value in enumerate(values)
    ]


def dot(a, b):
    return jnp.dot(a, b, preferred_element_type=F32)


def dot_back(a, b):
    return lax.dot_general(a, b, (((1,), (1,)), ((), ())), preferred_element_type=F32)


def dot_outer(a, b):
    return lax.dot_general(a, b, (((0,), (0,)), ((), ())), preferred_element_type=F32)


def normalize(values):
    center = values - jnp.mean(values, axis=-1, keepdims=True)
    inverse = lax.rsqrt(jnp.mean(center * center, axis=-1, keepdims=True) + EPSILON)
    return (center * inverse, inverse)


def norm_back(grad_normed, normed, inverse):
    first = jnp.mean(grad_normed, axis=-1, keepdims=True)
    second = jnp.mean(grad_normed * normed, axis=-1, keepdims=True)
    return inverse * (grad_normed - first - normed * second)


def total(values):
    return jnp.sum(values.astype(F32), axis=0, keepdims=True)


def loads(pieces, refs, me, target, span, sems):
    copies = []
    for ref, (mask, first) in zip(refs, pieces):
        low, high = max(span[0], first), min(span[1], first + ref.shape[0])
        if low < high:
            view = target(me ^ mask, low - span[0], high - span[0])
            copies.append(
                pltpu.make_async_copy(ref.at[low - first : high - first], view, sems.at[len(copies)])
            )
    return copies


def start(copies):
    for copy in copies:
        copy.start()


def finish(copies):
    for copy in copies:
        copy.wait()


def by_unit(scratch):
    return lambda block, low, high: scratch.at[low:high, block]


def by_block(scratch):
    return lambda block, low, high: scratch.at[block, low:high]


def matrix_of(scratch, unit):
    block = scratch[unit]
    return block.reshape(block.shape[0] * block.shape[1], block.shape[2])


def stores(scratch, outs, me, units, sems, base):
    copies = []
    blocks = scratch.shape[0]
    for mask in range(blocks):
        place = mask >> 1
        out = outs[0].at[place]
        if mask & 1:
            out = outs[1 + place] if place < 3 else None
        count = units[1] - units[0]
        spans = [(out, 0, units[0], count)]
        if out is None:
            middle = outs[4].shape[0]
            spans = [
                (outs[4 + half], max(half * middle - units[0], 0), max(units[0] - half * middle, 0),
                 min(units[1], (half + 1) * middle) - max(units[0], half * middle))
                for half in range(2)
            ]
        for target, source, first, number in spans:
            if number > 0:
                copies.append(
                    pltpu.make_async_copy(
                        scratch.at[me ^ mask, source : source + number],
                        target.at[first : first + number],
                        sems.at[base + len(copies)],
                    )
                )
    return copies


def lanes(shape):
    return lax.broadcasted_iota(jnp.int32, shape, 1)


def copy_kernel(spec, me_ref, source, target):
    target[...] = source[...]


def pack_kernel(spec, me_ref, tokens_ref, part_ref, out_ref, rows):
    held, tok, width = tokens_ref.shape
    half = width // 2
    mod = part_ref[0]
    for index in range(1, part_ref.shape[0]):
        mod = mod + part_ref[index]
    high = mod.astype(BF).astype(F32)
    low = mod - high
    rows[...] = jnp.zeros_like(rows)
    for index in range(held):
        out_ref[index, :tok] = tokens_ref[index]
        own = slice(index, index + 1)
        rows[0:1] = high[own, :width]
        rows[1:2] = low[own, :width]
        rows[2:3, :half] = high[own, width:]
        rows[2:3, half:] = low[own, width:]
        out_ref[index, tok:] = rows[...].astype(BF)


def attend_kernel(spec, me_ref, packed_ref, qkv_off_ref, proj_off_ref, *rest):
    width, pieces, factor, pairs = spec
    refs, rest = rest[: len(pieces)], rest[len(pieces) :]
    hidden_ref, qkv_ref, att_ref, branch_ref, middle_ref, mod_ref, tokens_ref, weights, sems = rest
    me = me_ref[0]
    count, tok = packed_ref.shape[0], packed_ref.shape[1] - 16
    half = width // 2
    for seq in range(count):
        tokens_ref[seq * tok : (seq + 1) * tok] = packed_ref[seq, :tok]
        row = packed_ref[seq, tok:].astype(F32)
        at = seq * (width + half)
        mod_ref[:, at : at + width] = row[0:1] + row[1:2]
        mod_ref[:, at + width : at + width + half] = row[2:3, :half] + row[2:3, half:]
    copies = loads(pieces, refs, me, by_unit(weights), (0, 4), sems)
    start(copies)
    tokens = tokens_ref[...].astype(F32)
    part = lambda i: mod_ref[:, i * width : (i + 1) * width]
    normed, _ = normalize(tokens)
    hidden = (normed * (1.0 + part(1)) + part(0)).astype(BF)
    hidden_ref[...] = hidden
    finish(copies)
    for unit in range(3):
        offset = qkv_off_ref[:, unit * width : (unit + 1) * width]
        qkv_ref[unit] = (dot(hidden, matrix_of(weights, unit)) + offset).astype(BF)
    for pair in range(pairs):
        cols = slice(pair * 128, (pair + 1) * 128)
        q, k, v = qkv_ref[0, :, cols], qkv_ref[1, :, cols], qkv_ref[2, :, cols]
        first = lanes(k.shape) < 64
        mixed = []
        for which in range(2):
            masked = jnp.where(first if which == 0 else ~first, k, jnp.zeros_like(k))
            scores = dot_back(q, masked) * factor
            expo = jnp.exp(scores - jnp.max(scores, axis=-1, keepdims=True))
            probs = expo * (1.0 / jnp.sum(expo, axis=-1, keepdims=True))
            mixed.append(dot(probs.astype(BF), v))
        att_ref[:, cols] = jnp.where(first, mixed[0], mixed[1]).astype(BF)
    branch = dot(att_ref[...], matrix_of(weights, 3)) + proj_off_ref[...]
    branch_ref[...] = branch
    middle_ref[...] = tokens + part(2) * branch


GELU_C = 0.7978845608028654
GELU_A = 0.044715


def mlp_kernel(spec, me_ref, middle_ref, mod_ref, cot_ref, up_off_ref, down_off_ref, *rest):
    width, wide, pieces = spec
    refs, rest = rest[: len(pieces)], rest[len(pieces) :]
    outs, rest = rest[: len(rest) - 14], rest[len(rest) - 14 :]
    (
        result_ref, dbefore_ref, gate_ref, up_bias_ref, down_bias_ref,
        up, down, up_grad, down_grad, active, slope, up_sems, down_sems, out_sems,
    ) = rest
    me = me_ref[0]
    up_copies = loads(pieces, refs, me, by_unit(up), (0, wide), up_sems)
    down_copies = loads(pieces, refs, me, by_block(down), (wide, 2 * wide), down_sems)
    start(up_copies)
    start(down_copies)
    part = lambda i: mod_ref[:, i * width : (i + 1) * width]
    middle = middle_ref[...]
    cot = cot_ref[...].astype(F32)
    normed, _ = normalize(middle)
    hidden = (normed * (1.0 + part(4)) + part(3)).astype(BF)
    gate = part(5)
    dbranch = (gate * cot).astype(BF)
    down_bias_ref[...] = total(dbranch)
    finish(up_copies)
    for unit in range(wide):
        before = dot(hidden, matrix_of(up, unit)) + up_off_ref[:, unit * width : (unit + 1) * width]
        square = before * before
        bent = jnp.tanh(GELU_C * before * (1.0 + GELU_A * square))
        active[unit] = (0.5 * before * (1.0 + bent)).astype(BF)
        slope[unit] = 0.5 * (1.0 + bent) + (0.5 * GELU_C) * before * (1.0 - bent * bent) * (
            1.0 + (3.0 * GELU_A) * square
        )
    finish(down_copies)
    down_rows = down[...].reshape(wide * width, width)
    grads = down_grad.shape
    span = grads[0] // wide if grads[0] > 1 else 0
    branch = down_off_ref[...]
    for unit in range(wide):
        branch = branch + dot(active[unit], down_rows[unit * width : (unit + 1) * width])
        grad = dot_outer(active[unit], dbranch).astype(BF)
        if span:
            down_grad[unit * span : (unit + 1) * span] = grad.reshape((span,) + grads[1:])
        else:
            down_grad[0, unit] = grad
    down_stores = stores(down_grad, outs, me, (wide, 2 * wide), out_sems, 0)
    start(down_stores)
    result_ref[...] = (middle + gate * branch).astype(BF)
    gate_ref[...] = total(cot * branch)
    for unit in range(wide):
        dactive = dot_back(dbranch, down_rows[unit * width : (unit + 1) * width])
        dbefore = (dactive * slope[unit]).astype(BF)
        dbefore_ref[unit] = dbefore
        up_bias_ref[:, unit * width : (unit + 1) * width] = total(dbefore)
        grad = dot_outer(hidden, dbefore).astype(BF)
        up_grad[:, unit] = grad.reshape(up_grad.shape[0], up_grad.shape[2], width)
    up_stores = stores(up_grad, outs, me, (0, wide), out_sems, len(down_stores))
    start(up_stores)
    finish(down_stores)
    finish(up_stores)


def middle_back_kernel(spec, me_ref, middle_ref, mod_ref, cot_ref, dbefore_ref, branch_ref, *rest):
    width, wide, up_pieces, pieces = spec
    up_refs, rest = rest[: len(up_pieces)], rest[len(up_pieces) :]
    refs, rest = rest[: len(pieces)], rest[len(pieces) :]
    dmiddle_ref, dbranch_ref, datt_ref, sums_ref, bias_ref, up, proj, up_sems, proj_sems = rest
    me = me_ref[0]
    up_copies = loads(up_pieces, up_refs, me, by_unit(up), (0, wide), up_sems)
    proj_copies = loads(pieces, refs, me, by_unit(proj), (3, 4), proj_sems)
    start(up_copies)
    start(proj_copies)
    part = lambda i: mod_ref[:, i * width : (i + 1) * width]
    normed, inverse = normalize(middle_ref[...])
    finish(up_copies)
    dhidden = dot_back(dbefore_ref[0], matrix_of(up, 0))
    for unit in range(1, wide):
        dhidden = dhidden + dot_back(dbefore_ref[unit], matrix_of(up, unit))
    dmiddle = cot_ref[...].astype(F32) + norm_back(dhidden * (1.0 + part(4)), normed, inverse)
    dmiddle_ref[...] = dmiddle
    dbranch = (part(2) * dmiddle).astype(BF)
    dbranch_ref[...] = dbranch
    sums_ref[:, :width] = total(dmiddle * branch_ref[...])
    sums_ref[:, width : 2 * width] = total(dhidden)
    sums_ref[:, 2 * width : 3 * width] = total(dhidden * normed)
    bias_ref[...] = total(dbranch)
    finish(proj_copies)
    datt_ref[...] = dot_back(dbranch, matrix_of(proj, 0)).astype(BF)


def attend_back_kernel(spec, me_ref, dbranch_ref, datt_ref, att_ref, hidden_ref, qkv_ref, *rest):
    width, factor, pairs = spec
    outs, rest = rest[: len(rest) - 4], rest[len(rest) - 4 :]
    dqkv_ref, bias_ref, grads, out_sems = rest
    me = me_ref[0]
    for pair in range(pairs):
        cols = slice(pair * 128, (pair + 1) * 128)
        q, k, v = qkv_ref[0, :, cols], qkv_ref[1, :, cols], qkv_ref[2, :, cols]
        da = datt_ref[:, cols]
        first = lanes(k.shape) < 64
        zero = jnp.zeros_like(k)
        grad_q, grad_k, grad_v = [], [], []
        for which in range(2):
            own = first if which == 0 else ~first
            scores = dot_back(q, jnp.where(own, k, zero)) * factor
            expo = jnp.exp(scores - jnp.max(scores, axis=-1, keepdims=True))
            probs = expo * (1.0 / jnp.sum(expo, axis=-1, keepdims=True))
            dprobs = dot_back(da, jnp.where(own, v, zero))
            rowsum = jnp.sum(dprobs * probs, axis=-1, keepdims=True)
            dscores = (probs * (dprobs - rowsum)).astype(BF)
            grad_q.append(dot(dscores, k))
            grad_k.append(dot_outer(dscores, q))
            grad_v.append(dot_outer(probs.astype(BF), da))
        dqkv_ref[0, :, cols] = (jnp.where(first, grad_q[0], grad_q[1]) * factor).astype(BF)
        dqkv_ref[1, :, cols] = (jnp.where(first, grad_k[0], grad_k[1]) * factor).astype(BF)
        dqkv_ref[2, :, cols] = jnp.where(first, grad_v[0], grad_v[1]).astype(BF)
    bias_ref[:, :width] = total(dqkv_ref[0])
    bias_ref[:, width : 2 * width] = total(dqkv_ref[2])
    shape = (grads.shape[0], grads.shape[2], width)
    for unit in range(3):
        grads[:, unit] = dot_outer(hidden_ref[...], dqkv_ref[unit]).astype(BF).reshape(shape)
    grads[:, 3] = dot_outer(att_ref[...], dbranch_ref[...]).astype(BF).reshape(shape)
    out_copies = stores(grads, outs, me, (0, 4), out_sems, 0)
    start(out_copies)
    finish(out_copies)


def input_back_kernel(spec, me_ref, tokens_ref, mod_ref, dmiddle_ref, dqkv_ref, sums_ref, gate_ref,
                      qv_ref, proj_off_ref, up_off_ref, down_off_ref, result_ref, *rest):
    width, tok, chunk, pieces = spec
    refs, rest = rest[: len(pieces)], rest[len(pieces) :]
    packed_ref, weights, dmod, rows, sems = rest
    copies = loads(pieces, refs, me_ref[0], by_unit(weights), (0, 3), sems)
    start(copies)
    normed, inverse = normalize(tokens_ref[...].astype(F32))
    finish(copies)
    dhidden = dot_back(dqkv_ref[0], matrix_of(weights, 0))
    for unit in range(1, 3):
        dhidden = dhidden + dot_back(dqkv_ref[unit], matrix_of(weights, unit))
    dmod[:, :width] = total(dhidden)
    dmod[:, width : 2 * width] = total(dhidden * normed)
    dmod[:, 2 * width : 5 * width] = sums_ref[...]
    dmod[:, 5 * width :] = gate_ref[...]
    scale = 1.0 + mod_ref[:, width : 2 * width]
    dtokens = (dmiddle_ref[...] + norm_back(dhidden * scale, normed, inverse)).astype(BF)
    rows[...] = jnp.zeros_like(rows)
    half = width // 2
    for seq in range(packed_ref.shape[0]):
        packed_ref[seq, :tok] = dtokens[seq * tok : (seq + 1) * tok]
        at, own = seq * (width + half), slice(seq * chunk, (seq + 1) * chunk)
        rows[0:1, :] = dmod[:, at : at + width]
        rows[1:2, :half] = dmod[:, at + width : at + width + half]
        rows[1:2, half : half + chunk] = qv_ref[:, own]
        rows[1:2, half + chunk :] = qv_ref[:, width + seq * chunk : width + (seq + 1) * chunk]
        rows[2:3, :] = up_off_ref[:, seq * width : (seq + 1) * width]
        rows[3:4, :chunk] = proj_off_ref[:, own]
        rows[3:4, chunk : 2 * chunk] = down_off_ref[:, own]
        packed_ref[seq, tok : tok + 16] = rows[...].astype(BF)
        packed_ref[seq, tok + 16 :] = result_ref[seq * tok : (seq + 1) * tok]


def mod_grad_kernel(spec, me_ref, small_ref, cond_ref, matrix_ref, grad_ref, sums_ref, dcond_ref):
    n_seq = spec
    columns = matrix_ref.shape[1]
    dmod = small_ref[:, :columns]
    grad_ref[...] = dot_outer(cond_ref[...], dmod)
    sums_ref[...] = total(small_ref[...])
    dcond = dot_back(dmod, matrix_ref[...])
    held = dcond_ref.shape[1]
    for index in range(dcond_ref.shape[0]):
        first = index // n_seq * held
        dcond_ref[index] = dcond[first : first + held]


def chunks(width, chunk):
    table = []
    for seq in range(width // chunk):
        entry = []
        for j in range(3):
            index = 3 * seq + j
            per = width // chunk
            entry.append((index // per, index % per * chunk, j * chunk, chunk))
        entry.append((3, seq * chunk, 3 * chunk, chunk))
        table.append(entry)
    return table


def pick(values, me, seq):
    value = values[0]
    for mask in range(1, len(values)):
        value = jnp.where((me ^ seq) == mask, values[mask], value)
    return value


def spread1_kernel(spec, me_ref, *refs):
    width, chunk, rows, n_seq = spec
    blocks, (units_ref, qkv_off_ref, proj_off_ref, up_off_ref, down_off_ref) = refs[:n_seq], refs[n_seq:]
    me = me_ref[0]
    qkv_off_ref[...] = jnp.zeros_like(qkv_off_ref)
    for seq, entry in enumerate(chunks(width, chunk)):
        value = pick([ref[...] for ref in blocks], me, seq)
        for unit, there, here, columns in entry:
            units_ref[unit, :, there : there + columns] = value[:rows, here : here + columns]
        tail = value[rows:].astype(F32)
        for index, ref in enumerate((qkv_off_ref, qkv_off_ref, proj_off_ref, down_off_ref)):
            at = seq * chunk + (2 * width if index == 1 else 0)
            ref[:, at : at + chunk] = tail[0:1, index * chunk : (index + 1) * chunk]
        up_off_ref[:, seq * width : (seq + 1) * width] = tail[1:2]


def spread2_kernel(spec, me_ref, own_ref, far_ref, near_ref, units_ref):
    width, chunk, wide, n_seq = spec
    me = me_ref[0]
    for seq in range(n_seq):
        value = pick([own_ref[...], near_ref[0], far_ref[...], near_ref[1]], me, seq)
        units_ref[seq] = value[0]
        for unit in range(wide):
            units_ref[wide + unit, :, seq * chunk : (seq + 1) * chunk] = value[
                1, :, unit * chunk : (unit + 1) * chunk
            ]


def whole_kernel(spec, me_ref, kept_corner, low_in, high_in, kept_x, other_x, corner, side):
    middle = low_in.shape[0]
    for unit in range(2 * middle):
        source = low_in if unit < middle else high_in
        value = kept_corner[0, unit].astype(F32) + source[unit % middle].astype(F32)
        corner[unit] = value.astype(BF)
        side[unit] = (kept_x[0, unit].astype(F32) + other_x[unit].astype(F32)).astype(BF)


def add_kernel(spec, me_ref, *refs):
    outs = refs[len(refs) * spec // (spec + 1) :]
    for index, out in enumerate(outs):
        terms = refs[index * spec : (index + 1) * spec]
        for unit in range(out.shape[0]):
            value = terms[0][0, unit].astype(F32)
            for term in terms[1:]:
                value = value + term[unit].astype(F32)
            out[unit] = value.astype(BF)


def cut_kernel(spec, me_ref, over_x, over_y, low, high):
    low[...] = over_x[...]
    high[...] = over_y[...]


def summed(refs, unit):
    kept, other, x_low, x_high, y_low, y_high = refs
    middle = x_low.shape[0]
    over_x, over_y = (x_low, y_low) if unit < middle else (x_high, y_high)
    value = kept[0, unit].astype(F32) + other[unit].astype(F32)
    return value + (over_x[unit % middle].astype(F32) + over_y[unit % middle].astype(F32))


def send_blocks(scratch, outs, me, sems):
    copies = [
        pltpu.make_async_copy(scratch.at[me ^ mask], out, sems.at[mask]) for mask, out in enumerate(outs)
    ]
    start(copies)
    finish(copies)


def collect1_kernel(spec, me_ref, *refs):
    width, chunk, wide, n_seq = spec
    ins, outs, (scratch, sems) = refs[:6], refs[6 : 6 + n_seq], refs[6 + n_seq :]
    table = chunks(width, chunk)
    for unit in range(4):
        value = summed(ins, unit).astype(BF)
        for seq, entry in enumerate(table):
            for source, there, here, columns in entry:
                if source == unit:
                    scratch[seq, :, here : here + columns] = value[:, there : there + columns]
    send_blocks(scratch, outs, me_ref[0], sems)


def collect2_kernel(spec, me_ref, *refs):
    width, chunk, wide, n_seq = spec
    ins, outs, (scratch, sems) = refs[:6], refs[6 : 6 + n_seq], refs[6 + n_seq :]
    for unit in range(wide):
        scratch[unit, 0] = summed(ins, unit).astype(BF)
        value = summed(ins, wide + unit).astype(BF)
        for seq in range(n_seq):
            scratch[seq, 1, :, unit * chunk : (unit + 1) * chunk] = value[:, seq * chunk : (seq + 1) * chunk]
    send_blocks(scratch, outs, me_ref[0], sems)


def final1_kernel(spec, me_ref, *refs):
    width, chunk, wide, n_seq = spec
    value = refs[0][...].astype(F32)
    for ref in refs[1:n_seq]:
        value = value + ref[...].astype(F32)
    qkv_ref, proj_ref = refs[n_seq:]
    qkv_ref[...] = value[:, : 3 * chunk]
    proj_ref[...] = value[:, 3 * chunk :]


def final2_kernel(spec, me_ref, *refs):
    width, chunk, wide, n_seq = spec
    packed_ref, up_ref, down_ref, result_ref, tokens_ref = refs[n_seq:]
    tok = tokens_ref.shape[1]
    result_ref[...] = packed_ref[:, tok + 16 :]
    tokens_ref[...] = packed_ref[:, :tok]
    rows = up_ref.shape[0]
    for index in range(2):
        value = refs[0][index].astype(F32)
        for ref in refs[1:n_seq]:
            value = value + ref[index].astype(F32)
        if index == 0:
            up_ref[...] = value
        else:
            for unit in range(wide):
                down_ref[unit * rows : (unit + 1) * rows] = value[:, unit * chunk : (unit + 1) * chunk]


def call(body, spec, me, inputs, pieces, outs, far_outs, scratch, name, first=(), flops=0):
    vmem = pl.BlockSpec(memory_space=pltpu.VMEM)
    far = pl.BlockSpec(memory_space=pl.ANY)
    specs, arrays = [], []
    for value in inputs:
        if isinstance(value, tuple):
            value, index, shape = value
            index = index + (0,) * (value.ndim - len(index))
            shape = shape + value.shape[len(shape) :]
            specs.append(pl.BlockSpec(shape, lambda step, index=index: index))
        else:
            specs.append(vmem)
        arrays.append(value)
    used = 1 + len(inputs) + len(pieces)

    def run(*refs):
        body(spec, *refs[:used], *refs[used + len(first) :])

    return pl.pallas_call(
        run,
        grid=(1,),
        out_shape=far_outs + outs,
        in_specs=[pl.BlockSpec(memory_space=pltpu.SMEM)]
        + specs
        + [far] * (len(pieces) + len(first)),
        out_specs=[far] * len(far_outs) + [vmem] * len(outs),
        scratch_shapes=scratch,
        compiler_params=pltpu.CompilerParams(vmem_limit_bytes=52 * 1024 * 1024),
        cost_estimate=pl.CostEstimate(flops=flops, bytes_accessed=0, transcendentals=0),
        name=name,
    )(me, *arrays, *pieces, *first)


def local(
    latents,
    conditions,
    modulator,
    modbias,
    qkvweight,
    querybias,
    valuebias,
    projection,
    projbias,
    expand,
    expandbias,
    contract,
    contractbias,
    cotangent,
):
    n_dp, n_seq = lax.axis_size("dp"), lax.axis_size("seq")
    micro, lats, tok, width = latents.shape
    held = micro * lats
    assert held == n_seq
    length = n_seq * tok
    rows = width // n_dp
    chunk = width // n_seq
    wide = contract.shape[0] // rows
    head = width // H
    assert 2 * head == 128
    factor = head ** (-0.5)
    layout = Layout(n_dp, n_seq, rows, width)

    def to_latents(values):
        return lax.all_to_all(values, "seq", 0, 0, tiled=True)

    shaped = jax.ShapeDtypeStruct
    dma = pltpu.SemaphoreType.DMA
    here = lax.axis_index("seq").reshape(1).astype(jnp.int32)
    spec_seq = (width, chunk, wide, n_seq)
    offsets_low = jnp.concatenate([querybias, valuebias, projbias, contractbias, expandbias])
    tail = jnp.pad(offsets_low.reshape(-1, width), ((0, 14), (0, 0)))
    down_shard = contract.reshape(wide, rows, chunk)
    shards1 = jnp.concatenate([jnp.concatenate([qkvweight, projection], axis=1), tail])
    shards2 = jnp.stack([expand, jnp.concatenate([down_shard[i] for i in range(wide)], axis=1)])
    if layout.direct:
        blocks1 = [shards1] + swap_seq([shards1] * (n_seq - 1))
    else:
        blocks1, blocks2 = gather_seq(shards1), gather_seq(shards2)

    cond_float = conditions.reshape(held, width).astype(F32)
    cond_act = jax.nn.silu(cond_float).astype(BF)
    cond_parts = cond_act.reshape(held, n_dp, rows)
    if layout.direct:
        (cond_parts,) = after([cond_parts], [swap(modbias, "dp", 0)])
    cond_rows = lax.all_to_all(cond_parts, "dp", 1, 0, tiled=True).reshape(n_dp * held, rows)
    part = jnp.dot(cond_rows, modulator, preferred_element_type=F32)
    part = part + jnp.where(lax.axis_index("dp") == 0, modbias.astype(F32), 0.0)
    part = lax.all_to_all(part.reshape(n_dp, held, -1), "dp", 0, 0, tiled=True)

    def pack(*first):
        return call(
            pack_kernel, None, here, [latents.reshape(held, tok, width), part], [],
            [shaped((held, tok + 16, width), BF)], [], [pltpu.VMEM((16, width), F32)], "pack", first,
        )[0]

    offset_shapes = [shaped((1, n), F32) for n in ( 3 * width, width, wide * width, width)]
    if layout.direct:
        me = lax.axis_index("dp").reshape(1).astype(jnp.int32)
        u1, offsets, proj_offset, up_offset, down_offset = call(
            spread1_kernel, (width, chunk, rows, n_seq), here, blocks1, [],
            [shaped((4, rows, width), BF)] + offset_shapes, [], [], "spread1", [part],
        )
        (shards2,) = after([shards2], blocks1[1:])
        far2 = swap(shards2, "seq", 1)
        near2 = swap(jnp.stack([shards2, far2]), "seq", 0)
        w1 = gather_square(u1, [near2])
        (u2,) = call(
            spread2_kernel, spec_seq, here, [shards2, far2, near2], [],
            [shaped((2 * wide, rows, width), BF)], [], [], "spread2", [w1[6][0], w1[8][0]],
        )
        packed = to_latents(pack(near2))
        (cotangent,) = call(
            copy_kernel, None, here, [cotangent], [],
            [shaped(cotangent.shape, BF)], [], [], "cotangent", [packed],
        )
        cot = to_latents(cotangent.reshape(held, tok, width)).reshape(length, width)
    else:
        packed = to_latents(pack())
        cot = to_latents(cotangent.reshape(held, tok, width)).reshape(length, width)
        me = jnp.zeros((1,), jnp.int32)
        order = jnp.arange(n_seq) ^ lax.axis_index("seq")
        b1, b2 = (jnp.take(jnp.stack(b), order, axis=0) for b in (blocks1, blocks2))
        b1, b_off = b1[:, :rows], b1[:, rows:]
        b_up, b_down = b2[:, 0], b2[:, 1]
        u_qkv = b1[:, :, : 3 * chunk].transpose(1, 0, 2).reshape(rows, 3, width).transpose(1, 0, 2)
        u_proj = b1[:, :, 3 * chunk :].transpose(1, 0, 2).reshape(1, rows, width)
        u_up = b_up.transpose(1, 0, 2).reshape(rows, wide, width).transpose(1, 0, 2)
        u_down = b_down.reshape(n_seq, rows, wide, chunk).transpose(2, 1, 0, 3).reshape(wide, rows, width)
        natural = lambda v: gather_dp(v).transpose(1, 0, 2, 3).reshape(v.shape[0], width, width)
        w1 = [(natural(jnp.concatenate([u_qkv, u_proj])), 0, 0)]
        w2 = [(natural(u_up), 0, 0), (gather_dp(u_down).reshape(wide, width, width), 0, wide)]
        four = b_off[:, 0].reshape(n_seq, 4, chunk).transpose(1, 0, 2).reshape(4, 1, width).astype(F32)
        offsets = jnp.concatenate([four[0], jnp.zeros_like(four[0]), four[1]], axis=1)
        proj_offset, down_offset = four[2], four[3]
        up_offset = b_off[:, 1].reshape(1, -1).astype(F32)
    arrays1, spec1 = [w[0] for w in w1], tuple(w[1:] for w in w1)

    pairs = H // 2
    blocks, block_rows = layout.blocks, layout.rows

    def far_shapes(units):
        if not layout.direct:
            return [shaped((1, units, block_rows, width), BF)]
        block = (block_rows, width)
        return (
            [shaped((4, units) + block, BF)]
            + [shaped((units,) + block, BF)] * 3
            + [shaped((units // 2,) + block, BF)] * 2
        )

    n1, n2 = len(w1), 10 if layout.direct else len(w2)
    hidden1, qkv, attended, branch1, middle, mod, tokens = call(
        attend_kernel,
        (width, spec1, factor, pairs),
        me,
        [packed, offsets, proj_offset],
        arrays1,
        [
            shaped((length, width), BF),
            shaped((3, length, width), BF),
            shaped((length, width), BF),
            shaped((length, width), F32),
            shaped((length, width), F32),
            shaped((1, 6 * width), F32),
            shaped((length, width), BF),
        ],
        [],
        [pltpu.VMEM((4, blocks, block_rows, width), BF), dma((n1,))],
        "attention",
    )
    if layout.direct:
        w2 = gather_square(u2, [middle, cot])
    arrays2, spec2 = [w[0] for w in w2], tuple(w[1:] for w in w2)
    *grads2, result, dbefore, dgate2, up_bias, down_bias = call(
        mlp_kernel,
        (width, wide, spec2),
        me,
        [middle, mod, cot, up_offset, down_offset],
        arrays2,
        [
            shaped((length, width), BF),
            shaped((wide, length, width), BF),
            shaped((1, width), F32),
            shaped((1, wide * width), F32),
            shaped((1, width), F32),
        ],
        far_shapes(2 * wide),
        [
            pltpu.VMEM((wide, blocks, block_rows, width), BF),
            pltpu.VMEM((blocks, wide, block_rows, width), BF),
            pltpu.VMEM((blocks, wide, block_rows, width), BF),
            pltpu.VMEM((blocks, wide, block_rows, width), BF),
            pltpu.VMEM((wide, length, width), BF),
            pltpu.VMEM((wide, length, width), F32),
            dma((n2,)),
            dma((n2,)),
            dma((2 * blocks + 2,)),
        ],
        "mlp",
    )
    dmiddle, dbranch1, datt, sums1, proj_bias = call(
        middle_back_kernel,
        (width, wide, spec2, spec1),
        me,
        [middle, mod, cot, dbefore, branch1],
        arrays2 + arrays1,
        [
            shaped((length, width), F32),
            shaped((length, width), BF),
            shaped((length, width), BF),
            shaped((1, 3 * width), F32),
            shaped((1, width), F32),
        ],
        [],
        [
            pltpu.VMEM((wide, blocks, block_rows, width), BF),
            pltpu.VMEM((1, blocks, block_rows, width), BF),
            dma((n2,)),
            dma((n1,)),
        ],
        "middle_back",
    )
    if layout.direct:
        kept2, others2 = grads2[0], [swap(g, "dp", 0) for g in grads2[1:]]
        first2 = scatter_first(kept2, others2, [datt])
        low2, high2 = swap(first2[0], "dp", 2), swap(first2[1], "dp", 1)
        x_high2, y_low2 = swap(first2[2], "dp", 1), swap(first2[3], "dp", 2)
    *grads1, dqkv, qv_bias = call(
        attend_back_kernel,
        (width, factor, pairs),
        me,
        [dbranch1, datt, attended, hidden1, qkv],
        [],
        [shaped((3, length, width), BF), shaped((1, 2 * width), F32)],
        far_shapes(4),
        [pltpu.VMEM((blocks, 4, block_rows, width), BF), dma((blocks + 1,))],
        "attention_back",
        first2 if layout.direct else (),
    )
    if layout.direct:
        kept1, others1 = grads1[0], [swap(g, "dp", 0) for g in grads1[1:]]
    assert n_seq == 4 and wide == 4
    (packed,) = call(
        input_back_kernel,
        (width, tok, chunk, spec1),
        me,
        [tokens, mod, dmiddle, dqkv, sums1, dgate2, qv_bias, proj_bias, up_bias, down_bias, result],
        arrays1,
        [shaped((n_seq, 2 * tok + 16, width), BF)],
        [],
        [
            pltpu.VMEM((3, blocks, block_rows, width), BF),
            pltpu.VMEM((1, 6 * width), F32),
            pltpu.VMEM((16, width), F32),
            dma((n1,)),
        ],
        "input_back",
        (),
        4 * 10**9,
    )

    if layout.direct:
        last2 = scatter_last(kept2, others2, low2, high2, [dqkv, x_high2, y_low2, packed])
        x_low2, y_high2 = swap(last2[0], "dp", 1), swap(last2[1], "dp", 2)
    packed = lax.all_to_all(packed, "seq", 0, 0, tiled=True)
    if layout.direct:
        first1 = whole_first(kept1, others1, [x_low2, y_high2])
        corner1, over_x1 = swap(first1[0], "dp", 1), swap(first1[1], "dp", 1)
    token_grad, result = packed[:, :tok], packed[:, tok + 16 :]
    small = packed[:, tok : tok + 4].reshape(n_seq, 4 * width)
    small = jnp.broadcast_to(small[None], (n_dp,) + small.shape)
    small = lax.all_to_all(small, "dp", 0, 0, tiled=True).reshape(n_dp * held, 4 * width)
    grad_mod, row_sums, dcond_part = call(
        mod_grad_kernel, n_seq, here, [small, cond_rows, modulator], [],
        [
            shaped(modulator.shape, F32),
            shaped((1, 4 * width), F32),
            shaped((n_dp * n_seq, held, rows), F32),
        ],
        [], [], "mod_grad",
    )
    row_sums = row_sums.reshape(4 * width)
    grad_mod_offset = row_sums[: modulator.shape[1]]
    dcond = lax.all_to_all(dcond_part, ("dp", "seq"), 0, 0, tiled=True)
    if layout.direct:
        blocks2 = call(
            collect2_kernel, spec_seq, here,
            [(kept2, (0,), (1,)), others2[0], x_low2, x_high2, y_low2, y_high2], [], [],
            [shaped((2, rows, width), BF)] * n_seq,
            [pltpu.VMEM((n_seq, 2, rows, width), BF), dma((n_seq,))], "collect2",
        )
        over_z2 = swap_seq(blocks2[1:])
        last1 = whole_last(kept1, others1, corner1, [blocks2[0]])
        over_y1 = swap(last1, "dp", 2)
        blocks1 = call(
            collect1_kernel, spec_seq, here,
            [(kept1, (0,), (1,)), others1[0]]
            + [(v, (half,), (2,)) for v in (over_x1, over_y1) for half in range(2)], [], [],
            [shaped((rows, width), BF)] * n_seq,
            [pltpu.VMEM((n_seq, rows, width), BF), dma((n_seq,))], "collect1", over_z2,
        )
        over_z1 = swap_seq(blocks1[1:])

    if layout.direct:
        up_out, down_out, result, token_grad = call(
            final2_kernel, spec_seq, here, [blocks2[0]] + over_z2 + [packed], [],
            [shaped((rows, width), F32), shaped((wide * rows, chunk), F32)]
            + [shaped((held, tok, width), BF)] * 2, [], [], "final2", [dcond_part],
        )
        qkv_out, proj_out = call(
            final1_kernel, spec_seq, here, [blocks1[0]] + over_z1, [],
            [shaped((rows, 3 * chunk), F32), shaped((rows, chunk), F32)], [], [], "final1", [dcond],
        )
    else:
        unit_rows = lambda v: v.reshape(-1, n_dp, rows, width).transpose(1, 0, 2, 3)
        s1 = scatter_dp(unit_rows(grads1[0][0]))
        s_up = scatter_dp(unit_rows(grads2[0][0, :wide]))
        s_down = scatter_dp(grads2[0][0, wide:].reshape(n_dp, wide, rows, width))
        t1 = s1[:3].transpose(1, 0, 2).reshape(rows, n_seq, 3 * chunk)
        t1 = jnp.concatenate([t1, s1[3].reshape(rows, n_seq, chunk)], axis=2).transpose(1, 0, 2)
        t2 = s_up.transpose(1, 0, 2).reshape(rows, n_seq, -1).transpose(1, 0, 2)
        t3 = s_down.reshape(wide * rows, n_seq, chunk).transpose(1, 0, 2)
        r1, up_out, down_out = scatter_seq(t1), scatter_seq(t2), scatter_seq(t3)
        qkv_out, proj_out = r1[:, : 3 * chunk], r1[:, 3 * chunk :]
    dcond = jnp.sum(dcond.reshape(n_dp, n_seq, held, rows), axis=1)
    dcond = dcond.transpose(1, 0, 2).reshape(held, width)
    dconds = jax.vjp(jax.nn.silu, cond_float)[1](dcond)[0].reshape(micro, lats, width)

    at_q = 3 * width // 2
    at = [at_q, at_q + chunk, 3 * width, 2 * width, 3 * width + chunk]
    bias_grads = (querybias, valuebias, projbias, expandbias, contractbias)
    sums = [row_sums[first : first + b.shape[0]] for first, b in zip(at, bias_grads)]
    return (
        result.reshape(micro, lats, tok, width),
        token_grad.reshape(micro, lats, tok, width),
        dconds,
        grad_mod,
        grad_mod_offset,
        qkv_out,
        sums[0],
        sums[1],
        proj_out,
        sums[2],
        up_out,
        sums[3],
        down_out,
        sums[4],
    )


def solution(mesh):
    placed = (
        P(None, "dp", "seq", None),
        P(None, "dp", None),
        P("dp", "seq"),
        P("seq"),
        P("dp", "seq"),
        P("seq"),
        P("seq"),
        P("dp", "seq"),
        P("seq"),
        P("dp", "seq"),
        P("seq"),
        P("dp", "seq"),
        P("seq"),
        P(None, "dp", "seq", None),
    )
    return jax.shard_map(
        local,
        mesh=mesh,
        in_specs=placed,
        out_specs=(
            P(None, "dp", "seq", None),
            P(None, "dp", "seq", None),
            P(None, "dp", None),
            P("dp", "seq"),
            P("seq"),
            P("dp", "seq"),
            P("seq"),
            P("seq"),
            P("dp", "seq"),
            P("seq"),
            P("dp", "seq"),
            P("seq"),
            P("dp", "seq"),
            P("seq"),
        ),
        check_vma=False,
    )
```
